128 devices in a mesh: lat: 4 (over z_hi, core), lon: 32 (over z_lo, x, y).
Axes of the slice: x: 4, y: 4, z: 4 (z_hi: 2, z_lo: 2; z = z_hi * 2 + z_lo), core: 2. Of those that a mesh axis runs over, the one named last changes fastest.
Arguments:
- adjoint_in: float32 [3, 72, 1440, 512], P(None, None, 'lon', 'lat'), may hold values from -6 to 6
- courant_lon: float32 [72, 1440, 512], P(None, 'lon', 'lat'), may hold values from -0.2 to 0.2
- courant_lat: float32 [72, 1440, 512], P(None, 'lon', 'lat'), may hold values from -0.2 to 0.2
- vertical_mix: float32 [72, 72], replicated, may hold values from -0.375 to 0.375
- sounding_values: float32 [20, 1048576], P(None, ('lat', 'lon')), may hold values from -6 to 6
- sounding_dest: int32 [1048576, 1], P(('lat', 'lon')), may hold values from 0 to 127; in each aligned block of 8192 rows (0 to 8191, 8192 to 16383, ...) at most 128 rows name the same one
- sounding_target: int32 [1048576], P(('lat', 'lon')), may hold values from 0 to 17279
- level_index: int32 [20], replicated, may hold values from 0 to 71
Outputs:
- adjoint_out: float32 [3, 72, 1440, 512], P(None, None, 'lon', 'lat')
- flux_grad: float32 [3, 1440, 512], P(None, 'lon', 'lat')
The draws below stay inside these ranges and needn't reach their ends.
Inputs may be any that keep to these rules, and one draw needn't show every extreme that they name: `sounding_dest`: among the rows of one device, at most 128 name the same tile, a bound that some block reaches of them.
All inputs are finite; a program needn't handle non-finite values.
Results may differ from the reference program's by a relative error of at most 0.000065.
Values sent between devices are 32-bit elements; how exact they have to be, the bound alone decides.
No kernel may reach another device: no remote copies, remote signals or barrier semaphores. Data moves between devices by JAX's collectives and lax.ppermute only.
A program may use at most 128 MiB of HBM per device.

```python
import math
import jax
import jax.numpy as jnp
import numpy as np
from jax import lax

SPECIES = 3
LEV = 72
AKL = 20
CLAT = 128
CLON = 45
S_DEV = 8192
CAP = 128
NLAT = 512
NLON = 1440
S_TOTAL = 1048576
N_LON = 32
DEVICES = 128


def place_ends(values, own_key, least, high):
    spot = [jax.random.randint(jax.random.fold_in(own_key, axis), (), 0, length) for axis, length in enumerate(values.shape)]
    longest = values.shape.index(max(values.shape))
    beside = spot[:longest] + [(spot[longest] + 1) % values.shape[longest]] + spot[longest + 1:]
    return values.at[tuple(spot)].set(least).at[tuple(beside)].set(high)


def block_scale(rng, extent, shards, smallest, high):
    level = 1.0
    for axis_at, shards_of in shards:
        draws = jax.random.uniform(jax.random.fold_in(jax.random.fold_in(rng, 6), axis_at), (shards_of,), jnp.float32, smallest / len(shards), high / len(shards))
        level = level * jnp.repeat(jnp.exp(draws), extent[axis_at] // shards_of).reshape((-1,) + (1,) * (len(extent) - 1 - axis_at))
    return level


def deal_out(rng, own, number, rows, number_of, top, most, skew):
    ranking = jax.random.permutation(rng, number_of)
    packed, usual = portions_of(number_of, rows * top, most, skew, True), portions_of(number_of, rows * top, most, skew, False)
    places = jnp.arange(number_of)

    def named(sizes, rotation):
        used = int((sizes > 0).sum())
        fixed = max(1, used // 4)
        moved = fixed + (places - fixed + rotation * (used - fixed)) % max(1, number_of - fixed)
        return jnp.zeros((number_of,), jnp.int32).at[ranking[jnp.where(places < fixed, places, moved)]].set(jnp.asarray(sizes, jnp.int32))

    sizes = jnp.where(number % 4 == 0, named(packed, number // 4), named(usual, number - number // 4 - 1))
    mixed = jax.random.permutation(jax.random.fold_in(own, 3), number_of)
    source_of, receiver = mixed[0:number_of // 2 * 2:2], mixed[1:number_of // 2 * 2:2]
    slack = jnp.minimum(sizes[source_of] - 1, most - sizes[receiver]) // 2
    slack = jnp.where((source_of == ranking[0]) | (receiver == ranking[0]) | (sizes[receiver] == 0), 0, jnp.maximum(slack, 0))
    moved = jax.random.randint(jax.random.fold_in(own, 4), (number_of // 2,), 0, 1 << 20) % (slack + 1)
    sizes = sizes.at[source_of].add(-moved).at[receiver].add(moved)
    items = jnp.searchsorted(jnp.cumsum(sizes), jnp.arange(rows * top), side="right").astype(jnp.int32)
    table = items.reshape(top, rows).T
    table = table[jax.random.permutation(jax.random.fold_in(own, 1), rows)]
    rotation = jax.random.randint(jax.random.fold_in(own, 2), (rows, 1), 0, top)
    return jnp.take_along_axis(table, (jnp.arange(top)[None, :] + rotation) % top, axis=1)


def portions_of(count, total, bound, slope, full):
    portions = [(1 << 20) // math.isqrt(grade ** slope) + 1 for grade in range(1, count + 1)]
    largest = bound if full else min(bound, max(-(-total // count), total * portions[0] // sum(portions)))
    least = 1 if total - largest >= count - 1 else 0
    counts, rest = [largest] + [least] * (count - 1), total - largest - least * (count - 1)
    while rest > 0:
        candidates = [i for i in range(1, count) if counts[i] < largest] or [i for i in range(1, count) if counts[i] < bound]
        whole, remaining = sum([portions[i] for i in candidates]), rest
        for i in candidates:
            more = min(bound - counts[i], max(1, remaining * portions[i] // whole), rest)
            counts[i] = counts[i] + more
            rest = rest - more
    return np.array(counts)


def noise(stream_key, dims, width, most, shards=(), held_as=jnp.bfloat16):
    entries = jax.random.normal(stream_key, dims, jnp.float32) * width
    if len(shards) > 0:
        entries = block_scale(stream_key, dims, shards, -0.22, 0.18) * entries
    return jnp.clip(entries, min=-most, max=most).astype(held_as)


def setup_inputs(seed: int = 0) -> dict:
    splits = jax.random.split(jax.random.key(seed), 9)
    adjoint_in = noise(splits[0], (SPECIES, LEV, NLON, NLAT), 1.0, 6.0, ((2, 32), (3, 4)), jnp.float32)
    courant_lon = jnp.clip(jax.random.uniform(splits[1], (LEV, NLON, NLAT), jnp.float32, -0.2, 0.2) * block_scale(splits[1], (LEV, NLON, NLAT), ((1, 32), (2, 4)), -0.4, 0.0), -0.2, 0.2)
    courant_lat = jnp.clip(jax.random.uniform(splits[2], (LEV, NLON, NLAT), jnp.float32, -0.2, 0.2) * block_scale(splits[2], (LEV, NLON, NLAT), ((1, 32), (2, 4)), -0.4, 0.0), -0.2, 0.2)
    vertical_mix = noise(splits[3], (LEV, LEV), (4 * LEV) ** -0.5, 0.375, (), jnp.float32)
    sounding_values = noise(splits[4], (AKL, S_TOTAL), 1.0, 6.0, ((1, 128),), jnp.float32)
    sounding_dest_keys = jax.random.split(jax.random.fold_in(splits[5], 1), S_TOTAL // S_DEV)
    sounding_dest_turns = jax.random.permutation(jax.random.fold_in(splits[5], 3), S_TOTAL // S_DEV)
    sounding_dest = jax.vmap(lambda own, number: deal_out(jax.random.fold_in(splits[5], 2), own, number, S_DEV, DEVICES, 1, CAP, 2))(sounding_dest_keys, sounding_dest_turns).reshape((S_TOTAL, 1))
    sounding_target = place_ends(jax.random.randint(splits[6], (S_TOTAL,), 0, SPECIES * CLAT * CLON), jax.random.fold_in(splits[6], 1), 0, (SPECIES * CLAT * CLON) - 1).astype(jnp.int32)
    level_index = place_ends(jax.random.randint(splits[7], (AKL,), 0, LEV), jax.random.fold_in(splits[7], 1), 0, LEV - 1).astype(jnp.int32)
    return {"adjoint_in": adjoint_in, "courant_lon": courant_lon, "courant_lat": courant_lat, "vertical_mix": vertical_mix, "sounding_values": sounding_values, "sounding_dest": sounding_dest, "sounding_target": sounding_target, "level_index": level_index}


kappa_mix = 0.05


def reference(adjoint_in, courant_lon, courant_lat, vertical_mix, sounding_values, sounding_dest, sounding_target, level_index):
    levels = (level_index[:, None] == jnp.arange(LEV, dtype=jnp.int32)[None, :]).astype(jnp.float32)
    mapped = jnp.dot(sounding_values.T, levels, precision=lax.Precision.HIGHEST, preferred_element_type=jnp.float32)
    tile = sounding_dest[:, 0].astype(jnp.int32)
    cell = sounding_target // SPECIES
    species = sounding_target % SPECIES
    lat_cell = (tile // N_LON) * CLAT + cell // CLON
    lon_cell = (tile % N_LON) * CLON + cell % CLON
    segment = ((species * NLON + lon_cell) * NLAT + lat_cell).astype(jnp.int32)
    forcing = jax.ops.segment_sum(mapped, segment, num_segments=SPECIES * NLON * NLAT)
    forcing = forcing.reshape(SPECIES, NLON, NLAT, LEV).transpose(0, 3, 1, 2)
    lat_global = jnp.arange(NLAT, dtype=jnp.int32)
    inside = (lat_global <= NLAT - 2).astype(jnp.float32)[None, None, :]
    below = (lat_global >= 1).astype(jnp.float32)[None, None, :]
    west_courant = jnp.roll(courant_lon, 1, axis=1)
    south_courant = jnp.concatenate([jnp.zeros((LEV, NLON, 1), jnp.float32), courant_lat[:, :, :-1]], axis=2)
    east_coef = jnp.maximum(courant_lon, 0.0) + kappa_mix
    west_coef = jnp.minimum(west_courant, 0.0) - kappa_mix
    north_coef = (jnp.maximum(courant_lat, 0.0) + kappa_mix) * inside
    south_coef = (jnp.minimum(south_courant, 0.0) - kappa_mix) * below
    matrix = jnp.eye(LEV, dtype=jnp.float32) + vertical_mix
    zero_col = jnp.zeros((SPECIES, LEV, NLON, 1), jnp.float32)

    def advance(field):
        east = jnp.roll(field, -1, axis=2)
        west = jnp.roll(field, 1, axis=2)
        north = jnp.concatenate([field[:, :, :, 1:], zero_col], axis=3)
        south = jnp.concatenate([zero_col, field[:, :, :, :-1]], axis=3)
        return field + east_coef * (east - field) + west_coef * (field - west) + north_coef * (north - field) + south_coef * (field - south)

    def mixing(field):
        return jnp.einsum('lm,slxy->smxy', matrix, field, precision=lax.Precision.HIGHEST)

    first = mixing(advance(adjoint_in)) + forcing
    second = mixing(advance(first))
    return second, first[:, 0] + second[:, 0]
```

```python
import functools

import jax
import jax.numpy as jnp
from jax import lax
from jax.experimental import pallas as pl
from jax.experimental.pallas import tpu as pltpu
from jax.sharding import PartitionSpec as P

kappa_mix = 0.05
LANES = 128
WIDE = 256
f32 = jnp.float32
bf16 = jnp.bfloat16
VMEM_LIMIT = 56 * 2**20


def call(kernel, out_shape, *args, scratch=(), smem=(), flops=0, nbytes=0):
    specs = [
        pl.BlockSpec(memory_space=pltpu.SMEM if i in smem else pltpu.VMEM) for i in range(len(args))
    ]
    return pl.pallas_call(
        kernel,
        out_shape=out_shape,
        in_specs=specs,
        out_specs=jax.tree.map(lambda _: pl.BlockSpec(memory_space=pltpu.VMEM), out_shape),
        scratch_shapes=list(scratch),
        compiler_params=pltpu.CompilerParams(vmem_limit_bytes=VMEM_LIMIT),
        cost_estimate=pl.CostEstimate(flops=flops, bytes_accessed=nbytes, transcendentals=0),
    )(*args)


def split(value):
    high = value.astype(bf16).astype(f32)
    return high, value - high


def nt_dot(a, b):
    return lax.dot_general(a, b, (((1,), (1,)), ((), ())), preferred_element_type=f32)


def onehot_product(parts, group, spot, total, count, step, together, depth):
    rows, length = parts.shape
    chunks = length // depth

    def of_group(g, carry):
        def of_chunk(c, carry):
            at = pl.ds(pl.multiple_of(c * depth, depth), depth)
            held, key = parts[:, at], group[:, at]
            left = jnp.concatenate(
                [
                    jnp.where(
                        key == ((g * together + i) * step).astype(f32).astype(bf16), held, jnp.zeros_like(held)
                    )
                    for i in range(together)
                ],
                axis=0,
            )
            product = nt_dot(left, spot[:, at])
            to = pl.ds(pl.multiple_of(g * (together * rows), together * rows), together * rows)
            if chunks == 1:
                total[to, :] = product
            else:

                @pl.when(c == 0)
                def _():
                    total[to, :] = product

                @pl.when(c > 0)
                def _():
                    total[to, :] += product

            return carry

        return lax.fori_loop(0, chunks, of_chunk, carry)

    lax.fori_loop(0, count // together, of_group, 0)


PACK = (4, 2048)
ADD = (2, 2048)


def pack_kernel(dest, values, target, out, ranked, parts, group, spot, total):
    blocks = dest.shape[0]
    n_tiles, held, _ = out.shape
    levels = values.shape[0]
    iota_t = lax.broadcasted_iota(jnp.int32, (n_tiles, WIDE), 0)
    square = (WIDE, WIDE)
    upper = (
        lax.broadcasted_iota(jnp.int32, square, 0) < lax.broadcasted_iota(jnp.int32, square, 1)
    ).astype(f32).astype(bf16)
    iota_w = lax.broadcasted_iota(jnp.int32, square, 0)

    def rank(b, base):
        d = dest[pl.ds(b, 1), :]
        hot = iota_t == d
        hot_f = jnp.where(hot, 1.0, 0.0)
        earlier = jnp.dot(hot_f.astype(bf16), upper, preferred_element_type=f32) + base
        own = jnp.sum(jnp.where(hot, earlier, 0.0), axis=0, keepdims=True).astype(jnp.int32)
        at = pl.ds(pl.multiple_of(b * WIDE, WIDE), WIDE)
        low = own + (d & 1) * LANES
        spot[:, at] = jnp.where(iota_w == low, 1.0, 0.0).astype(bf16)
        group[:, at] = jnp.broadcast_to((d >> 1).astype(f32), (2 * held, WIDE)).astype(bf16)
        row = jnp.concatenate(
            [values[:, at], target[:, at], jnp.zeros((held - levels - 1, WIDE), f32)], axis=0
        )
        parts[:, at] = jnp.concatenate(split(row), axis=0).astype(bf16)
        return base + jnp.sum(hot_f, axis=1, keepdims=True)

    lax.fori_loop(0, blocks, rank, jnp.zeros((n_tiles, 1), f32))
    onehot_product(parts, group, spot, total, n_tiles // 2, 1, *PACK)

    def put(j, carry):
        at = pl.multiple_of(j * 2 * held, 2 * held)
        both = total[pl.ds(at, held), :] + total[pl.ds(at + held, held), :]
        out[2 * j] = both[:, :LANES]
        out[2 * j + 1] = both[:, LANES:]
        return carry

    lax.fori_loop(0, n_tiles // 2, put, 0)


def pack(dest, values, target, n_tiles):
    levels, rows = values.shape
    held = -(-(levels + 1) // 8) * 8
    scratch = (
        pltpu.VMEM((8, LANES), f32),
        pltpu.VMEM((2 * held, rows), bf16),
        pltpu.VMEM((2 * held, rows), bf16),
        pltpu.VMEM((WIDE, rows), bf16),
        pltpu.VMEM((n_tiles // 2 * 2 * held, WIDE), f32),
    )
    return call(
        pack_kernel,
        jax.ShapeDtypeStruct((n_tiles, held, LANES), f32),
        dest.reshape(rows // WIDE, WIDE),
        values,
        target.reshape(1, rows),
        scratch=scratch,
        flops=2 * rows * n_tiles * LANES * 2 * held,
        nbytes=4 * (rows * 22 + n_tiles * held * LANES),
    )


def edges_kernel(field, courant_lat, up, down):
    species, cols, levels, rows = field.shape
    lane = lax.broadcasted_iota(jnp.int32, (levels, rows), 1)

    def column(x, carry):
        for s in range(species):
            v = field[s, x]
            up[s] = jnp.where(lane == x, pltpu.roll(v, x + 1, 1), up[s])
            down[s] = jnp.where(lane == x, pltpu.roll(v, x, 1), down[s])
        up[species] = jnp.where(lane == x, pltpu.roll(courant_lat[x], x + 1, 1), up[species])
        return carry

    up[...] = jnp.zeros_like(up)
    down[...] = jnp.zeros_like(down)
    lax.fori_loop(0, cols, column, 0)


def edges(field, courant_lat):
    species, cols, levels, rows = field.shape
    return call(
        edges_kernel,
        (
            jax.ShapeDtypeStruct((species + 1, levels, rows), f32),
            jax.ShapeDtypeStruct((species, levels, rows), f32),
        ),
        field,
        courant_lat,
        flops=field.size * 4,
        nbytes=field.size * 4,
    )


def mix_weights(vertical_mix):
    levels = vertical_mix.shape[0]
    matrix = (jnp.eye(levels, dtype=f32) + vertical_mix).T
    high = lax.reduce_precision(matrix, 8, 7)
    return jnp.concatenate([high, high, matrix - high], axis=1).astype(bf16)


def step_kernel(
    lat_ref, field, clon, clat, west_col, east_col, clon_col, south, north, clat_south, weights, *refs, lat_size, after
):
    species, cols, levels, rows = field.shape
    lane = lax.broadcasted_iota(jnp.int32, (levels, rows), 1)
    first, last = lane == 0, lane == rows - 1
    lat = lat_ref[0]
    below = jnp.where(jnp.logical_and(first, lat == 0), 0.0, 1.0)
    inside = jnp.where(jnp.logical_and(last, lat == lat_size - 1), 0.0, 1.0)
    w = weights[...]

    def column(x, west, east, clon_west):
        cl, cw = clon[x], clat[x]
        e = jnp.maximum(cl, 0.0) + kappa_mix
        wst = jnp.minimum(clon_west, 0.0) - kappa_mix
        n = (jnp.maximum(cw, 0.0) + kappa_mix) * inside
        cs = jnp.where(first, pltpu.roll(clat_south[...], rows - x, 1), pltpu.roll(cw, 1, 1))
        s_ = (jnp.minimum(cs, 0.0) - kappa_mix) * below
        centre = 1.0 - e + wst - n + s_
        wide = []
        for s in range(species):
            v = field[s, x]
            v_n = jnp.where(last, pltpu.roll(north[s], rows - 1 - x, 1), pltpu.roll(v, rows - 1, 1))
            v_s = jnp.where(first, pltpu.roll(south[s], rows - x, 1), pltpu.roll(v, 1, 1))
            h = centre * v + e * east(s) - wst * west(s) + n * v_n - s_ * v_s
            high, low = split(h)
            wide.append(jnp.concatenate([high, low, high], axis=0).astype(bf16))
        mixed = jnp.dot(w, jnp.concatenate(wide, axis=1), preferred_element_type=f32)
        after(x, [mixed[:, s * rows : (s + 1) * rows] for s in range(species)], refs)

    roll_fix = None
    column(0, lambda s: west_col[s], lambda s: field[s, 1], clon_col[...])

    def body(x, carry):
        column(x, lambda s: field[s, x - 1], lambda s: field[s, x + 1], clon[x - 1])
        return carry

    lax.fori_loop(1, cols - 1, body, 0)
    column(cols - 1, lambda s: field[s, cols - 2], lambda s: east_col[s], clon[cols - 2])


def after_first(x, mixed, refs):
    (out,) = refs
    for s, m in enumerate(mixed):
        out[s, x] = m


def after_second(x, mixed, refs):
    level0, out, flux = refs
    for s, m in enumerate(mixed):
        out[s, x] = m
        flux[s, pl.ds(x, 1), :] = level0[s, pl.ds(x, 1), :] + m[0:1]


def step(lat, field, clon, clat, halo, weights, lat_size, level0=None):
    species, cols, levels, rows = field.shape
    shape = jax.ShapeDtypeStruct(field.shape, f32)
    if level0 is None:
        shapes, after, more = (shape,), after_first, ()
    else:
        shapes, after, more = (shape, jax.ShapeDtypeStruct((species, cols, rows), f32)), after_second, (level0,)
    west_col, east_col, clon_col, south, north, clat_south = halo
    return call(
        functools.partial(step_kernel, lat_size=lat_size, after=after),
        shapes,
        lat,
        field,
        clon,
        clat,
        west_col,
        east_col,
        clon_col,
        south,
        north,
        clat_south,
        weights,
        *more,
        smem=(0,),
        flops=field.size * levels * 6,
        nbytes=field.size * 12,
    )


def add_kernel(got, plain, table, first, up, down, level0, parts, group, spot, total):
    sources, held, slots = got.shape
    species, cols, levels, rows = plain.shape
    akl = table.shape[1] // 4
    iota_w = lax.broadcasted_iota(jnp.int32, (WIDE, WIDE), 0)
    second = (lax.broadcasted_iota(jnp.int32, (4 * akl, WIDE), 0) >= 2 * akl).astype(f32)

    def prepare(b, carry):
        row = jnp.concatenate([got[2 * b], got[2 * b + 1]], axis=1)
        at = pl.ds(pl.multiple_of(b * WIDE, WIDE), WIDE)
        segment = row[akl : akl + 1].astype(jnp.int32)
        spot[:, at] = jnp.where(iota_w == (segment & (WIDE - 1)), 1.0, 0.0).astype(bf16)
        group[:, at] = ((segment >> 8).astype(f32) - second).astype(bf16)
        high, low = split(row[:akl])
        both = jnp.concatenate([high, low], axis=0)
        parts[:, at] = jnp.concatenate([both, both], axis=0).astype(bf16)
        return carry

    lax.fori_loop(0, sources // 2, prepare, 0)
    onehot_product(parts, group, spot, total, -(-species * cols // 4), 2, *ADD)

    lane = lax.broadcasted_iota(jnp.int32, (levels, rows), 1)
    up[...] = jnp.zeros_like(up)
    down[...] = jnp.zeros_like(down)
    t = table[...]

    def place(at, half, s, x):
        pair = total[pl.ds(at, 2 * akl), half * rows : (half + 1) * rows]
        high, low = split(pair)
        forcing = jnp.dot(t, jnp.concatenate([high, low], axis=0).astype(bf16), preferred_element_type=f32)
        v = plain[s, x] + forcing
        first[s, x] = v
        level0[s, pl.ds(x, 1), :] = v[0:1]
        up[s] = jnp.where(lane == x, pltpu.roll(v, x + 1, 1), up[s])
        down[s] = jnp.where(lane == x, pltpu.roll(v, x, 1), down[s])

    for s in range(species):

        def column(x, carry):
            sx = s * cols + x
            at = pl.multiple_of((sx >> 1) * 2 * akl, 8)

            @pl.when((sx & 1) == 0)
            def _():
                place(at, 0, s, x)

            @pl.when((sx & 1) == 1)
            def _():
                place(at, 1, s, x)

            return carry

        lax.fori_loop(0, cols, column, 0)


def add_soundings(got, plain, table):
    sources, held, slots = got.shape
    species, cols, levels, rows = plain.shape
    akl = table.shape[1] // 4
    length = sources * slots
    pairs = -(-species * cols // 4)
    edge = jax.ShapeDtypeStruct((species, levels, rows), f32)
    return call(
        add_kernel,
        (jax.ShapeDtypeStruct(plain.shape, f32), edge, edge, jax.ShapeDtypeStruct((species, cols, rows), f32)),
        got,
        plain,
        table,
        scratch=(
            pltpu.VMEM((4 * akl, length), bf16),
            pltpu.VMEM((4 * akl, length), bf16),
            pltpu.VMEM((WIDE, length), bf16),
            pltpu.VMEM((pairs * 4 * akl, WIDE), f32),
        ),
        flops=2 * pairs * 4 * akl * WIDE * length,
        nbytes=4 * (got.size + 2 * plain.size),
    )


def on_device(
    adjoint_in,
    courant_lon,
    courant_lat,
    vertical_mix,
    sounding_values,
    sounding_dest,
    sounding_target,
    level_index,
):
    lat_size, lon_size = lax.axis_size("lat"), lax.axis_size("lon")
    n_tiles = lat_size * lon_size
    species, levels, cols, rows = adjoint_in.shape
    east_way = [(i, (i + 1) % lon_size) for i in range(lon_size)]
    west_way = [(j, i) for i, j in east_way]
    north_way = [(i, i + 1) for i in range(lat_size - 1)]
    south_way = [(j, i) for i, j in north_way]

    field = adjoint_in.transpose(0, 2, 1, 3)
    clon = courant_lon.transpose(1, 0, 2)
    clat = courant_lat.transpose(1, 0, 2)
    lat = lax.axis_index("lat").reshape(1)

    cell, tracer = sounding_target // species, sounding_target % species
    segment = (tracer * cols + cell % cols) * rows + cell // cols
    sent = pack(sounding_dest, sounding_values, segment.astype(f32), n_tiles)
    got = lax.all_to_all(sent, ("lat", "lon"), split_axis=0, concat_axis=0, tiled=True)

    up, down = edges(field, clat)
    south = lax.ppermute(up, "lat", north_way)
    north = lax.ppermute(down, "lat", south_way)
    clat_south = south[species]
    west = lax.ppermute(jnp.concatenate([field[:, cols - 1], clon[None, cols - 1]], axis=0), "lon", east_way)
    east = lax.ppermute(field[:, 0], "lon", west_way)
    clon_west = west[species]

    weights = mix_weights(vertical_mix)
    table = (jnp.arange(levels, dtype=jnp.int32)[:, None] == level_index[None, :]).astype(bf16)
    table = jnp.concatenate([table] * 4, axis=1)
    (plain,) = step(lat, field, clon, clat, (west, east, clon_west, south, north, clat_south), weights, lat_size)
    first, up, down, level0 = add_soundings(got, plain, table)
    south = lax.ppermute(up, "lat", north_way)
    north = lax.ppermute(down, "lat", south_way)
    west = lax.ppermute(first[:, cols - 1], "lon", east_way)
    east = lax.ppermute(first[:, 0], "lon", west_way)
    out, flux = step(
        lat, first, clon, clat, (west, east, clon_west, south, north, clat_south), weights, lat_size, level0
    )
    return out.transpose(0, 2, 1, 3), flux


def solution(mesh):
    return jax.shard_map(
        on_device,
        mesh=mesh,
        in_specs=(
            P(None, None, "lon", "lat"),
            P(None, "lon", "lat"),
            P(None, "lon", "lat"),
            P(),
            P(None, ("lat", "lon")),
            P(("lat", "lon"), None),
            P(("lat", "lon")),
            P(),
        ),
        out_specs=(P(None, None, "lon", "lat"), P(None, "lon", "lat")),
        check_vma=False,
    )
```

```python
import functools

import jax
import jax.numpy as jnp
from jax import lax
from jax.experimental import pallas as pl
from jax.experimental.pallas import tpu as pltpu
from jax.sharding import PartitionSpec as P

kappa_mix = 0.05
LANES = 128
WIDE = 256
f32 = jnp.float32
bf16 = jnp.bfloat16
BLOCK = 9
VMEM_LIMIT = 56 * 2**20


def call(kernel, out_shape, *args, scratch=(), smem=(), flops=0, nbytes=0):
    specs = [
        pl.BlockSpec(memory_space=pltpu.SMEM if i in smem else pltpu.VMEM) for i in range(len(args))
    ]
    return pl.pallas_call(
        kernel,
        out_shape=out_shape,
        in_specs=specs,
        out_specs=jax.tree.map(lambda _: pl.BlockSpec(memory_space=pltpu.VMEM), out_shape),
        scratch_shapes=list(scratch),
        compiler_params=pltpu.CompilerParams(vmem_limit_bytes=VMEM_LIMIT),
        cost_estimate=pl.CostEstimate(flops=flops, bytes_accessed=nbytes, transcendentals=0),
    )(*args)


def split(value):
    high = value.astype(bf16).astype(f32)
    return high, value - high


def nt_dot(a, b):
    return lax.dot_general(a, b, (((1,), (1,)), ((), ())), preferred_element_type=f32)


def onehot_product(parts, group, spot, total, count, step, together, depth):
    rows, length = parts.shape
    chunks = length // depth

    def of_group(g, carry):
        def of_chunk(c, carry):
            at = pl.ds(pl.multiple_of(c * depth, depth), depth)
            held, key = parts[:, at], group[:, at]
            left = jnp.concatenate(
                [
                    jnp.where(
                        key == ((g * together + i) * step).astype(f32).astype(bf16), held, jnp.zeros_like(held)
                    )
                    for i in range(together)
                ],
                axis=0,
            )
            product = nt_dot(left, spot[:, at])
            to = pl.ds(pl.multiple_of(g * (together * rows), together * rows), together * rows)
            if chunks == 1:
                total[to, :] = product
            else:

                @pl.when(c == 0)
                def _():
                    total[to, :] = product

                @pl.when(c > 0)
                def _():
                    total[to, :] += product

            return carry

        return lax.fori_loop(0, chunks, of_chunk, carry)

    lax.fori_loop(0, count // together, of_group, 0)


PACK = (16, 8192)
ADD = (17, 4096)


def whole_part(value, divisor):
    return ((value.astype(f32) + 0.5) * (1.0 / divisor)).astype(jnp.int32)


def pack_kernel(dest, values, target, out, parts, group, spot, total, *, species, cols, rows):
    n_tiles, held, _ = out.shape
    levels, length = values.shape
    iota_t = lax.broadcasted_iota(jnp.int32, (n_tiles, WIDE), 0)
    square = (WIDE, WIDE)
    upper = (
        lax.broadcasted_iota(jnp.int32, square, 0) < lax.broadcasted_iota(jnp.int32, square, 1)
    ).astype(f32).astype(bf16)
    iota_w = lax.broadcasted_iota(jnp.int32, square, 0)

    def rank(at, base):
        d = dest[:, at]
        hot = iota_t == d
        hot_f = jnp.where(hot, 1.0, 0.0)
        earlier = jnp.dot(hot_f.astype(bf16), upper, preferred_element_type=f32) + base
        own = jnp.sum(jnp.where(hot, earlier, 0.0), axis=0, keepdims=True).astype(jnp.int32)
        low = own + (d & 1) * LANES
        spot[:, at] = jnp.where(iota_w == low, 1.0, 0.0).astype(bf16)
        group[:, at] = jnp.broadcast_to((d >> 1).astype(f32), (2 * held, WIDE)).astype(bf16)
        t = target[:, at]
        cell = whole_part(t, species)
        row_of = whole_part(cell, cols)
        segment = ((t - cell * species) * cols + cell - row_of * cols) * rows + row_of
        row = jnp.concatenate(
            [values[:, at], segment.astype(f32), jnp.zeros((held - levels - 1, WIDE), f32)], axis=0
        )
        parts[:, at] = jnp.concatenate(split(row), axis=0).astype(bf16)
        return base + jnp.sum(hot_f, axis=1, keepdims=True)

    def ranks(b, base):
        for i in range(4):
            base = rank(pl.ds(pl.multiple_of((4 * b + i) * WIDE, WIDE), WIDE), base)
        return base

    lax.fori_loop(0, length // (4 * WIDE), ranks, jnp.zeros((n_tiles, 1), f32))
    onehot_product(parts, group, spot, total, n_tiles // 2, 1, *PACK)

    def put(g, carry):
        for i in range(4):
            j = 4 * g + i
            at = pl.multiple_of(j * 2 * held, 2 * held)
            both = total[pl.ds(at, held), :] + total[pl.ds(at + held, held), :]
            out[2 * j] = both[:, :LANES]
            out[2 * j + 1] = both[:, LANES:]
        return carry

    lax.fori_loop(0, n_tiles // 8, put, 0)


def pack(dest, values, target, n_tiles, species, cols, rows):
    levels, length = values.shape
    held = -(-(levels + 1) // 8) * 8
    scratch = (
        pltpu.VMEM((2 * held, length), bf16),
        pltpu.VMEM((2 * held, length), bf16),
        pltpu.VMEM((WIDE, length), bf16),
        pltpu.VMEM((n_tiles // 2 * 2 * held, WIDE), f32),
    )
    return call(
        functools.partial(pack_kernel, species=species, cols=cols, rows=rows),
        jax.ShapeDtypeStruct((n_tiles, held, LANES), f32),
        dest.reshape(1, length),
        values,
        target.reshape(1, length),
        scratch=scratch,
        flops=2 * length * n_tiles * LANES * 2 * held,
        nbytes=4 * (length * 22 + n_tiles * held * LANES),
    )


def lane_put(kept, lane, x, value, by):
    return jnp.where(lane == x, pltpu.roll(value, by, 1), kept)


def edges_kernel(field, clat, up, down):
    species, block, levels, rows = field.shape
    lane = lax.broadcasted_iota(jnp.int32, (levels, rows), 1)
    first = pl.program_id(0) * block

    @pl.when(first == 0)
    def _():
        up[...] = jnp.zeros_like(up)
        down[...] = jnp.zeros_like(down)

    for s in range(species + 1):
        u = up[s]
        for i in range(block):
            x = first + i
            u = lane_put(u, lane, x, field[s, i] if s < species else clat[i], x + 1)
        up[s] = u
        if s < species:
            d = down[s]
            for i in range(block):
                x = first + i
                d = lane_put(d, lane, x, field[s, i], x)
            down[s] = d


def edges(field, clat):
    species, cols, levels, rows = field.shape
    up, down = (species + 1, levels, rows), (species, levels, rows)
    return pl.pallas_call(
        edges_kernel,
        out_shape=(jax.ShapeDtypeStruct(up, f32), jax.ShapeDtypeStruct(down, f32)),
        grid=(cols // BLOCK,),
        in_specs=[
            pl.BlockSpec((species, BLOCK, levels, rows), lambda i: (0, i, 0, 0)),
            pl.BlockSpec((BLOCK, levels, rows), lambda i: (i, 0, 0)),
        ],
        out_specs=(pl.BlockSpec(up, lambda i: (0, 0, 0)), pl.BlockSpec(down, lambda i: (0, 0, 0))),
        compiler_params=pltpu.CompilerParams(vmem_limit_bytes=VMEM_LIMIT),
        cost_estimate=pl.CostEstimate(flops=field.size * 4, bytes_accessed=field.size * 5, transcendentals=0),
    )(field, clat)


def mix_weights(vertical_mix):
    levels = vertical_mix.shape[0]
    matrix = (jnp.eye(levels, dtype=f32) + vertical_mix).T
    high = lax.reduce_precision(matrix, 8, 7)
    return jnp.concatenate([high, high, matrix - high], axis=1).astype(bf16)


def step_kernel(
    lat_ref,
    field,
    field_west,
    field_east,
    clon,
    clon_before,
    clat,
    west_col,
    east_col,
    clon_col,
    south,
    north,
    clat_south,
    weights,
    *refs,
    lat_size,
):
    species, block, levels, rows = field.shape
    lane = lax.broadcasted_iota(jnp.int32, (levels, rows), 1)
    first, last = lane == 0, lane == rows - 1
    lat = lat_ref[0]
    below = jnp.where(jnp.logical_and(first, lat == 0), 0.0, 1.0)
    inside = jnp.where(jnp.logical_and(last, lat == lat_size - 1), 0.0, 1.0)
    w = weights[...]
    here = pl.program_id(0)
    at_start, at_end = here == 0, here == pl.num_programs(0) - 1
    waiting = []

    def mix(ready):
        mixed = jnp.dot(
            w, jnp.concatenate([r for _, _, r in ready], axis=1), preferred_element_type=f32
        )
        for k, (s, i, _) in enumerate(ready):
            m = mixed[:, k * rows : (k + 1) * rows]
            if len(refs) == 1:
                refs[0][s, i] = m
            else:
                level0, out, flux = refs
                x = here * block + i
                out[s, i] = m
                flux[s, pl.ds(x, 1), :] = level0[s, pl.ds(x, 1), :] + m[0:1]

    for i in range(block):
        x = here * block + i
        cl, cw = clon[i], clat[i]
        cl_west = clon[i - 1] if i else jnp.where(at_start, clon_col[0], clon_before[0])
        e = jnp.maximum(cl, 0.0) + kappa_mix
        w_ = kappa_mix - jnp.minimum(cl_west, 0.0)
        n = (jnp.maximum(cw, 0.0) + kappa_mix) * inside
        cs = jnp.where(first, pltpu.roll(clat_south[0], lax.rem(rows - x, rows), 1), pltpu.roll(cw, 1, 1))
        s_ = (kappa_mix - jnp.minimum(cs, 0.0)) * below
        centre = 1.0 - (e + w_ + n + s_)
        for s in range(species):
            v = field[s, i]
            v_w = field[s, i - 1] if i else jnp.where(at_start, west_col[s], field_west[s, 0])
            v_e = field[s, i + 1] if i < block - 1 else jnp.where(at_end, east_col[s], field_east[s, 0])
            v_n = jnp.where(last, pltpu.roll(north[s], rows - 1 - x, 1), pltpu.roll(v, rows - 1, 1))
            v_s = jnp.where(first, pltpu.roll(south[s], lax.rem(rows - x, rows), 1), pltpu.roll(v, 1, 1))
            h = centre * v + e * v_e + w_ * v_w + n * v_n + s_ * v_s
            high, low = split(h)
            waiting.append((s, i, jnp.concatenate([high, low, high], axis=0).astype(bf16)))
            if len(waiting) == 2:
                mix(waiting)
                waiting.clear()
    if waiting:
        mix(waiting)


def step(lat, field, clon, clat, halo, weights, lat_size, level0=None):
    species, cols, levels, rows = field.shape
    shapes = [jax.ShapeDtypeStruct(field.shape, f32)]
    columns = pl.BlockSpec((species, BLOCK, levels, rows), lambda i: (0, i, 0, 0))
    courant = pl.BlockSpec((BLOCK, levels, rows), lambda i: (i, 0, 0))
    out_specs = [columns]
    whole = lambda shape: pl.BlockSpec(shape, lambda i: (0,) * len(shape))
    part = lambda at: pl.BlockSpec((1, levels, rows), lambda i: (at, 0, 0))
    more = ()
    if level0 is not None:
        more = (level0,)
        shapes.append(jax.ShapeDtypeStruct(level0.shape, f32))
        out_specs.append(whole(level0.shape))
    west, east, clon_west, south, north, clat_south = halo
    three = whole((species, levels, rows))
    return pl.pallas_call(
        functools.partial(step_kernel, lat_size=lat_size),
        out_shape=shapes,
        grid=(cols // BLOCK,),
        in_specs=[
            pl.BlockSpec(memory_space=pltpu.SMEM),
            columns,
            pl.BlockSpec((species, 1, levels, rows), lambda i: (0, jnp.maximum(i * BLOCK - 1, 0), 0, 0)),
            pl.BlockSpec((species, 1, levels, rows), lambda i: (0, jnp.minimum(i * BLOCK + BLOCK, cols - 1), 0, 0)),
            courant,
            pl.BlockSpec((1, levels, rows), lambda i: (jnp.maximum(i * BLOCK - 1, 0), 0, 0)),
            courant,
            three,
            three,
            part(species),
            three,
            three,
            part(species),
            whole(weights.shape),
            *[whole(m.shape) for m in more],
        ],
        out_specs=out_specs,
        compiler_params=pltpu.CompilerParams(vmem_limit_bytes=VMEM_LIMIT),
        cost_estimate=pl.CostEstimate(
            flops=field.size * levels * 6, bytes_accessed=field.size * 12, transcendentals=0
        ),
    )(
        lat,
        field,
        field,
        field,
        clon,
        clon,
        clat,
        west,
        east,
        clon_west,
        south,
        north,
        clat_south,
        weights,
        *more,
    )


def add_kernel(
    got, plain, table, first, up, down, west, east, level0, parts, group, spot, total, held_field, sem_in, sem_out
):
    sources, held, slots = got.shape
    species, cols, levels, rows = plain.shape
    akl = table.shape[1] // 4
    fetch = pltpu.make_async_copy(plain, held_field, sem_in)
    fetch.start()
    iota_w = lax.broadcasted_iota(jnp.int32, (WIDE, WIDE), 0)
    second = (lax.broadcasted_iota(jnp.int32, (4 * akl, WIDE), 0) >= 2 * akl).astype(f32)

    def prepare(g, carry):
        for i in range(2):
            b = 2 * g + i
            row = jnp.concatenate([got[2 * b], got[2 * b + 1]], axis=1)
            at = pl.ds(pl.multiple_of(b * WIDE, WIDE), WIDE)
            segment = row[akl : akl + 1].astype(jnp.int32)
            spot[:, at] = jnp.where(iota_w == (segment & (WIDE - 1)), 1.0, 0.0).astype(bf16)
            group[:, at] = ((segment >> 8).astype(f32) - second).astype(bf16)
            high, low = split(row[:akl])
            both = jnp.concatenate([high, low], axis=0)
            parts[:, at] = jnp.concatenate([both, both], axis=0).astype(bf16)
        return carry

    lax.fori_loop(0, sources // 4, prepare, 0)
    onehot_product(parts, group, spot, total, -(-species * cols // 4), 2, *ADD)

    lane = lax.broadcasted_iota(jnp.int32, (levels, rows), 1)
    up[...] = jnp.zeros_like(up)
    down[...] = jnp.zeros_like(down)
    t = table[...]
    fetch.wait()
    blocks = cols // BLOCK

    def leave(s, b):
        at = pl.ds(b * BLOCK, BLOCK)
        return pltpu.make_async_copy(held_field.at[s, at], first.at[s, at], sem_out.at[s, b])

    for s in range(species):

        def columns(b, carry):
            u, d = up[s], down[s]
            for i in range(BLOCK):
                x = b * BLOCK + i
                sx = s * cols + x
                pair = total[
                    pl.ds(pl.multiple_of((sx >> 1) * 2 * akl, 8), 2 * akl),
                    pl.ds(pl.multiple_of((sx & 1) * rows, rows), rows),
                ]
                high, low = split(pair)
                forcing = jnp.dot(
                    t, jnp.concatenate([high, low], axis=0).astype(bf16), preferred_element_type=f32
                )
                v = held_field[s, x] + forcing
                held_field[s, x] = v
                level0[s, pl.ds(x, 1), :] = v[0:1]
                u = lane_put(u, lane, x, v, x + 1)
                d = lane_put(d, lane, x, v, x)
            up[s] = u
            down[s] = d
            leave(s, b).start()
            return carry

        lax.fori_loop(0, blocks, columns, 0)
        east[s] = held_field[s, 0]
        west[s] = held_field[s, cols - 1]
    for s in range(species):
        for b in range(blocks):
            leave(s, b).wait()


def add_soundings(got, plain, table):
    sources, held, slots = got.shape
    species, cols, levels, rows = plain.shape
    akl = table.shape[1] // 4
    length = sources * slots
    pairs = -(-species * cols // 4)
    edge = jax.ShapeDtypeStruct((species, levels, rows), f32)
    vmem, hbm = pl.BlockSpec(memory_space=pltpu.VMEM), pl.BlockSpec(memory_space=pl.ANY)
    return pl.pallas_call(
        add_kernel,
        out_shape=(
            jax.ShapeDtypeStruct(plain.shape, f32),
            edge,
            edge,
            edge,
            edge,
            jax.ShapeDtypeStruct((species, cols, rows), f32),
        ),
        in_specs=[vmem, hbm, vmem],
        out_specs=(hbm, vmem, vmem, vmem, vmem, vmem),
        scratch_shapes=(
            pltpu.VMEM((4 * akl, length), bf16),
            pltpu.VMEM((4 * akl, length), bf16),
            pltpu.VMEM((WIDE, length), bf16),
            pltpu.VMEM((pairs * 4 * akl, WIDE), f32),
            pltpu.VMEM(plain.shape, f32),
            pltpu.SemaphoreType.DMA,
            pltpu.SemaphoreType.DMA((species, cols // BLOCK)),
        ),
        compiler_params=pltpu.CompilerParams(vmem_limit_bytes=VMEM_LIMIT),
        cost_estimate=pl.CostEstimate(
            flops=2 * pairs * 4 * akl * WIDE * length,
            bytes_accessed=4 * (got.size + 2 * plain.size),
            transcendentals=0,
        ),
    )(got, plain, table)


def on_device(
    adjoint_in,
    courant_lon,
    courant_lat,
    vertical_mix,
    sounding_values,
    sounding_dest,
    sounding_target,
    level_index,
):
    lat_size, lon_size = lax.axis_size("lat"), lax.axis_size("lon")
    n_tiles = lat_size * lon_size
    species, levels, cols, rows = adjoint_in.shape
    east_way = [(i, (i + 1) % lon_size) for i in range(lon_size)]
    west_way = [(j, i) for i, j in east_way]
    north_way = [(i, i + 1) for i in range(lat_size - 1)]
    south_way = [(j, i) for i, j in north_way]

    field = adjoint_in.transpose(0, 2, 1, 3)
    clon = courant_lon.transpose(1, 0, 2)
    clat = courant_lat.transpose(1, 0, 2)
    lat = lax.axis_index("lat").reshape(1)

    sent = pack(sounding_dest, sounding_values, sounding_target, n_tiles, species, cols, rows)
    got = lax.all_to_all(sent, ("lat", "lon"), split_axis=0, concat_axis=0, tiled=True)

    up, down = edges(field, clat)
    clat_south = south = lax.ppermute(up, "lat", north_way)
    north = lax.ppermute(down, "lat", south_way)
    clon_west = west = lax.ppermute(
        jnp.concatenate([field[:, cols - 1], clon[None, cols - 1]], axis=0), "lon", east_way
    )
    east = lax.ppermute(field[:, 0], "lon", west_way)

    weights = mix_weights(vertical_mix)
    table = (jnp.arange(levels, dtype=jnp.int32)[:, None] == level_index[None, :]).astype(bf16)
    table = jnp.concatenate([table] * 4, axis=1)
    (plain,) = step(lat, field, clon, clat, (west, east, clon_west, south, north, clat_south), weights, lat_size)
    first, up, down, west, east, level0 = add_soundings(got, plain, table)
    south = lax.ppermute(up, "lat", north_way)
    north = lax.ppermute(down, "lat", south_way)
    west = lax.ppermute(west, "lon", east_way)
    east = lax.ppermute(east, "lon", west_way)
    out, flux = step(
        lat, first, clon, clat, (west, east, clon_west, south, north, clat_south), weights, lat_size, level0
    )
    return out.transpose(0, 2, 1, 3), flux


def solution(mesh):
    return jax.shard_map(
        on_device,
        mesh=mesh,
        in_specs=(
            P(None, None, "lon", "lat"),
            P(None, "lon", "lat"),
            P(None, "lon", "lat"),
            P(),
            P(None, ("lat", "lon")),
            P(("lat", "lon"), None),
            P(("lat", "lon")),
            P(),
        ),
        out_specs=(P(None, None, "lon", "lat"), P(None, "lon", "lat")),
        check_vma=False,
    )
```

```python
import functools

import jax
import jax.numpy as jnp
from jax import lax
from jax.experimental import pallas as pl
from jax.experimental.pallas import tpu as pltpu
from jax.sharding import PartitionSpec as P

kappa_mix = 0.05
LANES = 128
WIDE = 256
f32 = jnp.float32
bf16 = jnp.bfloat16
BLOCK = 15
VMEM_LIMIT = 52 * 2**20
ADD_LIMIT = 46 * 2**20


def call(kernel, out_shape, *args, scratch=(), smem=(), flops=0, nbytes=0):
    specs = [
        pl.BlockSpec(memory_space=pltpu.SMEM if i in smem else pltpu.VMEM) for i in range(len(args))
    ]
    return pl.pallas_call(
        kernel,
        out_shape=out_shape,
        in_specs=specs,
        out_specs=jax.tree.map(lambda _: pl.BlockSpec(memory_space=pltpu.VMEM), out_shape),
        scratch_shapes=list(scratch),
        compiler_params=pltpu.CompilerParams(vmem_limit_bytes=VMEM_LIMIT),
        cost_estimate=pl.CostEstimate(flops=flops, bytes_accessed=nbytes, transcendentals=0),
    )(*args)


def split(value):
    high = value.astype(bf16).astype(f32)
    return high, value - high


def nt_dot(a, b):
    return lax.dot_general(a, b, (((1,), (1,)), ((), ())), preferred_element_type=f32)


def onehot_product(parts, group, spot, total, count, step, together, depth):
    rows, length = parts.shape
    chunks = length // depth

    def of_group(g, carry):
        def of_chunk(c, carry):
            at = pl.ds(pl.multiple_of(c * depth, depth), depth)
            held, key = parts[:, at], group[:, at]
            left = jnp.concatenate(
                [
                    jnp.where(
                        key == ((g * together + i) * step).astype(f32).astype(bf16), held, jnp.zeros_like(held)
                    )
                    for i in range(together)
                ],
                axis=0,
            )
            product = nt_dot(left, spot[:, at])
            to = pl.ds(pl.multiple_of(g * (together * rows), together * rows), together * rows)
            if chunks == 1:
                total[to, :] = product
            else:

                @pl.when(c == 0)
                def _():
                    total[to, :] = product

                @pl.when(c > 0)
                def _():
                    total[to, :] += product

            return carry

        return lax.fori_loop(0, chunks, of_chunk, carry)

    lax.fori_loop(0, count // together, of_group, 0)


PACK = (16, 8192)
ADD = (17, 4096)


def whole_part(value, divisor):
    return ((value.astype(f32) + 0.5) * (1.0 / divisor)).astype(jnp.int32)


def pack_kernel(dest, values, target, out, parts, group, spot, total, *, species, cols, rows):
    n_tiles, held, _ = out.shape
    levels, length = values.shape
    iota_t = lax.broadcasted_iota(jnp.int32, (n_tiles, WIDE), 0)
    square = (WIDE, WIDE)
    upper = (
        lax.broadcasted_iota(jnp.int32, square, 0) < lax.broadcasted_iota(jnp.int32, square, 1)
    ).astype(f32).astype(bf16)
    iota_w = lax.broadcasted_iota(jnp.int32, square, 0)

    def rank(at, base):
        d = dest[:, at]
        hot = iota_t == d
        hot_f = jnp.where(hot, 1.0, 0.0)
        earlier = jnp.dot(hot_f.astype(bf16), upper, preferred_element_type=f32) + base
        own = jnp.sum(jnp.where(hot, earlier, 0.0), axis=0, keepdims=True).astype(jnp.int32)
        low = own + (d & 1) * LANES
        spot[:, at] = jnp.where(iota_w == low, 1.0, 0.0).astype(bf16)
        group[:, at] = jnp.broadcast_to((d >> 1).astype(f32), (2 * held, WIDE)).astype(bf16)
        t = target[:, at]
        cell = whole_part(t, species)
        row_of = whole_part(cell, cols)
        segment = ((t - cell * species) * cols + cell - row_of * cols) * rows + row_of
        row = jnp.concatenate(
            [values[:, at], segment.astype(f32), jnp.zeros((held - levels - 1, WIDE), f32)], axis=0
        )
        parts[:, at] = jnp.concatenate(split(row), axis=0).astype(bf16)
        return base + jnp.sum(hot_f, axis=1, keepdims=True)

    def ranks(b, base):
        for i in range(4):
            base = rank(pl.ds(pl.multiple_of((4 * b + i) * WIDE, WIDE), WIDE), base)
        return base

    lax.fori_loop(0, length // (4 * WIDE), ranks, jnp.zeros((n_tiles, 1), f32))
    onehot_product(parts, group, spot, total, n_tiles // 2, 1, *PACK)

    def put(g, carry):
        for i in range(4):
            j = 4 * g + i
            at = pl.multiple_of(j * 2 * held, 2 * held)
            both = total[pl.ds(at, held), :] + total[pl.ds(at + held, held), :]
            out[2 * j] = both[:, :LANES]
            out[2 * j + 1] = both[:, LANES:]
        return carry

    lax.fori_loop(0, n_tiles // 8, put, 0)


def pack(dest, values, target, n_tiles, species, cols, rows):
    levels, length = values.shape
    held = -(-(levels + 1) // 8) * 8
    scratch = (
        pltpu.VMEM((2 * held, length), bf16),
        pltpu.VMEM((2 * held, length), bf16),
        pltpu.VMEM((WIDE, length), bf16),
        pltpu.VMEM((n_tiles // 2 * 2 * held, WIDE), f32),
    )
    return call(
        functools.partial(pack_kernel, species=species, cols=cols, rows=rows),
        jax.ShapeDtypeStruct((n_tiles, held, LANES), f32),
        dest.reshape(1, length),
        values,
        target.reshape(1, length),
        scratch=scratch,
        flops=2 * length * n_tiles * LANES * 2 * held,
        nbytes=4 * (length * 22 + n_tiles * held * LANES),
    )


def edge_lanes(columns, kept, first, by):
    lane = lax.broadcasted_iota(jnp.int32, kept.shape, 1)
    own = kept
    for i, v in enumerate(columns):
        own = jnp.where(lane == i, pltpu.roll(v, i + by, 1), own)
    inside = jnp.logical_and(lane >= first, lane < first + len(columns))
    return jnp.where(inside, pltpu.roll(own, first, 1), kept)


def edges_kernel(field, clat, clon_last, up, down, west, east):
    species, block, levels, rows = field.shape
    here = pl.program_id(0)
    first = here * block

    @pl.when(here == 0)
    def _():
        up[...] = jnp.zeros_like(up)
        down[...] = jnp.zeros_like(down)
        for s in range(species):
            east[s] = field[s, 0]

    @pl.when(here == pl.num_programs(0) - 1)
    def _():
        for s in range(species):
            west[s] = field[s, block - 1]
        west[species] = clon_last[0]

    for s in range(species + 1):
        columns = [field[s, i] if s < species else clat[i] for i in range(block)]
        up[s] = edge_lanes(columns, up[s], first, 1)
        if s < species:
            down[s] = edge_lanes(columns, down[s], first, 0)


def edges(field, clat, clon):
    species, cols, levels, rows = field.shape
    four, three = (species + 1, levels, rows), (species, levels, rows)
    shapes = (four, three, four, three)
    return pl.pallas_call(
        edges_kernel,
        out_shape=tuple(jax.ShapeDtypeStruct(shape, f32) for shape in shapes),
        grid=(cols // BLOCK,),
        in_specs=[
            pl.BlockSpec((species, BLOCK, levels, rows), lambda i: (0, i, 0, 0)),
            pl.BlockSpec((BLOCK, levels, rows), lambda i: (i, 0, 0)),
            pl.BlockSpec((1, levels, rows), lambda i: (cols - 1, 0, 0)),
        ],
        out_specs=tuple(pl.BlockSpec(shape, lambda i: (0, 0, 0)) for shape in shapes),
        compiler_params=pltpu.CompilerParams(vmem_limit_bytes=VMEM_LIMIT),
        cost_estimate=pl.CostEstimate(flops=field.size * 4, bytes_accessed=field.size * 5, transcendentals=0),
    )(field, clat, clon)


def mix_weights(vertical_mix):
    levels = vertical_mix.shape[0]
    matrix = (jnp.eye(levels, dtype=f32) + vertical_mix).T
    high = lax.reduce_precision(matrix, 8, 7)
    return jnp.concatenate([high, high, matrix - high], axis=1).astype(bf16)


def step_kernel(
    lat_ref,
    field,
    field_west,
    field_east,
    clon,
    clon_before,
    clat,
    west_col,
    east_col,
    clon_col,
    south,
    north,
    clat_south,
    weights,
    *refs,
    lat_size,
):
    species, block, levels, rows = field.shape
    lane = lax.broadcasted_iota(jnp.int32, (levels, rows), 1)
    first, last = lane == 0, lane == rows - 1
    lat = lat_ref[0]
    below = jnp.where(jnp.logical_and(first, lat == 0), 0.0, 1.0)
    inside = jnp.where(jnp.logical_and(last, lat == lat_size - 1), 0.0, 1.0)
    w = weights[...]
    here = pl.program_id(0)
    at_start, at_end = here == 0, here == pl.num_programs(0) - 1
    start = here * block
    south_on = lax.rem(rows - start, rows)
    north_on = rows - 1 - start
    souths = [pltpu.roll(south[s], south_on, 1) for s in range(species)]
    norths = [pltpu.roll(north[s], north_on, 1) for s in range(species)]
    courant_south = pltpu.roll(clat_south[0], south_on, 1)
    waiting = []

    def back(v, i):
        return pltpu.roll(v, rows - i, 1) if i else v

    def mix(ready):
        mixed = jnp.dot(
            w, jnp.concatenate([r for _, _, r in ready], axis=1), preferred_element_type=f32
        )
        for k, (s, i, _) in enumerate(ready):
            m = mixed[:, k * rows : (k + 1) * rows]
            if len(refs) == 1:
                refs[0][s, i] = m
            else:
                level0, out, flux = refs
                x = here * block + i
                out[s, i] = m
                flux[s, pl.ds(x, 1), :] = level0[s, pl.ds(x, 1), :] + m[0:1]

    for i in range(block):
        cl, cw = clon[i], clat[i]
        cl_west = clon[i - 1] if i else jnp.where(at_start, clon_col[0], clon_before[0])
        e = jnp.maximum(cl, 0.0) + kappa_mix
        w_ = kappa_mix - jnp.minimum(cl_west, 0.0)
        n = (jnp.maximum(cw, 0.0) + kappa_mix) * inside
        cs = jnp.where(first, back(courant_south, i), pltpu.roll(cw, 1, 1))
        s_ = (kappa_mix - jnp.minimum(cs, 0.0)) * below
        centre = 1.0 - (e + w_ + n + s_)
        for s in range(species):
            v = field[s, i]
            v_w = field[s, i - 1] if i else jnp.where(at_start, west_col[s], field_west[s, 0])
            v_e = field[s, i + 1] if i < block - 1 else jnp.where(at_end, east_col[s], field_east[s, 0])
            v_n = jnp.where(last, back(norths[s], i), pltpu.roll(v, rows - 1, 1))
            v_s = jnp.where(first, back(souths[s], i), pltpu.roll(v, 1, 1))
            h = centre * v + e * v_e + w_ * v_w + n * v_n + s_ * v_s
            high, low = split(h)
            waiting.append((s, i, jnp.concatenate([high, low, high], axis=0).astype(bf16)))
            if len(waiting) == 2:
                mix(waiting)
                waiting.clear()
    if waiting:
        mix(waiting)


def step(lat, field, clon, clat, halo, weights, lat_size, level0=None):
    species, cols, levels, rows = field.shape
    shapes = [jax.ShapeDtypeStruct(field.shape, f32)]
    columns = pl.BlockSpec((species, BLOCK, levels, rows), lambda i: (0, i, 0, 0))
    courant = pl.BlockSpec((BLOCK, levels, rows), lambda i: (i, 0, 0))
    out_specs = [columns]
    whole = lambda shape: pl.BlockSpec(shape, lambda i: (0,) * len(shape))
    part = lambda at: pl.BlockSpec((1, levels, rows), lambda i: (at, 0, 0))
    more = ()
    if level0 is not None:
        more = (level0,)
        shapes.append(jax.ShapeDtypeStruct(level0.shape, f32))
        out_specs.append(whole(level0.shape))
    west, east, clon_west, south, north, clat_south = halo
    three = whole((species, levels, rows))
    return pl.pallas_call(
        functools.partial(step_kernel, lat_size=lat_size),
        out_shape=shapes,
        grid=(cols // BLOCK,),
        in_specs=[
            pl.BlockSpec(memory_space=pltpu.SMEM),
            columns,
            pl.BlockSpec((species, 1, levels, rows), lambda i: (0, jnp.maximum(i * BLOCK - 1, 0), 0, 0)),
            pl.BlockSpec((species, 1, levels, rows), lambda i: (0, jnp.minimum(i * BLOCK + BLOCK, cols - 1), 0, 0)),
            courant,
            pl.BlockSpec((1, levels, rows), lambda i: (jnp.maximum(i * BLOCK - 1, 0), 0, 0)),
            courant,
            three,
            three,
            part(species),
            three,
            three,
            part(species),
            whole(weights.shape),
            *[whole(m.shape) for m in more],
        ],
        out_specs=out_specs,
        compiler_params=pltpu.CompilerParams(vmem_limit_bytes=VMEM_LIMIT),
        cost_estimate=pl.CostEstimate(
            flops=field.size * levels * 6, bytes_accessed=field.size * 12, transcendentals=0
        ),
    )(
        lat,
        field,
        field,
        field,
        clon,
        clon,
        clat,
        west,
        east,
        clon_west,
        south,
        north,
        clat_south,
        weights,
        *more,
    )


def add_kernel(
    got_at,
    plain,
    table,
    first,
    up,
    down,
    west,
    east,
    level0,
    got,
    parts,
    group,
    spot,
    total,
    held_field,
    sem_in,
    sem_got,
    sem_out,
):
    sources, held, slots = got_at.shape
    species, cols, levels, rows = plain.shape
    akl = table.shape[1] // 4
    quarters = sem_got.shape[0]
    quarter = sources // quarters
    came = [
        pltpu.make_async_copy(got_at.at[pl.ds(q * quarter, quarter)], got.at[pl.ds(q * quarter, quarter)], sem_got.at[q])
        for q in range(quarters)
    ]
    for copy in came:
        copy.start()
    fetch = pltpu.make_async_copy(plain, held_field, sem_in)
    fetch.start()
    iota_w = lax.broadcasted_iota(jnp.int32, (WIDE, WIDE), 0)
    second = (lax.broadcasted_iota(jnp.int32, (4 * akl, WIDE), 0) >= 2 * akl).astype(f32)

    def prepare(g, carry):
        for i in range(2):
            b = 2 * g + i
            row = jnp.concatenate([got[2 * b], got[2 * b + 1]], axis=1)
            at = pl.ds(pl.multiple_of(b * WIDE, WIDE), WIDE)
            segment = row[akl : akl + 1].astype(jnp.int32)
            spot[:, at] = jnp.where(iota_w == (segment & (WIDE - 1)), 1.0, 0.0).astype(bf16)
            group[:, at] = ((segment >> 8).astype(f32) - second).astype(bf16)
            high, low = split(row[:akl])
            both = jnp.concatenate([high, low], axis=0)
            parts[:, at] = jnp.concatenate([both, both], axis=0).astype(bf16)
        return carry

    for q, copy in enumerate(came):
        copy.wait()
        lax.fori_loop(q * quarter // 4, (q + 1) * quarter // 4, prepare, 0)
    onehot_product(parts, group, spot, total, -(-species * cols // 4), 2, *ADD)

    up[...] = jnp.zeros_like(up)
    down[...] = jnp.zeros_like(down)
    t = table[...]
    fetch.wait()
    blocks = cols // BLOCK

    def leave(s, b):
        at = pl.ds(b * BLOCK, BLOCK)
        return pltpu.make_async_copy(held_field.at[s, at], first.at[s, at], sem_out.at[s, b])

    for s in range(species):

        def columns(b, carry):
            done = []
            for i in range(BLOCK):
                x = b * BLOCK + i
                sx = s * cols + x
                pair = total[
                    pl.ds(pl.multiple_of((sx >> 1) * 2 * akl, 8), 2 * akl),
                    pl.ds(pl.multiple_of((sx & 1) * rows, rows), rows),
                ]
                high, low = split(pair)
                forcing = jnp.dot(
                    t, jnp.concatenate([high, low], axis=0).astype(bf16), preferred_element_type=f32
                )
                v = held_field[s, x] + forcing
                held_field[s, x] = v
                level0[s, pl.ds(x, 1), :] = v[0:1]
                done.append(v)
            up[s] = edge_lanes(done, up[s], b * BLOCK, 1)
            down[s] = edge_lanes(done, down[s], b * BLOCK, 0)
            leave(s, b).start()
            return carry

        lax.fori_loop(0, blocks, columns, 0)
        east[s] = held_field[s, 0]
        west[s] = held_field[s, cols - 1]
    for s in range(species):
        for b in range(blocks):
            leave(s, b).wait()


def add_soundings(got, plain, table):
    sources, held, slots = got.shape
    species, cols, levels, rows = plain.shape
    akl = table.shape[1] // 4
    length = sources * slots
    pairs = -(-species * cols // 4)
    edge = jax.ShapeDtypeStruct((species, levels, rows), f32)
    vmem, hbm = pl.BlockSpec(memory_space=pltpu.VMEM), pl.BlockSpec(memory_space=pl.ANY)
    return pl.pallas_call(
        add_kernel,
        out_shape=(
            jax.ShapeDtypeStruct(plain.shape, f32),
            edge,
            edge,
            edge,
            edge,
            jax.ShapeDtypeStruct((species, cols, rows), f32),
        ),
        in_specs=[hbm, hbm, vmem],
        out_specs=(hbm, vmem, vmem, vmem, vmem, vmem),
        scratch_shapes=(
            pltpu.VMEM(got.shape, f32),
            pltpu.VMEM((4 * akl, length), bf16),
            pltpu.VMEM((4 * akl, length), bf16),
            pltpu.VMEM((WIDE, length), bf16),
            pltpu.VMEM((pairs * 4 * akl, WIDE), f32),
            pltpu.VMEM(plain.shape, f32),
            pltpu.SemaphoreType.DMA,
            pltpu.SemaphoreType.DMA((4,)),
            pltpu.SemaphoreType.DMA((species, cols // BLOCK)),
        ),
        compiler_params=pltpu.CompilerParams(vmem_limit_bytes=ADD_LIMIT),
        cost_estimate=pl.CostEstimate(
            flops=2 * pairs * 4 * akl * WIDE * length,
            bytes_accessed=4 * (got.size + 2 * plain.size),
            transcendentals=0,
        ),
    )(got, plain, table)


def on_device(
    adjoint_in,
    courant_lon,
    courant_lat,
    vertical_mix,
    sounding_values,
    sounding_dest,
    sounding_target,
    level_index,
):
    lat_size, lon_size = lax.axis_size("lat"), lax.axis_size("lon")
    n_tiles = lat_size * lon_size
    species, levels, cols, rows = adjoint_in.shape
    east_way = [(i, (i + 1) % lon_size) for i in range(lon_size)]
    west_way = [(j, i) for i, j in east_way]
    north_way = [(i, i + 1) for i in range(lat_size - 1)]
    south_way = [(j, i) for i, j in north_way]

    field = adjoint_in.transpose(0, 2, 1, 3)
    clon = courant_lon.transpose(1, 0, 2)
    clat = courant_lat.transpose(1, 0, 2)
    lat = lax.axis_index("lat").reshape(1)

    up, down, west, east = edges(field, clat, clon)
    south = lax.ppermute(up, "lat", north_way)
    north = lax.ppermute(down, "lat", south_way)
    west = lax.ppermute(west, "lon", east_way)
    east = lax.ppermute(east, "lon", west_way)
    sent = pack(sounding_dest, sounding_values, sounding_target, n_tiles, species, cols, rows)
    sent, south, north, west, east = lax.optimization_barrier((sent, south, north, west, east))
    clat_south, clon_west = south, west
    got = lax.all_to_all(sent, ("lat", "lon"), split_axis=0, concat_axis=0, tiled=True)

    weights = mix_weights(vertical_mix)
    table = (jnp.arange(levels, dtype=jnp.int32)[:, None] == level_index[None, :]).astype(bf16)
    table = jnp.concatenate([table] * 4, axis=1)
    (plain,) = step(lat, field, clon, clat, (west, east, clon_west, south, north, clat_south), weights, lat_size)
    first, up, down, west, east, level0 = add_soundings(got, plain, table)
    south = lax.ppermute(up, "lat", north_way)
    north = lax.ppermute(down, "lat", south_way)
    west = lax.ppermute(west, "lon", east_way)
    east = lax.ppermute(east, "lon", west_way)
    out, flux = step(
        lat, first, clon, clat, (west, east, clon_west, south, north, clat_south), weights, lat_size, level0
    )
    return out.transpose(0, 2, 1, 3), flux


def solution(mesh):
    return jax.shard_map(
        on_device,
        mesh=mesh,
        in_specs=(
            P(None, None, "lon", "lat"),
            P(None, "lon", "lat"),
            P(None, "lon", "lat"),
            P(),
            P(None, ("lat", "lon")),
            P(("lat", "lon"), None),
            P(("lat", "lon")),
            P(),
        ),
        out_specs=(P(None, None, "lon", "lat"), P(None, "lon", "lat")),
        check_vma=False,
    )
```

```python
import functools

import jax
import jax.numpy as jnp
from jax import lax
from jax.experimental import pallas as pl
from jax.experimental.pallas import tpu as pltpu
from jax.sharding import PartitionSpec as P

kappa_mix = 0.05
LANES = 128
WIDE = 256
f32 = jnp.float32
bf16 = jnp.bfloat16
BLOCK = 15
VMEM_LIMIT = 52 * 2**20
ADD_LIMIT = 49 * 2**20


def call(kernel, out_shape, *args, scratch=(), smem=(), flops=0, nbytes=0):
    specs = [
        pl.BlockSpec(memory_space=pltpu.SMEM if i in smem else pltpu.VMEM) for i in range(len(args))
    ]
    return pl.pallas_call(
        kernel,
        out_shape=out_shape,
        in_specs=specs,
        out_specs=jax.tree.map(lambda _: pl.BlockSpec(memory_space=pltpu.VMEM), out_shape),
        scratch_shapes=list(scratch),
        compiler_params=pltpu.CompilerParams(vmem_limit_bytes=VMEM_LIMIT),
        cost_estimate=pl.CostEstimate(flops=flops, bytes_accessed=nbytes, transcendentals=0),
    )(*args)


def split(value):
    high = value.astype(bf16).astype(f32)
    return high, value - high


def nt_dot(a, b):
    return lax.dot_general(a, b, (((1,), (1,)), ((), ())), preferred_element_type=f32)


def onehot_product(parts, group, spot, total, count, step, together, depth):
    rows, length = parts.shape
    chunks = length // depth

    def of_group(g, carry):
        def of_chunk(c, carry):
            at = pl.ds(pl.multiple_of(c * depth, depth), depth)
            held, key = parts[:, at], group[:, at]
            left = jnp.concatenate(
                [
                    jnp.where(
                        key == ((g * together + i) * step).astype(f32).astype(bf16), held, jnp.zeros_like(held)
                    )
                    for i in range(together)
                ],
                axis=0,
            )
            product = nt_dot(left, spot[:, at])
            to = pl.ds(pl.multiple_of(g * (together * rows), together * rows), together * rows)
            if chunks == 1:
                total[to, :] = product
            else:

                @pl.when(c == 0)
                def _():
                    total[to, :] = product

                @pl.when(c > 0)
                def _():
                    total[to, :] += product

            return carry

        return lax.fori_loop(0, chunks, of_chunk, carry)

    lax.fori_loop(0, count // together, of_group, 0)


PACK = (16, 8192)
ADD = (17, 4096)


def whole_part(value, divisor):
    return ((value.astype(f32) + 0.5) * (1.0 / divisor)).astype(jnp.int32)


def pack_kernel(dest, values, target, out, parts, group, spot, total, *, species, cols, rows):
    n_tiles, held, _ = out.shape
    levels, length = values.shape
    iota_t = lax.broadcasted_iota(jnp.int32, (n_tiles, WIDE), 0)
    square = (WIDE, WIDE)
    upper = (
        lax.broadcasted_iota(jnp.int32, square, 0) < lax.broadcasted_iota(jnp.int32, square, 1)
    ).astype(f32).astype(bf16)
    iota_w = lax.broadcasted_iota(jnp.int32, square, 0)

    def rank(at, base):
        d = dest[:, at]
        hot = iota_t == d
        hot_f = jnp.where(hot, 1.0, 0.0)
        earlier = jnp.dot(hot_f.astype(bf16), upper, preferred_element_type=f32) + base
        own = jnp.sum(jnp.where(hot, earlier, 0.0), axis=0, keepdims=True).astype(jnp.int32)
        low = own + (d & 1) * LANES
        spot[:, at] = jnp.where(iota_w == low, 1.0, 0.0).astype(bf16)
        group[:, at] = jnp.broadcast_to((d >> 1).astype(f32), (2 * held, WIDE)).astype(bf16)
        t = target[:, at]
        cell = whole_part(t, species)
        row_of = whole_part(cell, cols)
        segment = ((t - cell * species) * cols + cell - row_of * cols) * rows + row_of
        row = jnp.concatenate(
            [values[:, at], segment.astype(f32), jnp.zeros((held - levels - 1, WIDE), f32)], axis=0
        )
        parts[:, at] = jnp.concatenate(split(row), axis=0).astype(bf16)
        return base + jnp.sum(hot_f, axis=1, keepdims=True)

    def ranks(b, base):
        for i in range(4):
            base = rank(pl.ds(pl.multiple_of((4 * b + i) * WIDE, WIDE), WIDE), base)
        return base

    lax.fori_loop(0, length // (4 * WIDE), ranks, jnp.zeros((n_tiles, 1), f32))
    onehot_product(parts, group, spot, total, n_tiles // 2, 1, *PACK)

    def put(g, carry):
        for i in range(4):
            j = 4 * g + i
            at = pl.multiple_of(j * 2 * held, 2 * held)
            both = total[pl.ds(at, held), :] + total[pl.ds(at + held, held), :]
            out[2 * j] = both[:, :LANES]
            out[2 * j + 1] = both[:, LANES:]
        return carry

    lax.fori_loop(0, n_tiles // 8, put, 0)


def pack(dest, values, target, n_tiles, species, cols, rows):
    levels, length = values.shape
    held = -(-(levels + 1) // 8) * 8
    scratch = (
        pltpu.VMEM((2 * held, length), bf16),
        pltpu.VMEM((2 * held, length), bf16),
        pltpu.VMEM((WIDE, length), bf16),
        pltpu.VMEM((n_tiles // 2 * 2 * held, WIDE), f32),
    )
    return call(
        functools.partial(pack_kernel, species=species, cols=cols, rows=rows),
        jax.ShapeDtypeStruct((n_tiles, held, LANES), f32),
        dest.reshape(1, length),
        values,
        target.reshape(1, length),
        scratch=scratch,
        flops=2 * length * n_tiles * LANES * 2 * held,
        nbytes=4 * (length * 22 + n_tiles * held * LANES),
    )


def edge_lanes(columns, kept, first, by):
    lane = lax.broadcasted_iota(jnp.int32, kept.shape, 1)
    own = kept
    for i, v in enumerate(columns):
        own = jnp.where(lane == i, pltpu.roll(v, i + by, 1), own)
    inside = jnp.logical_and(lane >= first, lane < first + len(columns))
    return jnp.where(inside, pltpu.roll(own, first, 1), kept)


def edges_kernel(field, clat, clon_last, up, down, west, east):
    species, block, levels, rows = field.shape
    here = pl.program_id(0)
    first = here * block

    @pl.when(here == 0)
    def _():
        up[...] = jnp.zeros_like(up)
        down[...] = jnp.zeros_like(down)
        for s in range(species):
            east[s] = field[s, 0]

    @pl.when(here == pl.num_programs(0) - 1)
    def _():
        for s in range(species):
            west[s] = field[s, block - 1]
        west[species] = clon_last[0]

    for s in range(species + 1):
        columns = [field[s, i] if s < species else clat[i] for i in range(block)]
        up[s] = edge_lanes(columns, up[s], first, 1)
        if s < species:
            down[s] = edge_lanes(columns, down[s], first, 0)


def edges(field, clat, clon):
    species, cols, levels, rows = field.shape
    four, three = (species + 1, levels, rows), (species, levels, rows)
    shapes = (four, three, four, three)
    return pl.pallas_call(
        edges_kernel,
        out_shape=tuple(jax.ShapeDtypeStruct(shape, f32) for shape in shapes),
        grid=(cols // BLOCK,),
        in_specs=[
            pl.BlockSpec((species, BLOCK, levels, rows), lambda i: (0, i, 0, 0)),
            pl.BlockSpec((BLOCK, levels, rows), lambda i: (i, 0, 0)),
            pl.BlockSpec((1, levels, rows), lambda i: (cols - 1, 0, 0)),
        ],
        out_specs=tuple(pl.BlockSpec(shape, lambda i: (0, 0, 0)) for shape in shapes),
        compiler_params=pltpu.CompilerParams(vmem_limit_bytes=VMEM_LIMIT),
        cost_estimate=pl.CostEstimate(flops=field.size * 4, bytes_accessed=field.size * 5, transcendentals=0),
    )(field, clat, clon)


def mix_weights(vertical_mix):
    levels = vertical_mix.shape[0]
    matrix = (jnp.eye(levels, dtype=f32) + vertical_mix).T
    high = lax.reduce_precision(matrix, 8, 7)
    return jnp.concatenate([high, high, matrix - high], axis=1).astype(bf16)


def step_kernel(
    lat_ref,
    field,
    field_west,
    field_east,
    clon,
    clon_before,
    clat,
    west_col,
    east_col,
    clon_col,
    south,
    north,
    clat_south,
    weights,
    *refs,
    lat_size,
):
    species, block, levels, rows = field.shape
    lane = lax.broadcasted_iota(jnp.int32, (levels, rows), 1)
    first, last = lane == 0, lane == rows - 1
    lat = lat_ref[0]
    below = jnp.where(jnp.logical_and(first, lat == 0), 0.0, 1.0)
    inside = jnp.where(jnp.logical_and(last, lat == lat_size - 1), 0.0, 1.0)
    w = weights[...]
    here = pl.program_id(0)
    at_start, at_end = here == 0, here == pl.num_programs(0) - 1
    start = here * block
    south_on = lax.rem(rows - start, rows)
    north_on = rows - 1 - start
    souths = [pltpu.roll(south[s], south_on, 1) for s in range(species)]
    norths = [pltpu.roll(north[s], north_on, 1) for s in range(species)]
    courant_south = pltpu.roll(clat_south[0], south_on, 1)
    waiting = []

    def back(v, i):
        return pltpu.roll(v, rows - i, 1) if i else v

    def mix(ready):
        mixed = jnp.dot(
            w, jnp.concatenate([r for _, _, r in ready], axis=1), preferred_element_type=f32
        )
        for k, (s, i, _) in enumerate(ready):
            m = mixed[:, k * rows : (k + 1) * rows]
            if len(refs) == 1:
                refs[0][s, i] = m
            else:
                level0, out, flux = refs
                x = here * block + i
                out[s, i] = m
                flux[s, pl.ds(x, 1), :] = level0[s, pl.ds(x, 1), :] + m[0:1]

    for i in range(block):
        cl, cw = clon[i], clat[i]
        cl_west = clon[i - 1] if i else jnp.where(at_start, clon_col[0], clon_before[0])
        e = jnp.maximum(cl, 0.0) + kappa_mix
        w_ = kappa_mix - jnp.minimum(cl_west, 0.0)
        n = (jnp.maximum(cw, 0.0) + kappa_mix) * inside
        cs = jnp.where(first, back(courant_south, i), pltpu.roll(cw, 1, 1))
        s_ = (kappa_mix - jnp.minimum(cs, 0.0)) * below
        centre = 1.0 - (e + w_ + n + s_)
        for s in range(species):
            v = field[s, i]
            v_w = field[s, i - 1] if i else jnp.where(at_start, west_col[s], field_west[s, 0])
            v_e = field[s, i + 1] if i < block - 1 else jnp.where(at_end, east_col[s], field_east[s, 0])
            v_n = jnp.where(last, back(norths[s], i), pltpu.roll(v, rows - 1, 1))
            v_s = jnp.where(first, back(souths[s], i), pltpu.roll(v, 1, 1))
            h = centre * v + e * v_e + w_ * v_w + n * v_n + s_ * v_s
            high, low = split(h)
            waiting.append((s, i, jnp.concatenate([high, low, high], axis=0).astype(bf16)))
            if len(waiting) == 2:
                mix(waiting)
                waiting.clear()
    if waiting:
        mix(waiting)


def step(lat, field, clon, clat, halo, weights, lat_size, level0=None):
    species, cols, levels, rows = field.shape
    shapes = [pltpu.HBM(field.shape, f32)]
    columns = pl.BlockSpec((species, BLOCK, levels, rows), lambda i: (0, i, 0, 0))
    courant = pl.BlockSpec((BLOCK, levels, rows), lambda i: (i, 0, 0))
    out_specs = [columns]
    whole = lambda shape: pl.BlockSpec(shape, lambda i: (0,) * len(shape))
    part = lambda at: pl.BlockSpec((1, levels, rows), lambda i: (at, 0, 0))
    more = ()
    if level0 is not None:
        more = (level0,)
        shapes.append(jax.ShapeDtypeStruct(level0.shape, f32))
        out_specs.append(whole(level0.shape))
    west, east, clon_west, south, north, clat_south = halo
    three = whole((species, levels, rows))
    return pl.pallas_call(
        functools.partial(step_kernel, lat_size=lat_size),
        out_shape=shapes,
        grid=(cols // BLOCK,),
        in_specs=[
            pl.BlockSpec(memory_space=pltpu.SMEM),
            columns,
            pl.BlockSpec((species, 1, levels, rows), lambda i: (0, jnp.maximum(i * BLOCK - 1, 0), 0, 0)),
            pl.BlockSpec((species, 1, levels, rows), lambda i: (0, jnp.minimum(i * BLOCK + BLOCK, cols - 1), 0, 0)),
            courant,
            pl.BlockSpec((1, levels, rows), lambda i: (jnp.maximum(i * BLOCK - 1, 0), 0, 0)),
            courant,
            three,
            three,
            part(species),
            three,
            three,
            part(species),
            whole(weights.shape),
            *[whole(m.shape) for m in more],
        ],
        out_specs=out_specs,
        compiler_params=pltpu.CompilerParams(vmem_limit_bytes=VMEM_LIMIT),
        cost_estimate=pl.CostEstimate(
            flops=field.size * levels * 6, bytes_accessed=field.size * 12, transcendentals=0
        ),
    )(
        lat,
        field,
        field,
        field,
        clon,
        clon,
        clat,
        west,
        east,
        clon_west,
        south,
        north,
        clat_south,
        weights,
        *more,
    )


def add_kernel(
    got_at,
    plain,
    table,
    first,
    up,
    down,
    west,
    east,
    level0,
    got,
    parts,
    group,
    spot,
    total,
    held_field,
    sem_in,
    sem_got,
    sem_out,
):
    sources, held, slots = got_at.shape
    species, cols, levels, rows = plain.shape
    akl = table.shape[1] // 4
    quarters = sem_got.shape[0]
    quarter = sources // quarters
    came = [
        pltpu.make_async_copy(got_at.at[pl.ds(q * quarter, quarter)], got.at[pl.ds(q * quarter, quarter)], sem_got.at[q])
        for q in range(quarters)
    ]
    for copy in came:
        copy.start()
    fetch = pltpu.make_async_copy(plain, held_field, sem_in)
    fetch.start()
    iota_w = lax.broadcasted_iota(jnp.int32, (WIDE, WIDE), 0)
    second = (lax.broadcasted_iota(jnp.int32, (4 * akl, WIDE), 0) >= 2 * akl).astype(f32)

    def prepare(g, carry):
        for i in range(2):
            b = 2 * g + i
            row = jnp.concatenate([got[2 * b], got[2 * b + 1]], axis=1)
            at = pl.ds(pl.multiple_of(b * WIDE, WIDE), WIDE)
            segment = row[akl : akl + 1].astype(jnp.int32)
            spot[:, at] = jnp.where(iota_w == (segment & (WIDE - 1)), 1.0, 0.0).astype(bf16)
            group[:, at] = ((segment >> 8).astype(f32) - second).astype(bf16)
            high, low = split(row[:akl])
            both = jnp.concatenate([high, low], axis=0)
            parts[:, at] = jnp.concatenate([both, both], axis=0).astype(bf16)
        return carry

    for q, copy in enumerate(came):
        copy.wait()
        lax.fori_loop(q * quarter // 4, (q + 1) * quarter // 4, prepare, 0)
    onehot_product(parts, group, spot, total, -(-species * cols // 4), 2, *ADD)

    up[...] = jnp.zeros_like(up)
    down[...] = jnp.zeros_like(down)
    t = table[...]
    fetch.wait()
    blocks = cols // BLOCK

    def leave(s, b):
        at = pl.ds(b * BLOCK, BLOCK)
        return pltpu.make_async_copy(held_field.at[s, at], first.at[s, at], sem_out.at[s, b])

    for s in range(species):

        def columns(b, carry):
            done = []
            for i in range(BLOCK):
                x = b * BLOCK + i
                sx = s * cols + x
                pair = total[
                    pl.ds(pl.multiple_of((sx >> 1) * 2 * akl, 8), 2 * akl),
                    pl.ds(pl.multiple_of((sx & 1) * rows, rows), rows),
                ]
                high, low = split(pair)
                forcing = jnp.dot(
                    t, jnp.concatenate([high, low], axis=0).astype(bf16), preferred_element_type=f32
                )
                v = held_field[s, x] + forcing
                held_field[s, x] = v
                level0[s, pl.ds(x, 1), :] = v[0:1]
                done.append(v)
            up[s] = edge_lanes(done, up[s], b * BLOCK, 1)
            down[s] = edge_lanes(done, down[s], b * BLOCK, 0)
            leave(s, b).start()
            return carry

        lax.fori_loop(0, blocks, columns, 0)
        east[s] = held_field[s, 0]
        west[s] = held_field[s, cols - 1]
    for s in range(species):
        for b in range(blocks):
            leave(s, b).wait()


def add_soundings(got, plain, table):
    sources, held, slots = got.shape
    species, cols, levels, rows = plain.shape
    akl = table.shape[1] // 4
    length = sources * slots
    pairs = -(-species * cols // 4)
    edge = jax.ShapeDtypeStruct((species, levels, rows), f32)
    vmem, hbm = pl.BlockSpec(memory_space=pltpu.VMEM), pl.BlockSpec(memory_space=pl.ANY)
    return pl.pallas_call(
        add_kernel,
        out_shape=(
            pltpu.HBM(plain.shape, f32),
            edge,
            edge,
            edge,
            edge,
            jax.ShapeDtypeStruct((species, cols, rows), f32),
        ),
        in_specs=[hbm, pl.BlockSpec(memory_space=pltpu.HBM), vmem],
        out_specs=(hbm, vmem, vmem, vmem, vmem, vmem),
        scratch_shapes=(
            pltpu.VMEM(got.shape, f32),
            pltpu.VMEM((4 * akl, length), bf16),
            pltpu.VMEM((4 * akl, length), bf16),
            pltpu.VMEM((WIDE, length), bf16),
            pltpu.VMEM((pairs * 4 * akl, WIDE), f32),
            pltpu.VMEM(plain.shape, f32),
            pltpu.SemaphoreType.DMA,
            pltpu.SemaphoreType.DMA((4,)),
            pltpu.SemaphoreType.DMA((species, cols // BLOCK)),
        ),
        compiler_params=pltpu.CompilerParams(vmem_limit_bytes=ADD_LIMIT),
        cost_estimate=pl.CostEstimate(
            flops=2 * pairs * 4 * akl * WIDE * length,
            bytes_accessed=4 * (got.size + 2 * plain.size),
            transcendentals=0,
        ),
    )(got, plain, table)


def on_device(
    adjoint_in,
    courant_lon,
    courant_lat,
    vertical_mix,
    sounding_values,
    sounding_dest,
    sounding_target,
    level_index,
):
    lat_size, lon_size = lax.axis_size("lat"), lax.axis_size("lon")
    n_tiles = lat_size * lon_size
    species, levels, cols, rows = adjoint_in.shape
    east_way = [(i, (i + 1) % lon_size) for i in range(lon_size)]
    west_way = [(j, i) for i, j in east_way]
    north_way = [(i, (i + 1) % lat_size) for i in range(lat_size)]
    south_way = [(j, i) for i, j in north_way]

    field = adjoint_in.transpose(0, 2, 1, 3)
    clon = courant_lon.transpose(1, 0, 2)
    clat = courant_lat.transpose(1, 0, 2)
    lat = lax.axis_index("lat").reshape(1)

    up, down, west, east = edges(field, clat, clon)
    south = lax.ppermute(up, "lat", north_way)
    north = lax.ppermute(down, "lat", south_way)
    west = lax.ppermute(west, "lon", east_way)
    east = lax.ppermute(east, "lon", west_way)
    sent = pack(sounding_dest, sounding_values, sounding_target, n_tiles, species, cols, rows)
    sent, south, north, west, east = lax.optimization_barrier((sent, south, north, west, east))
    clat_south, clon_west = south, west
    got = lax.all_to_all(sent, ("lat", "lon"), split_axis=0, concat_axis=0, tiled=True)

    weights = mix_weights(vertical_mix)
    table = (jnp.arange(levels, dtype=jnp.int32)[:, None] == level_index[None, :]).astype(bf16)
    table = jnp.concatenate([table] * 4, axis=1)
    (plain,) = step(lat, field, clon, clat, (west, east, clon_west, south, north, clat_south), weights, lat_size)
    first, up, down, west, east, level0 = add_soundings(got, plain, table)
    south = lax.ppermute(up, "lat", north_way)
    north = lax.ppermute(down, "lat", south_way)
    west = lax.ppermute(west, "lon", east_way)
    east = lax.ppermute(east, "lon", west_way)
    out, flux = step(
        lat, first, clon, clat, (west, east, clon_west, south, north, clat_south), weights, lat_size, level0
    )
    return out.transpose(0, 2, 1, 3), flux


def solution(mesh):
    return jax.shard_map(
        on_device,
        mesh=mesh,
        in_specs=(
            P(None, None, "lon", "lat"),
            P(None, "lon", "lat"),
            P(None, "lon", "lat"),
            P(),
            P(None, ("lat", "lon")),
            P(("lat", "lon"), None),
            P(("lat", "lon")),
            P(),
        ),
        out_specs=(P(None, None, "lon", "lat"), P(None, "lon", "lat")),
        check_vma=False,
    )
```

```python
import functools

import jax
import jax.numpy as jnp
from jax import lax
from jax.experimental import pallas as pl
from jax.experimental.pallas import tpu as pltpu
from jax.sharding import PartitionSpec as P

kappa_mix = 0.05
LANES = 128
WIDE = 256
f32 = jnp.float32
bf16 = jnp.bfloat16
BLOCK = 15
VMEM_LIMIT = 52 * 2**20
PACK_LIMIT = 58 * 2**20
ADD_LIMIT = 49 * 2**20


def split(value):
    high = value.astype(bf16).astype(f32)
    return high, value - high


def nt_dot(a, b):
    return lax.dot_general(a, b, (((1,), (1,)), ((), ())), preferred_element_type=f32)


def onehot_product(parts, group, spot, total, count, step, together, depth, beside=None):
    rows, length = parts.shape
    chunks = length // depth

    def chunk(g, c):
        at = pl.ds(pl.multiple_of(c * depth, depth), depth)
        held, key = parts[:, at], group[:, at]
        left = jnp.concatenate(
            [
                jnp.where(key == ((g * together + i) * step).astype(f32).astype(bf16), held, jnp.zeros_like(held))
                for i in range(together)
            ],
            axis=0,
        )
        return nt_dot(left, spot[:, at])

    def of_group(g, carry):
        to = pl.ds(pl.multiple_of(g * (together * rows), together * rows), together * rows)
        if beside is not None:
            beside(g)
        if chunks == 1:
            total[to, :] = chunk(g, 0)
            return carry

        def of_chunk(c, carry):
            product = chunk(g, c)

            @pl.when(c == 0)
            def _():
                total[to, :] = product

            @pl.when(c > 0)
            def _():
                total[to, :] += product

            return carry

        return lax.fori_loop(0, chunks, of_chunk, carry)

    lax.fori_loop(0, count // together, of_group, 0)


def edge_lanes(columns, kept, first, up, share=None):
    rows = kept.shape[1]
    lane = lax.broadcasted_iota(jnp.int32, kept.shape, 1)
    own = jnp.zeros_like(kept)
    for i, v in enumerate(columns):
        if up:
            own = jnp.where(lane == 2 * i, pltpu.roll(v, 2 * i + 1, 1), own)
        else:
            own = jnp.where(lane == 2 * i + 1, pltpu.roll(v, 2 * i + 1, 1), own)
    if share is not None:
        own = own * share
    turn = 2 * first if up else lax.rem(2 * first + rows - 2, rows)
    return kept + pltpu.roll(own, turn, 1)


PACK = (16, 8192)
ADD = (17, 4096)


def whole_part(value, divisor):
    return ((value.astype(f32) + 0.5) * (1.0 / divisor)).astype(jnp.int32)


def pack_kernel(
    dest,
    values,
    target,
    field_at,
    clon_at,
    clat_at,
    out,
    up,
    down,
    west,
    east,
    parts,
    group,
    spot,
    total,
    field,
    clat,
    sems,
):
    n_tiles, held, _ = out.shape
    species, cols, _, rows = field.shape
    copies = [(field_at, field), (clat_at, clat), (clon_at.at[cols - 1], west.at[species])]
    for s in range(species):
        copies += [(field_at.at[s, cols - 1], west.at[s]), (field_at.at[s, 0], east.at[s])]
    copies = [pltpu.make_async_copy(*pair, sems.at[i]) for i, pair in enumerate(copies)]
    for copy in copies:
        copy.start()
    up[...] = jnp.zeros_like(up)
    down[...] = jnp.zeros_like(down)
    levels, length = values.shape
    iota_t = lax.broadcasted_iota(jnp.int32, (n_tiles, WIDE), 0)
    square = (WIDE, WIDE)
    upper = (
        lax.broadcasted_iota(jnp.int32, square, 0) < lax.broadcasted_iota(jnp.int32, square, 1)
    ).astype(f32).astype(bf16)
    iota_w = lax.broadcasted_iota(jnp.int32, square, 0)

    def rank(at, base):
        d = dest[:, at]
        hot = iota_t == d
        hot_f = jnp.where(hot, 1.0, 0.0)
        earlier = jnp.dot(hot_f.astype(bf16), upper, preferred_element_type=f32) + base
        own = jnp.sum(jnp.where(hot, earlier, 0.0), axis=0, keepdims=True).astype(jnp.int32)
        low = own + (d & 1) * LANES
        spot[:, at] = jnp.where(iota_w == low, 1.0, 0.0).astype(bf16)
        group[:, at] = jnp.broadcast_to((d >> 1).astype(f32), (2 * held, WIDE)).astype(bf16)
        t = target[:, at]
        cell = whole_part(t, species)
        row_of = whole_part(cell, cols)
        segment = ((t - cell * species) * cols + cell - row_of * cols) * rows + row_of
        row = jnp.concatenate(
            [values[:, at], segment.astype(f32), jnp.zeros((held - levels - 1, WIDE), f32)], axis=0
        )
        parts[:, at] = jnp.concatenate(split(row), axis=0).astype(bf16)
        return base + jnp.sum(hot_f, axis=1, keepdims=True)

    def ranks(b, base):
        for i in range(4):
            base = rank(pl.ds(pl.multiple_of((4 * b + i) * WIDE, WIDE), WIDE), base)
        return base

    lax.fori_loop(0, length // (4 * WIDE), ranks, jnp.zeros((n_tiles, 1), f32))
    for copy in copies:
        copy.wait()
    blocks = cols // BLOCK

    def take_edges(g):
        first = jnp.minimum(g, blocks - 1) * BLOCK
        new = (g < blocks).astype(f32)
        for s in range(species + 1):
            columns = [field[s, first + i] if s < species else clat[first + i] for i in range(BLOCK)]
            up[s] = edge_lanes(columns, up[s], first, True, new)
            if s < species:
                down[s] = edge_lanes(columns, down[s], first, False, new)

    onehot_product(parts, group, spot, total, n_tiles // 2, 1, *PACK, beside=take_edges)

    def put(g, carry):
        for i in range(4):
            j = 4 * g + i
            at = pl.multiple_of(j * 2 * held, 2 * held)
            both = total[pl.ds(at, held), :] + total[pl.ds(at + held, held), :]
            out[2 * j] = both[:, :LANES]
            out[2 * j + 1] = both[:, LANES:]
        return carry

    lax.fori_loop(0, n_tiles // 8, put, 0)


def pack(dest, values, target, field, clon, clat, n_tiles):
    levels, length = values.shape
    species, cols, depth, rows = field.shape
    held = -(-(levels + 1) // 8) * 8
    four, three = (species + 1, depth, rows), (species, depth, rows)
    vmem, hbm = pl.BlockSpec(memory_space=pltpu.VMEM), pl.BlockSpec(memory_space=pl.ANY)
    return pl.pallas_call(
        pack_kernel,
        out_shape=tuple(
            jax.ShapeDtypeStruct(shape, f32) for shape in ((n_tiles, held, LANES), four, three, four, three)
        ),
        in_specs=[vmem, vmem, vmem, hbm, hbm, hbm],
        out_specs=(vmem,) * 5,
        scratch_shapes=(
            pltpu.VMEM((2 * held, length), bf16),
            pltpu.VMEM((2 * held, length), bf16),
            pltpu.VMEM((WIDE, length), bf16),
            pltpu.VMEM((n_tiles // 2 * 2 * held, WIDE), f32),
            pltpu.VMEM(field.shape, f32),
            pltpu.VMEM(clat.shape, f32),
            pltpu.SemaphoreType.DMA((3 + 2 * species,)),
        ),
        compiler_params=pltpu.CompilerParams(vmem_limit_bytes=PACK_LIMIT),
        cost_estimate=pl.CostEstimate(
            flops=2 * length * n_tiles * LANES * 2 * held,
            bytes_accessed=4 * (length * 22 + n_tiles * held * LANES + field.size),
            transcendentals=0,
        ),
    )(dest.reshape(1, length), values, target.reshape(1, length), field, clon, clat)


def mix_weights(vertical_mix):
    levels = vertical_mix.shape[0]
    matrix = (jnp.eye(levels, dtype=f32) + vertical_mix).T
    high = lax.reduce_precision(matrix, 8, 7)
    return jnp.concatenate([high, high, matrix - high], axis=1).astype(bf16)


def step_kernel(
    lat_ref,
    field,
    field_west,
    field_east,
    clon,
    clon_before,
    clat,
    west_col,
    east_col,
    clon_col,
    south,
    north,
    clat_south,
    weights,
    *refs,
    lat_size,
    second,
):
    species, block, levels, rows = field.shape
    lane = lax.broadcasted_iota(jnp.int32, (levels, rows), 1)
    first, last = lane == 0, lane == rows - 1
    lat = lat_ref[0]
    below = jnp.where(jnp.logical_and(first, lat == 0), 0.0, 1.0)
    inside = jnp.where(jnp.logical_and(last, lat == lat_size - 1), 0.0, 1.0)
    w = weights[...]
    here = pl.program_id(0)
    at_start, at_end = here == 0, here == pl.num_programs(0) - 1
    start = here * block
    turn = lax.rem(rows - 2 * start, rows)
    even = lane % 2 == 0

    def turned(a, b):
        return pltpu.roll(jnp.where(even, a, b), turn, 1)

    halos = [turned(south[s], north[s]) for s in range(species)]
    courant_south = pltpu.roll(clat_south[0], turn, 1)
    waiting = []

    def back(v, i):
        return pltpu.roll(v, rows - 2 * i, 1) if i else v

    if second:
        total, table, out, flux = refs
        t = table[...]
        akl = t.shape[1] // 4
        wanted = []
        made = {}

        def make(ready):
            forcing = jnp.dot(t, jnp.concatenate([p for _, _, p in ready], axis=1), preferred_element_type=f32)
            for k, (key, v, _) in enumerate(ready):
                made[key] = v + forcing[:, k * rows : (k + 1) * rows]

        def want(s, i, v, x):
            wanted.append(((s, i), v, spread(total, s * cols + x, rows, akl)))
            if len(wanted) == 2:
                make(wanted)
                wanted.clear()

        cols = pl.num_programs(0) * block
        for i in range(-1, block + 1):
            for s in range(species):
                if i < 0:
                    want(s, i, field_west[s, 0], jnp.maximum(start - 1, 0))
                elif i == block:
                    want(s, i, field_east[s, 0], jnp.minimum(start + block, cols - 1))
                else:
                    want(s, i, field[s, i], start + i)
        if wanted:
            make(wanted)

        def at_column(s, i):
            return made[s, i]
    else:
        out, up, down, west, east = refs
        finished = [[None] * block for _ in range(species)]

        def at_column(s, i):
            return field_west[s, 0] if i < 0 else field_east[s, 0] if i == block else field[s, i]

    def mix(ready):
        mixed = jnp.dot(
            w, jnp.concatenate([r for _, _, r in ready], axis=1), preferred_element_type=f32
        )
        for k, (s, i, _) in enumerate(ready):
            m = mixed[:, k * rows : (k + 1) * rows]
            out[s, i] = m
            if second:
                flux[s, pl.ds(start + i, 1), :] = at_column(s, i)[0:1] + m[0:1]
            else:
                finished[s][i] = m

    for i in range(block):
        cl, cw = clon[i], clat[i]
        cl_west = clon[i - 1] if i else jnp.where(at_start, clon_col[0], clon_before[0])
        e = jnp.maximum(cl, 0.0) + kappa_mix
        w_ = kappa_mix - jnp.minimum(cl_west, 0.0)
        n = (jnp.maximum(cw, 0.0) + kappa_mix) * inside
        cs = jnp.where(first, back(courant_south, i), pltpu.roll(cw, 1, 1))
        s_ = (kappa_mix - jnp.minimum(cs, 0.0)) * below
        centre = 1.0 - (e + w_ + n + s_)
        for s in range(species):
            v, v_w, v_e = at_column(s, i), at_column(s, i - 1), at_column(s, i + 1)
            if i == 0:
                v_w = jnp.where(at_start, west_col[s], v_w)
            if i == block - 1:
                v_e = jnp.where(at_end, east_col[s], v_e)
            halo = back(halos[s], i)
            v_n = jnp.where(last, halo, pltpu.roll(v, rows - 1, 1))
            v_s = jnp.where(first, halo, pltpu.roll(v, 1, 1))
            h = centre * v + e * v_e + w_ * v_w + n * v_n + s_ * v_s
            high, low = split(h)
            waiting.append((s, i, jnp.concatenate([high, low, high], axis=0).astype(bf16)))
            if len(waiting) == 2:
                mix(waiting)
                waiting.clear()
    if waiting:
        mix(waiting)
    if not second:

        @pl.when(at_start)
        def _():
            up[...] = jnp.zeros_like(up)
            down[...] = jnp.zeros_like(down)
            for s in range(species):
                east[s] = out[s, 0]

        @pl.when(at_end)
        def _():
            for s in range(species):
                west[s] = out[s, block - 1]

        for s in range(species):
            up[s] = edge_lanes(finished[s], up[s], start, True)
            down[s] = edge_lanes(finished[s], down[s], start, False)


def spread(total, sx, rows, akl):
    pair = total[
        pl.ds(pl.multiple_of((sx >> 1) * 2 * akl, 8), 2 * akl),
        pl.ds(pl.multiple_of((sx & 1) * rows, rows), rows),
    ]
    return jnp.concatenate(split(pair), axis=0).astype(bf16)


def step(lat, field, clon, clat, halo, weights, lat_size, total=None, table=None):
    species, cols, levels, rows = field.shape
    columns = pl.BlockSpec((species, BLOCK, levels, rows), lambda i: (0, i, 0, 0))
    courant = pl.BlockSpec((BLOCK, levels, rows), lambda i: (i, 0, 0))
    whole = lambda shape: pl.BlockSpec(shape, lambda i: (0,) * len(shape))
    part = lambda at: pl.BlockSpec((1, levels, rows), lambda i: (at, 0, 0))
    west, east, clon_west, south, north, clat_south = halo
    three = whole((species, levels, rows))
    second = total is not None
    more = (total, table) if second else ()
    shapes = [(species, cols, rows)] if second else [(species, levels, rows)] * 4
    return pl.pallas_call(
        functools.partial(step_kernel, lat_size=lat_size, second=second),
        out_shape=[pltpu.HBM(field.shape, f32)] + [jax.ShapeDtypeStruct(shape, f32) for shape in shapes],
        grid=(cols // BLOCK,),
        in_specs=[
            pl.BlockSpec(memory_space=pltpu.SMEM),
            columns,
            pl.BlockSpec((species, 1, levels, rows), lambda i: (0, jnp.maximum(i * BLOCK - 1, 0), 0, 0)),
            pl.BlockSpec((species, 1, levels, rows), lambda i: (0, jnp.minimum(i * BLOCK + BLOCK, cols - 1), 0, 0)),
            courant,
            pl.BlockSpec((1, levels, rows), lambda i: (jnp.maximum(i * BLOCK - 1, 0), 0, 0)),
            courant,
            three,
            three,
            part(species),
            three,
            three,
            part(species),
            whole(weights.shape),
            *[whole(m.shape) for m in more],
        ],
        out_specs=[columns] + [whole(shape) for shape in shapes],
        compiler_params=pltpu.CompilerParams(vmem_limit_bytes=VMEM_LIMIT),
        cost_estimate=pl.CostEstimate(
            flops=field.size * levels * 6, bytes_accessed=field.size * 12, transcendentals=0
        ),
    )(
        lat,
        field,
        field,
        field,
        clon,
        clon,
        clat,
        west,
        east,
        clon_west,
        south,
        north,
        clat_south,
        weights,
        *more,
    )


def add_kernel(
    got_at,
    plain_up,
    plain_down,
    plain_west,
    plain_east,
    table,
    total,
    up,
    down,
    west,
    east,
    got,
    parts,
    group,
    spot,
    sem_got,
    *,
    cols,
):
    sources, held, slots = got_at.shape
    species, levels, rows = plain_up.shape
    akl = table.shape[1] // 4
    quarters = sem_got.shape[0]
    quarter = sources // quarters
    came = [
        pltpu.make_async_copy(got_at.at[pl.ds(q * quarter, quarter)], got.at[pl.ds(q * quarter, quarter)], sem_got.at[q])
        for q in range(quarters)
    ]
    for copy in came:
        copy.start()
    iota_w = lax.broadcasted_iota(jnp.int32, (WIDE, WIDE), 0)
    second = (lax.broadcasted_iota(jnp.int32, (4 * akl, WIDE), 0) >= 2 * akl).astype(f32)

    def prepare(g, carry):
        for i in range(2):
            b = 2 * g + i
            row = jnp.concatenate([got[2 * b], got[2 * b + 1]], axis=1)
            at = pl.ds(pl.multiple_of(b * WIDE, WIDE), WIDE)
            segment = row[akl : akl + 1].astype(jnp.int32)
            spot[:, at] = jnp.where(iota_w == (segment & (WIDE - 1)), 1.0, 0.0).astype(bf16)
            group[:, at] = ((segment >> 8).astype(f32) - second).astype(bf16)
            high, low = split(row[:akl])
            both = jnp.concatenate([high, low], axis=0)
            parts[:, at] = jnp.concatenate([both, both], axis=0).astype(bf16)
        return carry

    for q, copy in enumerate(came):
        copy.wait()
        lax.fori_loop(q * quarter // 4, (q + 1) * quarter // 4, prepare, 0)
    onehot_product(parts, group, spot, total, total.shape[0] // (4 * akl), 2, *ADD)

    t = table[...]

    def forced(parts_of, before):
        return before + jnp.dot(t, parts_of, preferred_element_type=f32)

    for s in range(species):
        east[s] = forced(spread(total, s * cols, rows, akl), plain_east[s])
        west[s] = forced(spread(total, s * cols + cols - 1, rows, akl), plain_west[s])

        def of_block(b, carry):
            columns = []
            for i in range(BLOCK):
                sx = s * cols + b * BLOCK + i
                columns.append(
                    total[
                        pl.ds(pl.multiple_of((sx >> 1) * 2 * akl, 8), 2 * akl),
                        pl.ds(pl.multiple_of((sx & 1) * rows, rows), rows),
                    ]
                )
            return tuple(edge_lanes(columns, kept, b * BLOCK, k == 0) for k, kept in enumerate(carry))

        none = jnp.zeros((2 * akl, rows), f32)
        ends = lax.fori_loop(0, cols // BLOCK, of_block, (none, none))
        for end, before, after in zip(ends, (plain_up, plain_down), (up, down)):
            after[s] = forced(jnp.concatenate(split(end), axis=0).astype(bf16), before[s])


def add_soundings(got, edges, table, cols):
    sources, held, slots = got.shape
    species, levels, rows = edges[0].shape
    akl = table.shape[1] // 4
    length = sources * slots
    pairs = -(-species * cols // 4)
    edge = jax.ShapeDtypeStruct((species, levels, rows), f32)
    vmem, hbm = pl.BlockSpec(memory_space=pltpu.VMEM), pl.BlockSpec(memory_space=pl.ANY)
    return pl.pallas_call(
        functools.partial(add_kernel, cols=cols),
        out_shape=(jax.ShapeDtypeStruct((pairs * 4 * akl, WIDE), f32), edge, edge, edge, edge),
        in_specs=[hbm] + [vmem] * 5,
        out_specs=(vmem,) * 5,
        scratch_shapes=(
            pltpu.VMEM(got.shape, f32),
            pltpu.VMEM((4 * akl, length), bf16),
            pltpu.VMEM((4 * akl, length), bf16),
            pltpu.VMEM((WIDE, length), bf16),
            pltpu.SemaphoreType.DMA((4,)),
        ),
        compiler_params=pltpu.CompilerParams(vmem_limit_bytes=ADD_LIMIT),
        cost_estimate=pl.CostEstimate(
            flops=2 * pairs * 4 * akl * WIDE * length,
            bytes_accessed=4 * got.size,
            transcendentals=0,
        ),
    )(got, *edges, table)


def on_device(
    adjoint_in,
    courant_lon,
    courant_lat,
    vertical_mix,
    sounding_values,
    sounding_dest,
    sounding_target,
    level_index,
):
    lat_size, lon_size = lax.axis_size("lat"), lax.axis_size("lon")
    n_tiles = lat_size * lon_size
    species, levels, cols, rows = adjoint_in.shape
    east_way = [(i, (i + 1) % lon_size) for i in range(lon_size)]
    west_way = [(j, i) for i, j in east_way]
    north_way = [(i, (i + 1) % lat_size) for i in range(lat_size)]
    south_way = [(j, i) for i, j in north_way]

    field = adjoint_in.transpose(0, 2, 1, 3)
    clon = courant_lon.transpose(1, 0, 2)
    clat = courant_lat.transpose(1, 0, 2)
    lat = lax.axis_index("lat").reshape(1)

    sent, up, down, west, east = pack(sounding_dest, sounding_values, sounding_target, field, clon, clat, n_tiles)
    south = lax.ppermute(up, "lat", north_way)
    north = lax.ppermute(down, "lat", south_way)
    west = lax.ppermute(west, "lon", east_way)
    east = lax.ppermute(east, "lon", west_way)
    sent, south, north, west, east = lax.optimization_barrier((sent, south, north, west, east))
    clat_south, clon_west = south, west
    got = lax.all_to_all(sent, ("lat", "lon"), split_axis=0, concat_axis=0, tiled=True)

    weights = mix_weights(vertical_mix)
    table = (jnp.arange(levels, dtype=jnp.int32)[:, None] == level_index[None, :]).astype(bf16)
    table = jnp.concatenate([table] * 4, axis=1)
    plain, *own_edges = step(lat, field, clon, clat, (west, east, clon_west, south, north, clat_south), weights, lat_size)
    total, up, down, west, east = add_soundings(got, own_edges, table, cols)
    south = lax.ppermute(up, "lat", north_way)
    north = lax.ppermute(down, "lat", south_way)
    west = lax.ppermute(west, "lon", east_way)
    east = lax.ppermute(east, "lon", west_way)
    halo = (west, east, clon_west, south, north, clat_south)
    out, flux = step(lat, plain, clon, clat, halo, weights, lat_size, total, table)
    return out.transpose(0, 2, 1, 3), flux


def solution(mesh):
    return jax.shard_map(
        on_device,
        mesh=mesh,
        in_specs=(
            P(None, None, "lon", "lat"),
            P(None, "lon", "lat"),
            P(None, "lon", "lat"),
            P(),
            P(None, ("lat", "lon")),
            P(("lat", "lon"), None),
            P(("lat", "lon")),
            P(),
        ),
        out_specs=(P(None, None, "lon", "lat"), P(None, "lon", "lat")),
        check_vma=False,
    )
```

```python
import functools

import jax
import jax.numpy as jnp
from jax import lax
from jax.experimental import pallas as pl
from jax.experimental.pallas import tpu as pltpu
from jax.sharding import PartitionSpec as P

kappa_mix = 0.05
LANES = 128
WIDE = 256
f32 = jnp.float32
bf16 = jnp.bfloat16
BLOCK = 15
VMEM_LIMIT = 52 * 2**20
PACK_LIMIT = 58 * 2**20
SMALL_LIMIT = 48 * 2**20
ADD_LIMIT = 49 * 2**20


def split(value):
    high = value.astype(bf16).astype(f32)
    return high, value - high


def nt_dot(a, b):
    return lax.dot_general(a, b, (((1,), (1,)), ((), ())), preferred_element_type=f32)


def onehot_product(parts, group, spot, total, count, step, together, depth, beside=None):
    rows, length = parts.shape
    chunks = length // depth

    def chunk(g, c):
        at = pl.ds(pl.multiple_of(c * depth, depth), depth)
        held, key = parts[:, at], group[:, at]
        left = jnp.concatenate(
            [
                jnp.where(key == ((g * together + i) * step).astype(f32).astype(bf16), held, jnp.zeros_like(held))
                for i in range(together)
            ],
            axis=0,
        )
        return nt_dot(left, spot[:, at])

    def of_group(g, carry):
        to = pl.ds(pl.multiple_of(g * (together * rows), together * rows), together * rows)
        if beside is not None:
            beside(g)
        if chunks == 1:
            total[to, :] = chunk(g, 0)
            return carry

        def of_chunk(c, carry):
            product = chunk(g, c)

            @pl.when(c == 0)
            def _():
                total[to, :] = product

            @pl.when(c > 0)
            def _():
                total[to, :] += product

            return carry

        return lax.fori_loop(0, chunks, of_chunk, carry)

    lax.fori_loop(0, count // together, of_group, 0)


def edge_lanes(columns, kept, first, up, share=None):
    rows = kept.shape[1]
    lane = lax.broadcasted_iota(jnp.int32, kept.shape, 1)
    own = jnp.zeros_like(kept)
    for i, v in enumerate(columns):
        if up:
            own = jnp.where(lane == 2 * i, pltpu.roll(v, 2 * i + 1, 1), own)
        else:
            own = jnp.where(lane == 2 * i + 1, pltpu.roll(v, 2 * i + 1, 1), own)
    if share is not None:
        own = own * share
    turn = 2 * first if up else lax.rem(2 * first + rows - 2, rows)
    return kept + pltpu.roll(own, turn, 1)


PACK = (16, 8192)
ADD = (17, 8192)


def whole_part(value, divisor):
    return ((value.astype(f32) + 0.5) * (1.0 / divisor)).astype(jnp.int32)


def pack_kernel(
    dest,
    values,
    target,
    field_at,
    clon_at,
    clat_at,
    out,
    up,
    down,
    west,
    east,
    parts,
    group,
    spot,
    total,
    field,
    clat,
    sems,
):
    n_tiles, held, _ = out.shape
    species, cols, _, rows = field.shape
    copies = [(field_at, field), (clat_at, clat), (clon_at.at[cols - 1], west.at[species])]
    for s in range(species):
        copies += [(field_at.at[s, cols - 1], west.at[s]), (field_at.at[s, 0], east.at[s])]
    copies = [pltpu.make_async_copy(*pair, sems.at[i]) for i, pair in enumerate(copies)]
    for copy in copies:
        copy.start()
    up[...] = jnp.zeros_like(up)
    down[...] = jnp.zeros_like(down)
    levels, length = values.shape
    iota_t = lax.broadcasted_iota(jnp.int32, (n_tiles, WIDE), 0)
    square = (WIDE, WIDE)
    upper = (
        lax.broadcasted_iota(jnp.int32, square, 0) < lax.broadcasted_iota(jnp.int32, square, 1)
    ).astype(f32).astype(bf16)
    iota_w = lax.broadcasted_iota(jnp.int32, square, 0)

    def rank(at, base):
        d = dest[:, at]
        hot = iota_t == d
        hot_f = jnp.where(hot, 1.0, 0.0)
        earlier = jnp.dot(hot_f.astype(bf16), upper, preferred_element_type=f32) + base
        own = jnp.sum(jnp.where(hot, earlier, 0.0), axis=0, keepdims=True).astype(jnp.int32)
        low = own + (d & 1) * LANES
        spot[:, at] = jnp.where(iota_w == low, 1.0, 0.0).astype(bf16)
        group[:, at] = jnp.broadcast_to((d >> 1).astype(f32), (2 * held, WIDE)).astype(bf16)
        t = target[:, at]
        cell = whole_part(t, species)
        row_of = whole_part(cell, cols)
        segment = ((t - cell * species) * cols + cell - row_of * cols) * rows + row_of
        row = jnp.concatenate(
            [values[:, at], segment.astype(f32), jnp.zeros((held - levels - 1, WIDE), f32)], axis=0
        )
        parts[:, at] = jnp.concatenate(split(row), axis=0).astype(bf16)
        return base + jnp.sum(hot_f, axis=1, keepdims=True)

    def ranks(b, base):
        for i in range(4):
            base = rank(pl.ds(pl.multiple_of((4 * b + i) * WIDE, WIDE), WIDE), base)
        return base

    lax.fori_loop(0, length // (4 * WIDE), ranks, jnp.zeros((n_tiles, 1), f32))
    for copy in copies:
        copy.wait()
    blocks = cols // BLOCK

    def take_edges(g):
        first = jnp.minimum(g, blocks - 1) * BLOCK
        new = (g < blocks).astype(f32)
        for s in range(species + 1):
            columns = [field[s, first + i] if s < species else clat[first + i] for i in range(BLOCK)]
            up[s] = edge_lanes(columns, up[s], first, True, new)
            if s < species:
                down[s] = edge_lanes(columns, down[s], first, False, new)

    onehot_product(parts, group, spot, total, n_tiles // 2, 1, *PACK, beside=take_edges)

    def put(g, carry):
        for i in range(4):
            j = 4 * g + i
            at = pl.multiple_of(j * 2 * held, 2 * held)
            both = total[pl.ds(at, held), :] + total[pl.ds(at + held, held), :]
            out[2 * j] = both[:, :LANES]
            out[2 * j + 1] = both[:, LANES:]
        return carry

    lax.fori_loop(0, n_tiles // 8, put, 0)


def pack(dest, values, target, field, clon, clat, n_tiles):
    levels, length = values.shape
    species, cols, depth, rows = field.shape
    held = -(-(levels + 1) // 8) * 8
    four, three = (species + 1, depth, rows), (species, depth, rows)
    vmem, hbm = pl.BlockSpec(memory_space=pltpu.VMEM), pl.BlockSpec(memory_space=pl.ANY)
    return pl.pallas_call(
        pack_kernel,
        out_shape=tuple(
            jax.ShapeDtypeStruct(shape, f32) for shape in ((n_tiles, held, LANES), four, three, four, three)
        ),
        in_specs=[vmem, vmem, vmem, hbm, hbm, hbm],
        out_specs=(vmem,) * 5,
        scratch_shapes=(
            pltpu.VMEM((2 * held, length), bf16),
            pltpu.VMEM((2 * held, length), bf16),
            pltpu.VMEM((WIDE, length), bf16),
            pltpu.VMEM((n_tiles // 2 * 2 * held, WIDE), f32),
            pltpu.VMEM(field.shape, f32),
            pltpu.VMEM(clat.shape, f32),
            pltpu.SemaphoreType.DMA((3 + 2 * species,)),
        ),
        compiler_params=pltpu.CompilerParams(vmem_limit_bytes=PACK_LIMIT),
        cost_estimate=pl.CostEstimate(
            flops=2 * length * n_tiles * LANES * 2 * held,
            bytes_accessed=4 * (length * 22 + n_tiles * held * LANES + field.size),
            transcendentals=0,
        ),
    )(dest.reshape(1, length), values, target.reshape(1, length), field, clon, clat)


def mix_weights(vertical_mix):
    levels = vertical_mix.shape[0]
    matrix = (jnp.eye(levels, dtype=f32) + vertical_mix).T
    high = lax.reduce_precision(matrix, 8, 7)
    return jnp.concatenate([high, high, matrix - high], axis=1).astype(bf16)


def step_kernel(*refs, names, lat_size):
    ref = dict(zip(names, refs))
    second = "total" in ref
    field, clon, clat, out = ref["field"], ref["clon"], ref["clat"], ref["out"]
    species, block, levels, rows = field.shape
    lane = lax.broadcasted_iota(jnp.int32, (levels, rows), 1)
    first, last = lane == 0, lane == rows - 1
    here = pl.program_id(0)
    at_start, at_end = here == 0, here == pl.num_programs(0) - 1
    start = here * block
    w = ref["weights"][...]
    waiting = []

    def back(v, i):
        return pltpu.roll(v, (rows - 2 * i) % rows, 1) if i else v

    if second:
        lat = ref["lat"][0]
        below = jnp.where(jnp.logical_and(first, lat == 0), 0.0, 1.0)
        inside = jnp.where(jnp.logical_and(last, lat == lat_size - 1), 0.0, 1.0)
        turn = lax.rem(rows - 2 * start, rows)
        even = lane % 2 == 0
        ends = jnp.logical_or(first, last)
        halos = [
            pltpu.roll(jnp.where(even, ref["south"][s], ref["north"][s]), turn, 1) for s in range(species)
        ]
        left_out = [pltpu.roll(ref["lanes"][s], turn, 1) for s in range(species)]
        courant_south = pltpu.roll(ref["clat_south"][0], turn, 1)
        t = ref["table"][...]
        cols = pl.num_programs(0) * block
        wanted = []
        made = {}

        def make(ready):
            forcing = jnp.dot(t, jnp.concatenate([p for _, _, p in ready], axis=1), preferred_element_type=f32)
            for k, ((s, i), v, _) in enumerate(ready):
                v = v + forcing[:, k * rows : (k + 1) * rows] + jnp.where(ends, back(left_out[s], i), 0.0)
                if i == 0:
                    v = v + jnp.where(at_start, ref["column_start"][s], 0.0)
                if i == block - 1:
                    v = v + jnp.where(at_end, ref["column_end"][s], 0.0)
                made[s, i] = v

        for i in range(-1, block + 1):
            x = jnp.clip(start + i, 0, cols - 1)
            for s in range(species):
                v = ref["field_west"][s, 0] if i < 0 else ref["field_east"][s, 0] if i == block else field[s, i]
                wanted.append(((s, i), v, spread(ref["total"], s * cols + x, rows, t.shape[1] // 4)))
                if len(wanted) == 2:
                    make(wanted)
                    wanted.clear()
        if wanted:
            make(wanted)

        def at_column(s, i):
            return made[s, i]
    else:
        below, inside = jnp.where(first, 0.0, 1.0), jnp.where(last, 0.0, 1.0)
        finished = [[None] * block for _ in range(species)]

        def at_column(s, i):
            return ref["field_west"][s, 0] if i < 0 else ref["field_east"][s, 0] if i == block else field[s, i]

    def mix(ready):
        mixed = jnp.dot(
            w, jnp.concatenate([r for _, _, r in ready], axis=1), preferred_element_type=f32
        )
        for k, (s, i, _) in enumerate(ready):
            m = mixed[:, k * rows : (k + 1) * rows]
            out[s, i] = m
            if second:
                ref["flux"][s, pl.ds(start + i, 1), :] = at_column(s, i)[0:1] + m[0:1]
            else:
                finished[s][i] = m

    for i in range(block):
        cl, cw = clon[i], clat[i]
        cl_west = clon[i - 1] if i else ref["clon_before"][0]
        if i == 0 and second:
            cl_west = jnp.where(at_start, ref["clon_col"][0], cl_west)
        e = jnp.maximum(cl, 0.0) + kappa_mix
        w_ = kappa_mix - jnp.minimum(cl_west, 0.0)
        if not second and i == 0:
            w_ = jnp.where(at_start, 0.0, w_)
        if not second and i == block - 1:
            e = jnp.where(at_end, 0.0, e)
        n = (jnp.maximum(cw, 0.0) + kappa_mix) * inside
        cs = pltpu.roll(cw, 1, 1)
        if second:
            cs = jnp.where(first, back(courant_south, i), cs)
        s_ = (kappa_mix - jnp.minimum(cs, 0.0)) * below
        centre = 1.0 - (e + w_ + n + s_)
        for s in range(species):
            v, v_w, v_e = at_column(s, i), at_column(s, i - 1), at_column(s, i + 1)
            v_n, v_s = pltpu.roll(v, rows - 1, 1), pltpu.roll(v, 1, 1)
            if second:
                if i == 0:
                    v_w = jnp.where(at_start, ref["west_col"][s], v_w)
                if i == block - 1:
                    v_e = jnp.where(at_end, ref["east_col"][s], v_e)
                halo = back(halos[s], i)
                v_n, v_s = jnp.where(last, halo, v_n), jnp.where(first, halo, v_s)
            h = centre * v + e * v_e + w_ * v_w + n * v_n + s_ * v_s
            waiting.append((s, i, mix_parts(h)))
            if len(waiting) == 2:
                mix(waiting)
                waiting.clear()
    if waiting:
        mix(waiting)
    if not second:
        up, down, west, east = ref["up"], ref["down"], ref["west"], ref["east"]

        @pl.when(at_start)
        def _():
            up[...] = jnp.zeros_like(up)
            down[...] = jnp.zeros_like(down)
            for s in range(species):
                east[s] = out[s, 0]

        @pl.when(at_end)
        def _():
            for s in range(species):
                west[s] = out[s, block - 1]

        for s in range(species):
            up[s] = edge_lanes(finished[s], up[s], start, True)
            down[s] = edge_lanes(finished[s], down[s], start, False)


def mix_parts(h):
    high, low = split(h)
    return jnp.concatenate([high, low, high], axis=0).astype(bf16)


def left_out_kernel(
    lat_ref,
    up_own,
    down_own,
    west_own,
    east_own,
    south,
    north,
    west,
    east,
    weights,
    up_in,
    down_in,
    west_in,
    east_in,
    up,
    down,
    west_out,
    east_out,
    lanes,
    column_start,
    column_end,
    *,
    cols,
    lat_size,
):
    species, levels, rows = up_in.shape
    lane = lax.broadcasted_iota(jnp.int32, (levels, rows), 1)
    even = lane % 2 == 0
    ends = jnp.logical_or(lane == 0, lane == rows - 1)
    lat = lat_ref[0]
    below = jnp.where(lat == 0, 0.0, 1.0)
    inside = jnp.where(lat == lat_size - 1, 0.0, 1.0)
    far = 2 * (cols - 1)

    def later(v):
        return pltpu.roll(v, 1, 1)

    def sooner(v):
        return pltpu.roll(v, rows - 1, 1)

    n = (jnp.maximum(sooner(up_own[species]), 0.0) + kappa_mix) * inside
    s_ = (kappa_mix - jnp.minimum(south[species], 0.0)) * below
    w_ = kappa_mix - jnp.minimum(west[species], 0.0)
    e = jnp.maximum(west_own[species], 0.0) + kappa_mix
    w = weights[...]
    for s in range(species):
        rim = jnp.where(even, s_ * (south[s] - later(down_own[s])), n * (north[s] - sooner(up_own[s])))
        terms = [rim, w_ * (west[s] - east_own[s]), e * (east[s] - west_own[s])]
        mixed = jnp.dot(w, jnp.concatenate([mix_parts(h) for h in terms], axis=1), preferred_element_type=f32)
        c, c_start, c_end = [mixed[:, k * rows : (k + 1) * rows] for k in range(3)]
        lanes[s], column_start[s], column_end[s] = c, c_start, c_end
        up[s] = (
            up_in[s]
            + jnp.where(even, later(c), 0.0)
            + jnp.where(lane == 0, later(c_start), 0.0)
            + jnp.where(lane == far, pltpu.roll(c_end, far + 1, 1), 0.0)
        )
        down[s] = (
            down_in[s]
            + jnp.where(even, 0.0, sooner(c))
            + jnp.where(lane == rows - 1, sooner(c_start), 0.0)
            + jnp.where(lane == far - 1, pltpu.roll(c_end, far - 1, 1), 0.0)
        )
        west_out[s] = west_in[s] + c_end + jnp.where(ends, pltpu.roll(c, rows - far, 1), 0.0)
        east_out[s] = east_in[s] + c_start + jnp.where(ends, c, 0.0)


def left_out(lat, own, halo, weights, edges, cols, lat_size):
    shape = jax.ShapeDtypeStruct(edges[0].shape, f32)
    vmem = pl.BlockSpec(memory_space=pltpu.VMEM)
    return pl.pallas_call(
        functools.partial(left_out_kernel, cols=cols, lat_size=lat_size),
        out_shape=(shape,) * 7,
        in_specs=[pl.BlockSpec(memory_space=pltpu.SMEM)] + [vmem] * 13,
        out_specs=(vmem,) * 7,
        compiler_params=pltpu.CompilerParams(vmem_limit_bytes=SMALL_LIMIT),
        cost_estimate=pl.CostEstimate(flops=shape.size * 3000, bytes_accessed=shape.size * 100, transcendentals=0),
    )(lat, *own, *halo, weights, *edges)


def spread(total, sx, rows, akl):
    pair = total[
        pl.ds(pl.multiple_of((sx >> 1) * 2 * akl, 8), 2 * akl),
        pl.ds(pl.multiple_of((sx & 1) * rows, rows), rows),
    ]
    return jnp.concatenate(split(pair), axis=0).astype(bf16)


def step(field, clon, clat, weights, lat_size, more=None):
    species, cols, levels, rows = field.shape
    columns = pl.BlockSpec((species, BLOCK, levels, rows), lambda i: (0, i, 0, 0))
    courant = pl.BlockSpec((BLOCK, levels, rows), lambda i: (i, 0, 0))
    whole = lambda shape: pl.BlockSpec(shape, lambda i: (0,) * len(shape))
    part = lambda at: pl.BlockSpec((1, levels, rows), lambda i: (at, 0, 0))
    three = (species, levels, rows)
    given = {
        "field": (field, columns),
        "field_west": (
            field,
            pl.BlockSpec((species, 1, levels, rows), lambda i: (0, jnp.maximum(i * BLOCK - 1, 0), 0, 0)),
        ),
        "field_east": (
            field,
            pl.BlockSpec((species, 1, levels, rows), lambda i: (0, jnp.minimum(i * BLOCK + BLOCK, cols - 1), 0, 0)),
        ),
        "clon": (clon, courant),
        "clon_before": (clon, pl.BlockSpec((1, levels, rows), lambda i: (jnp.maximum(i * BLOCK - 1, 0), 0, 0))),
        "clat": (clat, courant),
        "weights": (weights, whole(weights.shape)),
    }
    if more is None:
        made = dict(up=three, down=three, west=three, east=three)
    else:
        made = dict(flux=(species, cols, rows))
        for name, value in more.items():
            spec = whole(value.shape)
            if name == "lat":
                spec = pl.BlockSpec(memory_space=pltpu.SMEM)
            elif name in ("clon_col", "clat_south"):
                spec = part(species)
            given[name] = (value, spec)
    return pl.pallas_call(
        functools.partial(step_kernel, names=(*given, "out", *made), lat_size=lat_size),
        out_shape=[pltpu.HBM(field.shape, f32)] + [jax.ShapeDtypeStruct(shape, f32) for shape in made.values()],
        grid=(cols // BLOCK,),
        in_specs=[spec for _, spec in given.values()],
        out_specs=[columns] + [whole(shape) for shape in made.values()],
        compiler_params=pltpu.CompilerParams(vmem_limit_bytes=VMEM_LIMIT),
        cost_estimate=pl.CostEstimate(
            flops=field.size * levels * 6, bytes_accessed=field.size * 12, transcendentals=0
        ),
    )(*[value for value, _ in given.values()])


def add_kernel(
    got_at,
    plain_up,
    plain_down,
    plain_west,
    plain_east,
    table,
    total,
    up,
    down,
    west,
    east,
    got,
    parts,
    group,
    spot,
    sem_got,
    *,
    cols,
):
    sources, held, slots = got_at.shape
    species, levels, rows = plain_up.shape
    akl = table.shape[1] // 4
    quarters = sem_got.shape[0]
    quarter = sources // quarters
    came = [
        pltpu.make_async_copy(got_at.at[pl.ds(q * quarter, quarter)], got.at[pl.ds(q * quarter, quarter)], sem_got.at[q])
        for q in range(quarters)
    ]
    for copy in came:
        copy.start()
    iota_w = lax.broadcasted_iota(jnp.int32, (WIDE, WIDE), 0)
    second = (lax.broadcasted_iota(jnp.int32, (4 * akl, WIDE), 0) >= 2 * akl).astype(f32)

    def prepare(g, carry):
        for i in range(2):
            b = 2 * g + i
            row = jnp.concatenate([got[2 * b], got[2 * b + 1]], axis=1)
            at = pl.ds(pl.multiple_of(b * WIDE, WIDE), WIDE)
            segment = row[akl : akl + 1].astype(jnp.int32)
            spot[:, at] = jnp.where(iota_w == (segment & (WIDE - 1)), 1.0, 0.0).astype(bf16)
            group[:, at] = ((segment >> 8).astype(f32) - second).astype(bf16)
            high, low = split(row[:akl])
            both = jnp.concatenate([high, low], axis=0)
            parts[:, at] = jnp.concatenate([both, both], axis=0).astype(bf16)
        return carry

    for q, copy in enumerate(came):
        copy.wait()
        lax.fori_loop(q * quarter // 4, (q + 1) * quarter // 4, prepare, 0)
    onehot_product(parts, group, spot, total, total.shape[0] // (4 * akl), 2, *ADD)

    t = table[...]

    def forced(parts_of, before):
        return before + jnp.dot(t, parts_of, preferred_element_type=f32)

    for s in range(species):
        east[s] = forced(spread(total, s * cols, rows, akl), plain_east[s])
        west[s] = forced(spread(total, s * cols + cols - 1, rows, akl), plain_west[s])

        def of_block(b, carry):
            columns = []
            for i in range(BLOCK):
                sx = s * cols + b * BLOCK + i
                columns.append(
                    total[
                        pl.ds(pl.multiple_of((sx >> 1) * 2 * akl, 8), 2 * akl),
                        pl.ds(pl.multiple_of((sx & 1) * rows, rows), rows),
                    ]
                )
            return tuple(edge_lanes(columns, kept, b * BLOCK, k == 0) for k, kept in enumerate(carry))

        none = jnp.zeros((2 * akl, rows), f32)
        ends = lax.fori_loop(0, cols // BLOCK, of_block, (none, none))
        for end, before, after in zip(ends, (plain_up, plain_down), (up, down)):
            after[s] = forced(jnp.concatenate(split(end), axis=0).astype(bf16), before[s])


def add_soundings(got, edges, table, cols):
    sources, held, slots = got.shape
    species, levels, rows = edges[0].shape
    akl = table.shape[1] // 4
    length = sources * slots
    pairs = -(-species * cols // 4)
    edge = jax.ShapeDtypeStruct((species, levels, rows), f32)
    vmem, hbm = pl.BlockSpec(memory_space=pltpu.VMEM), pl.BlockSpec(memory_space=pl.ANY)
    return pl.pallas_call(
        functools.partial(add_kernel, cols=cols),
        out_shape=(jax.ShapeDtypeStruct((pairs * 4 * akl, WIDE), f32), edge, edge, edge, edge),
        in_specs=[hbm] + [vmem] * 5,
        out_specs=(vmem,) * 5,
        scratch_shapes=(
            pltpu.VMEM(got.shape, f32),
            pltpu.VMEM((4 * akl, length), bf16),
            pltpu.VMEM((4 * akl, length), bf16),
            pltpu.VMEM((WIDE, length), bf16),
            pltpu.SemaphoreType.DMA((4,)),
        ),
        compiler_params=pltpu.CompilerParams(vmem_limit_bytes=ADD_LIMIT),
        cost_estimate=pl.CostEstimate(
            flops=2 * pairs * 4 * akl * WIDE * length,
            bytes_accessed=4 * got.size,
            transcendentals=0,
        ),
    )(got, *edges, table)


def on_device(
    adjoint_in,
    courant_lon,
    courant_lat,
    vertical_mix,
    sounding_values,
    sounding_dest,
    sounding_target,
    level_index,
):
    lat_size, lon_size = lax.axis_size("lat"), lax.axis_size("lon")
    n_tiles = lat_size * lon_size
    species, levels, cols, rows = adjoint_in.shape
    east_way = [(i, (i + 1) % lon_size) for i in range(lon_size)]
    west_way = [(j, i) for i, j in east_way]
    north_way = [(i, (i + 1) % lat_size) for i in range(lat_size)]
    south_way = [(j, i) for i, j in north_way]

    field = adjoint_in.transpose(0, 2, 1, 3)
    clon = courant_lon.transpose(1, 0, 2)
    clat = courant_lat.transpose(1, 0, 2)
    lat = lax.axis_index("lat").reshape(1)

    sent, *own = pack(sounding_dest, sounding_values, sounding_target, field, clon, clat, n_tiles)
    got = lax.all_to_all(sent, ("lat", "lon"), split_axis=0, concat_axis=0, tiled=True)

    def exchange(up, down, west, east):
        return (
            lax.ppermute(up, "lat", north_way),
            lax.ppermute(down, "lat", south_way),
            lax.ppermute(west, "lon", east_way),
            lax.ppermute(east, "lon", west_way),
        )

    halo = exchange(*own)
    weights = mix_weights(vertical_mix)
    table = (jnp.arange(levels, dtype=jnp.int32)[:, None] == level_index[None, :]).astype(bf16)
    table = jnp.concatenate([table] * 4, axis=1)
    plain, *edges = step(field, clon, clat, weights, lat_size)
    total, *edges = add_soundings(got, edges, table, cols)
    *edges, lanes, column_start, column_end = left_out(lat, own, halo, weights, edges, cols, lat_size)
    south, north, west, east = exchange(*edges)
    more = dict(
        lat=lat,
        south=south,
        north=north,
        west_col=west,
        east_col=east,
        clon_col=halo[2],
        clat_south=halo[0],
        total=total,
        table=table,
        lanes=lanes,
        column_start=column_start,
        column_end=column_end,
    )
    out, flux = step(plain, clon, clat, weights, lat_size, more)
    return out.transpose(0, 2, 1, 3), flux


def solution(mesh):
    return jax.shard_map(
        on_device,
        mesh=mesh,
        in_specs=(
            P(None, None, "lon", "lat"),
            P(None, "lon", "lat"),
            P(None, "lon", "lat"),
            P(),
            P(None, ("lat", "lon")),
            P(("lat", "lon"), None),
            P(("lat", "lon")),
            P(),
        ),
        out_specs=(P(None, None, "lon", "lat"), P(None, "lon", "lat")),
        check_vma=False,
    )
```

```python
import functools

import jax
import jax.numpy as jnp
from jax import lax
from jax.experimental import pallas as pl
from jax.experimental.pallas import tpu as pltpu
from jax.sharding import PartitionSpec as P

kappa_mix = 0.05
LANES = 128
WIDE = 256
TILE = 16
f32 = jnp.float32
bf16 = jnp.bfloat16
BLOCK = 15
VMEM_LIMIT = 52 * 2**20
PACK_LIMIT = 58 * 2**20
SMALL_LIMIT = 48 * 2**20
ADD_LIMIT = 49 * 2**20


def split(value):
    high = value.astype(bf16).astype(f32)
    return high, value - high


def nt_dot(a, b):
    return lax.dot_general(a, b, (((1,), (1,)), ((), ())), preferred_element_type=f32)


def onehot_product(parts, keys, tiles, spot, total, groups, step, together, depth, begin, end, onto=False, beside=None):
    rows = parts.shape[0]
    chunks = (end - begin) // depth

    def chunk(g, c):
        at = pl.ds(pl.multiple_of(begin + c * depth, LANES), depth)
        key = [k[:, at] for k in keys]
        held = [parts[TILE * q : TILE * (q + 1), at] for q in range(len(tiles))]
        none = jnp.zeros_like(held[0])
        left = []
        for i in range(together):
            hit = {}
            for kind in tiles:
                if kind not in hit:
                    which, offset = kind
                    number = jnp.asarray((g * together + i) * step + offset, jnp.int32).astype(f32).astype(bf16)
                    hit[kind] = key[which] == number
            left += [jnp.where(hit[kind], part, none) for kind, part in zip(tiles, held)]
        return nt_dot(jnp.concatenate(left, axis=0), spot[:, at])

    def of_group(g, carry):
        to = pl.ds(pl.multiple_of(g * (together * rows), together * rows), together * rows)
        if beside is not None:
            beside(g)
        if not onto:
            total[to, :] = chunk(g, 0)

        def of_chunk(c, carry):
            total[to, :] += chunk(g, c)
            return carry

        return lax.fori_loop(0 if onto else 1, chunks, of_chunk, carry)

    lax.fori_loop(groups[0] // together, groups[1] // together, of_group, 0)


def mark(spot, at, row):
    row = jnp.broadcast_to(row.astype(f32), (TILE, row.shape[1])).astype(bf16)
    base = lax.broadcasted_iota(jnp.int32, row.shape, 0).astype(f32).astype(bf16)
    one, none = jnp.ones_like(row), jnp.zeros_like(row)
    for q in range(WIDE // TILE):
        spot[TILE * q : TILE * (q + 1), at] = jnp.where(row - jnp.asarray(TILE * q, bf16) == base, one, none)


def edge_lanes(columns, kept, first, up, share=None):
    rows = kept.shape[1]
    lane = lax.broadcasted_iota(jnp.int32, kept.shape, 1)
    own = jnp.zeros_like(kept)
    for i, v in enumerate(columns):
        if up:
            own = jnp.where(lane == 2 * i, pltpu.roll(v, 2 * i + 1, 1), own)
        else:
            own = jnp.where(lane == 2 * i + 1, pltpu.roll(v, 2 * i + 1, 1), own)
    if share is not None:
        own = own * share
    turn = 2 * first if up else lax.rem(2 * first + rows - 2, rows)
    return kept + pltpu.roll(own, turn, 1)


PACK = (16, 8192)
ADD = (17, 6144)


def whole_part(value, divisor):
    return ((value.astype(f32) + 0.5) * (1.0 / divisor)).astype(jnp.int32)


def half_segment(columns):
    return -(-columns // 4) // 2 * 2 * WIDE


def pack_kernel(
    dest,
    values,
    target,
    field_at,
    clon_at,
    clat_at,
    out,
    up,
    down,
    west,
    east,
    parts,
    group,
    spot,
    total,
    field,
    clat,
    sems,
):
    n_tiles, held, _ = out.shape
    species, cols, _, rows = field.shape
    copies = [(field_at, field), (clat_at, clat), (clon_at.at[cols - 1], west.at[species])]
    for s in range(species):
        copies += [(field_at.at[s, cols - 1], west.at[s]), (field_at.at[s, 0], east.at[s])]
    copies = [pltpu.make_async_copy(*pair, sems.at[i]) for i, pair in enumerate(copies)]
    for copy in copies:
        copy.start()
    up[...] = jnp.zeros_like(up)
    down[...] = jnp.zeros_like(down)
    levels, length = values.shape
    iota_t = lax.broadcasted_iota(jnp.int32, (n_tiles, WIDE), 0)
    square = (WIDE, WIDE)
    upper = (
        lax.broadcasted_iota(jnp.int32, square, 0) < lax.broadcasted_iota(jnp.int32, square, 1)
    ).astype(f32).astype(bf16)

    halfway = half_segment(species * cols)

    def rank(at, base):
        d = dest[:, at]
        t = target[:, at]
        cell = whole_part(t, species)
        row_of = whole_part(cell, cols)
        segment = ((t - cell * species) * cols + cell - row_of * cols) * rows + row_of
        upper_half = segment >= halfway
        hot = iota_t == d
        hot_f = jnp.where(hot, jnp.where(upper_half, 256.0, 1.0), 0.0)
        earlier = jnp.dot(hot_f.astype(bf16), upper, preferred_element_type=f32) + base
        own = jnp.sum(jnp.where(hot, earlier, 0.0), axis=0, keepdims=True).astype(jnp.int32)
        slot = jnp.where(upper_half, LANES - 1 - (own >> 8), own & 255)
        low = slot + (d & 1) * LANES
        mark(spot, at, low)
        group[:, at] = jnp.broadcast_to((d >> 1).astype(f32), (TILE, WIDE)).astype(bf16)
        row = jnp.concatenate(
            [values[:, at], (segment + 1).astype(f32), jnp.zeros((held - levels - 1, WIDE), f32)], axis=0
        )
        parts[:, at] = jnp.concatenate(split(row), axis=0).astype(bf16)
        return base + jnp.sum(hot_f, axis=1, keepdims=True)

    def ranks(b, base):
        for i in range(4):
            base = rank(pl.ds(pl.multiple_of((4 * b + i) * WIDE, WIDE), WIDE), base)
        return base

    lax.fori_loop(0, length // (4 * WIDE), ranks, jnp.zeros((n_tiles, 1), f32))
    for copy in copies:
        copy.wait()
    blocks = cols // BLOCK

    def take_edges(g):
        first = jnp.minimum(g, blocks - 1) * BLOCK
        new = (g < blocks).astype(f32)
        for s in range(species + 1):
            columns = [field[s, first + i] if s < species else clat[first + i] for i in range(BLOCK)]
            up[s] = edge_lanes(columns, up[s], first, True, new)
            if s < species:
                down[s] = edge_lanes(columns, down[s], first, False, new)

    tiles = ((0, 0),) * (2 * held // TILE)
    onehot_product(
        parts, [group], tiles, spot, total, (0, n_tiles // 2), 1, *PACK, 0, length, beside=take_edges
    )

    def put(g, carry):
        for i in range(4):
            j = 4 * g + i
            at = pl.multiple_of(j * 2 * held, 2 * held)
            both = total[pl.ds(at, held), :] + total[pl.ds(at + held, held), :]
            out[2 * j] = both[:, :LANES]
            out[2 * j + 1] = both[:, LANES:]
        return carry

    lax.fori_loop(0, n_tiles // 8, put, 0)


def pack(dest, values, target, field, clon, clat, n_tiles):
    levels, length = values.shape
    species, cols, depth, rows = field.shape
    held = -(-(levels + 1) // 8) * 8
    four, three = (species + 1, depth, rows), (species, depth, rows)
    vmem, hbm = pl.BlockSpec(memory_space=pltpu.VMEM), pl.BlockSpec(memory_space=pl.ANY)
    return pl.pallas_call(
        pack_kernel,
        out_shape=tuple(
            jax.ShapeDtypeStruct(shape, f32) for shape in ((n_tiles, held, LANES), four, three, four, three)
        ),
        in_specs=[vmem, vmem, vmem, hbm, hbm, hbm],
        out_specs=(vmem,) * 5,
        scratch_shapes=(
            pltpu.VMEM((2 * held, length), bf16),
            pltpu.VMEM((TILE, length), bf16),
            pltpu.VMEM((WIDE, length), bf16),
            pltpu.VMEM((n_tiles // 2 * 2 * held, WIDE), f32),
            pltpu.VMEM(field.shape, f32),
            pltpu.VMEM(clat.shape, f32),
            pltpu.SemaphoreType.DMA((3 + 2 * species,)),
        ),
        compiler_params=pltpu.CompilerParams(vmem_limit_bytes=PACK_LIMIT),
        cost_estimate=pl.CostEstimate(
            flops=2 * length * n_tiles * LANES * 2 * held,
            bytes_accessed=4 * (length * 22 + n_tiles * held * LANES + field.size),
            transcendentals=0,
        ),
    )(dest.reshape(1, length), values, target.reshape(1, length), field, clon, clat)


def mix_weights(vertical_mix):
    levels = vertical_mix.shape[0]
    matrix = (jnp.eye(levels, dtype=f32) + vertical_mix).T
    high = lax.reduce_precision(matrix, 8, 7)
    return jnp.concatenate([high, high, matrix - high], axis=1).astype(bf16)


def step_kernel(*refs, names, lat_size):
    ref = dict(zip(names, refs))
    second = "total" in ref
    field, clon, clat, out = ref["field"], ref["clon"], ref["clat"], ref["out"]
    species, block, levels, rows = field.shape
    lane = lax.broadcasted_iota(jnp.int32, (levels, rows), 1)
    first, last = lane == 0, lane == rows - 1
    here = pl.program_id(0)
    at_start, at_end = here == 0, here == pl.num_programs(0) - 1
    start = here * block
    w = ref["weights"][...]
    waiting = []

    def back(v, i):
        return pltpu.roll(v, (rows - 2 * i) % rows, 1) if i else v

    if second:
        lat = ref["lat"][0]
        below = jnp.where(jnp.logical_and(first, lat == 0), 0.0, 1.0)
        inside = jnp.where(jnp.logical_and(last, lat == lat_size - 1), 0.0, 1.0)
        turn = lax.rem(rows - 2 * start, rows)
        even = lane % 2 == 0
        ends = jnp.logical_or(first, last)
        halos = [
            pltpu.roll(jnp.where(even, ref["south"][s], ref["north"][s]), turn, 1) for s in range(species)
        ]
        left_out = [pltpu.roll(ref["lanes"][s], turn, 1) for s in range(species)]
        courant_south = pltpu.roll(ref["clat_south"][0], turn, 1)
        t = ref["table"][...]
        cols = pl.num_programs(0) * block
        wanted = []
        made = {}

        def make(ready):
            forcing = jnp.dot(t, jnp.concatenate([p for _, _, p in ready], axis=1), preferred_element_type=f32)
            for k, ((s, i), v, _) in enumerate(ready):
                v = v + forcing[:, k * rows : (k + 1) * rows] + jnp.where(ends, back(left_out[s], i), 0.0)
                if i == 0:
                    v = v + jnp.where(at_start, ref["column_start"][s], 0.0)
                if i == block - 1:
                    v = v + jnp.where(at_end, ref["column_end"][s], 0.0)
                made[s, i] = v

        for i in range(-1, block + 1):
            x = jnp.clip(start + i, 0, cols - 1)
            for s in range(species):
                v = ref["field_west"][s, 0] if i < 0 else ref["field_east"][s, 0] if i == block else field[s, i]
                wanted.append(((s, i), v, spread(ref["total"], s * cols + x, rows, t.shape[1] // 4)))
                if len(wanted) == 2:
                    make(wanted)
                    wanted.clear()
        if wanted:
            make(wanted)

        def at_column(s, i):
            return made[s, i]
    else:
        below, inside = jnp.where(first, 0.0, 1.0), jnp.where(last, 0.0, 1.0)
        finished = [[None] * block for _ in range(species)]

        def at_column(s, i):
            return ref["field_west"][s, 0] if i < 0 else ref["field_east"][s, 0] if i == block else field[s, i]

    def mix(ready):
        mixed = jnp.dot(
            w, jnp.concatenate([r for _, _, r in ready], axis=1), preferred_element_type=f32
        )
        for k, (s, i, _) in enumerate(ready):
            m = mixed[:, k * rows : (k + 1) * rows]
            out[s, i] = m
            if second:
                ref["flux"][s, pl.ds(start + i, 1), :] = at_column(s, i)[0:1] + m[0:1]
            else:
                finished[s][i] = m

    for i in range(block):
        cl, cw = clon[i], clat[i]
        cl_west = clon[i - 1] if i else ref["clon_before"][0]
        if i == 0 and second:
            cl_west = jnp.where(at_start, ref["clon_col"][0], cl_west)
        e = jnp.maximum(cl, 0.0) + kappa_mix
        w_ = kappa_mix - jnp.minimum(cl_west, 0.0)
        if not second and i == 0:
            w_ = jnp.where(at_start, 0.0, w_)
        if not second and i == block - 1:
            e = jnp.where(at_end, 0.0, e)
        n = (jnp.maximum(cw, 0.0) + kappa_mix) * inside
        cs = pltpu.roll(cw, 1, 1)
        if second:
            cs = jnp.where(first, back(courant_south, i), cs)
        s_ = (kappa_mix - jnp.minimum(cs, 0.0)) * below
        centre = 1.0 - (e + w_ + n + s_)
        for s in range(species):
            v, v_w, v_e = at_column(s, i), at_column(s, i - 1), at_column(s, i + 1)
            v_n, v_s = pltpu.roll(v, rows - 1, 1), pltpu.roll(v, 1, 1)
            if second:
                if i == 0:
                    v_w = jnp.where(at_start, ref["west_col"][s], v_w)
                if i == block - 1:
                    v_e = jnp.where(at_end, ref["east_col"][s], v_e)
                halo = back(halos[s], i)
                v_n, v_s = jnp.where(last, halo, v_n), jnp.where(first, halo, v_s)
            h = centre * v + e * v_e + w_ * v_w + n * v_n + s_ * v_s
            waiting.append((s, i, mix_parts(h)))
            if len(waiting) == 2:
                mix(waiting)
                waiting.clear()
    if waiting:
        mix(waiting)
    if not second:
        up, down, west, east = ref["up"], ref["down"], ref["west"], ref["east"]

        @pl.when(at_start)
        def _():
            up[...] = jnp.zeros_like(up)
            down[...] = jnp.zeros_like(down)
            for s in range(species):
                east[s] = out[s, 0]

        @pl.when(at_end)
        def _():
            for s in range(species):
                west[s] = out[s, block - 1]

        for s in range(species):
            up[s] = edge_lanes(finished[s], up[s], start, True)
            down[s] = edge_lanes(finished[s], down[s], start, False)


def mix_parts(h):
    high, low = split(h)
    return jnp.concatenate([high, low, high], axis=0).astype(bf16)


def left_out_kernel(
    lat_ref,
    up_own,
    down_own,
    west_own,
    east_own,
    south,
    north,
    west,
    east,
    weights,
    up_in,
    down_in,
    west_in,
    east_in,
    up,
    down,
    west_out,
    east_out,
    lanes,
    column_start,
    column_end,
    *,
    cols,
    lat_size,
):
    species, levels, rows = up_in.shape
    lane = lax.broadcasted_iota(jnp.int32, (levels, rows), 1)
    even = lane % 2 == 0
    ends = jnp.logical_or(lane == 0, lane == rows - 1)
    lat = lat_ref[0]
    below = jnp.where(lat == 0, 0.0, 1.0)
    inside = jnp.where(lat == lat_size - 1, 0.0, 1.0)
    far = 2 * (cols - 1)

    def later(v):
        return pltpu.roll(v, 1, 1)

    def sooner(v):
        return pltpu.roll(v, rows - 1, 1)

    n = (jnp.maximum(sooner(up_own[species]), 0.0) + kappa_mix) * inside
    s_ = (kappa_mix - jnp.minimum(south[species], 0.0)) * below
    w_ = kappa_mix - jnp.minimum(west[species], 0.0)
    e = jnp.maximum(west_own[species], 0.0) + kappa_mix
    w = weights[...]
    for s in range(species):
        rim = jnp.where(even, s_ * (south[s] - later(down_own[s])), n * (north[s] - sooner(up_own[s])))
        terms = [rim, w_ * (west[s] - east_own[s]), e * (east[s] - west_own[s])]
        mixed = jnp.dot(w, jnp.concatenate([mix_parts(h) for h in terms], axis=1), preferred_element_type=f32)
        c, c_start, c_end = [mixed[:, k * rows : (k + 1) * rows] for k in range(3)]
        lanes[s], column_start[s], column_end[s] = c, c_start, c_end
        up[s] = (
            up_in[s]
            + jnp.where(even, later(c), 0.0)
            + jnp.where(lane == 0, later(c_start), 0.0)
            + jnp.where(lane == far, pltpu.roll(c_end, far + 1, 1), 0.0)
        )
        down[s] = (
            down_in[s]
            + jnp.where(even, 0.0, sooner(c))
            + jnp.where(lane == rows - 1, sooner(c_start), 0.0)
            + jnp.where(lane == far - 1, pltpu.roll(c_end, far - 1, 1), 0.0)
        )
        west_out[s] = west_in[s] + c_end + jnp.where(ends, pltpu.roll(c, rows - far, 1), 0.0)
        east_out[s] = east_in[s] + c_start + jnp.where(ends, c, 0.0)


def left_out(lat, own, halo, weights, edges, cols, lat_size):
    shape = jax.ShapeDtypeStruct(edges[0].shape, f32)
    vmem = pl.BlockSpec(memory_space=pltpu.VMEM)
    return pl.pallas_call(
        functools.partial(left_out_kernel, cols=cols, lat_size=lat_size),
        out_shape=(shape,) * 7,
        in_specs=[pl.BlockSpec(memory_space=pltpu.SMEM)] + [vmem] * 13,
        out_specs=(vmem,) * 7,
        compiler_params=pltpu.CompilerParams(vmem_limit_bytes=SMALL_LIMIT),
        cost_estimate=pl.CostEstimate(flops=shape.size * 3000, bytes_accessed=shape.size * 100, transcendentals=0),
    )(lat, *own, *halo, weights, *edges)


def spread(total, sx, rows, akl):
    pair = total[
        pl.ds(pl.multiple_of((sx >> 1) * 2 * akl, 8), 2 * akl),
        pl.ds(pl.multiple_of((sx & 1) * rows, rows), rows),
    ]
    return jnp.concatenate(split(pair), axis=0).astype(bf16)


def step(field, clon, clat, weights, lat_size, more=None):
    species, cols, levels, rows = field.shape
    columns = pl.BlockSpec((species, BLOCK, levels, rows), lambda i: (0, i, 0, 0))
    courant = pl.BlockSpec((BLOCK, levels, rows), lambda i: (i, 0, 0))
    whole = lambda shape: pl.BlockSpec(shape, lambda i: (0,) * len(shape))
    part = lambda at: pl.BlockSpec((1, levels, rows), lambda i: (at, 0, 0))
    three = (species, levels, rows)
    given = {
        "field": (field, columns),
        "field_west": (
            field,
            pl.BlockSpec((species, 1, levels, rows), lambda i: (0, jnp.maximum(i * BLOCK - 1, 0), 0, 0)),
        ),
        "field_east": (
            field,
            pl.BlockSpec((species, 1, levels, rows), lambda i: (0, jnp.minimum(i * BLOCK + BLOCK, cols - 1), 0, 0)),
        ),
        "clon": (clon, courant),
        "clon_before": (clon, pl.BlockSpec((1, levels, rows), lambda i: (jnp.maximum(i * BLOCK - 1, 0), 0, 0))),
        "clat": (clat, courant),
        "weights": (weights, whole(weights.shape)),
    }
    if more is None:
        made = dict(up=three, down=three, west=three, east=three)
    else:
        made = dict(flux=(species, cols, rows))
        for name, value in more.items():
            spec = whole(value.shape)
            if name == "lat":
                spec = pl.BlockSpec(memory_space=pltpu.SMEM)
            elif name in ("clon_col", "clat_south"):
                spec = part(species)
            given[name] = (value, spec)
    return pl.pallas_call(
        functools.partial(step_kernel, names=(*given, "out", *made), lat_size=lat_size),
        out_shape=[pltpu.HBM(field.shape, f32)] + [jax.ShapeDtypeStruct(shape, f32) for shape in made.values()],
        grid=(cols // BLOCK,),
        in_specs=[spec for _, spec in given.values()],
        out_specs=[columns] + [whole(shape) for shape in made.values()],
        compiler_params=pltpu.CompilerParams(vmem_limit_bytes=VMEM_LIMIT),
        cost_estimate=pl.CostEstimate(
            flops=field.size * levels * 6, bytes_accessed=field.size * 12, transcendentals=0
        ),
    )(*[value for value, _ in given.values()])


def add_kernel(
    got_at,
    plain_up,
    plain_down,
    plain_west,
    plain_east,
    table,
    total,
    up,
    down,
    west,
    east,
    got,
    parts,
    group,
    middle,
    spot,
    sem_got,
    *,
    cols,
):
    sources, held, slots = got_at.shape
    species, levels, rows = plain_up.shape
    akl = table.shape[1] // 4
    quarters = sem_got.shape[0]
    quarter = sources // quarters
    came = [
        pltpu.make_async_copy(got_at.at[pl.ds(q * quarter, quarter)], got.at[pl.ds(q * quarter, quarter)], sem_got.at[q])
        for q in range(quarters)
    ]
    for copy in came:
        copy.start()
    second = (lax.broadcasted_iota(jnp.int32, (TILE, WIDE), 0) >= TILE // 2).astype(f32)
    quarter_of = lax.broadcasted_iota(jnp.int32, (held, slots), 1) // (slots // 4)
    length = sources * slots
    halfway = half_segment(species * cols)

    def put(row, at):
        wide = row.shape[1]
        at = pl.ds(pl.multiple_of(at, LANES), wide)
        segment = row[akl : akl + 1].astype(jnp.int32) - 1
        mark(spot, at, segment & (WIDE - 1))
        pair = jnp.broadcast_to((segment >> 8).astype(f32), (TILE, wide))
        group[:, at] = pair.astype(bf16)
        middle[:, at] = (pair - second[:, :wide]).astype(bf16)
        high, low = split(row[:akl])
        both = jnp.concatenate([high, low], axis=0)
        parts[:, at] = jnp.concatenate([both, both], axis=0).astype(bf16)
        return segment

    def prepare(g, carry):
        highest, lowest = carry
        fours = []
        for b in range(2):
            turned = [got[8 * g + 4 * b + k] for k in range(4)]
            turned = [pltpu.roll(v, k * (slots // 4), 1) if k else v for k, v in enumerate(turned)]
            rows_of = []
            for q in range(4):
                row = turned[0]
                for k in range(1, 4):
                    row = jnp.where(quarter_of == (q + k) % 4, turned[k], row)
                rows_of.append(row)
            fours.append(rows_of)
        row = [jnp.concatenate([fours[0][q], fours[1][q]], axis=1) for q in range(4)]
        segment = put(row[0], g * WIDE)
        highest = jnp.maximum(highest, segment)
        put(row[1], length // 4 + 2 * g * WIDE)
        put(row[2], length // 4 + (2 * g + 1) * WIDE)
        segment = put(row[3], 3 * (length // 4) + g * WIDE)
        lowest = jnp.minimum(lowest, jnp.where(segment < 0, 2 * halfway, segment))
        return highest, lowest

    carry = (jnp.full((1, WIDE), -1, jnp.int32), jnp.full((1, WIDE), 2 * halfway, jnp.int32))
    for q, copy in enumerate(came):
        copy.wait()
        carry = lax.fori_loop(q * quarter // 8, (q + 1) * quarter // 8, prepare, carry)
    highest, lowest = jnp.max(carry[0]), jnp.min(carry[1])

    tiles = ((0, 0), (0, 0), (1, 0), (0, 1), (0, 1))
    groups = total.shape[0] // (4 * akl)
    lower, higher = (0, groups // 2), (groups // 2, groups)
    add = functools.partial(onehot_product, parts, [group, middle], tiles, spot, total)
    add(lower, 2, *ADD, 0, 3 * (length // 4))
    add(higher, 2, *ADD, length // 4, length)

    @pl.when(highest >= halfway)
    def _():
        add(higher, 2, ADD[0], length // 8, 0, length // 4, onto=True)

    @pl.when(lowest < halfway)
    def _():
        add(lower, 2, ADD[0], length // 8, 3 * (length // 4), length, onto=True)

    t = table[...]

    def forced(parts_of, before):
        return before + jnp.dot(t, parts_of, preferred_element_type=f32)

    for s in range(species):
        east[s] = forced(spread(total, s * cols, rows, akl), plain_east[s])
        west[s] = forced(spread(total, s * cols + cols - 1, rows, akl), plain_west[s])

        def of_block(b, carry):
            columns = []
            for i in range(BLOCK):
                sx = s * cols + b * BLOCK + i
                columns.append(
                    total[
                        pl.ds(pl.multiple_of((sx >> 1) * 2 * akl, 8), 2 * akl),
                        pl.ds(pl.multiple_of((sx & 1) * rows, rows), rows),
                    ]
                )
            return tuple(edge_lanes(columns, kept, b * BLOCK, k == 0) for k, kept in enumerate(carry))

        none = jnp.zeros((2 * akl, rows), f32)
        ends = lax.fori_loop(0, cols // BLOCK, of_block, (none, none))
        for end, before, after in zip(ends, (plain_up, plain_down), (up, down)):
            after[s] = forced(jnp.concatenate(split(end), axis=0).astype(bf16), before[s])


def add_soundings(got, edges, table, cols):
    sources, held, slots = got.shape
    species, levels, rows = edges[0].shape
    akl = table.shape[1] // 4
    length = sources * slots
    pairs = -(-species * cols // 4)
    edge = jax.ShapeDtypeStruct((species, levels, rows), f32)
    vmem, hbm = pl.BlockSpec(memory_space=pltpu.VMEM), pl.BlockSpec(memory_space=pl.ANY)
    return pl.pallas_call(
        functools.partial(add_kernel, cols=cols),
        out_shape=(jax.ShapeDtypeStruct((pairs * 4 * akl, WIDE), f32), edge, edge, edge, edge),
        in_specs=[hbm] + [vmem] * 5,
        out_specs=(vmem,) * 5,
        scratch_shapes=(
            pltpu.VMEM(got.shape, f32),
            pltpu.VMEM((4 * akl, length), bf16),
            pltpu.VMEM((TILE, length), bf16),
            pltpu.VMEM((TILE, length), bf16),
            pltpu.VMEM((WIDE, length), bf16),
            pltpu.SemaphoreType.DMA((4,)),
        ),
        compiler_params=pltpu.CompilerParams(vmem_limit_bytes=ADD_LIMIT),
        cost_estimate=pl.CostEstimate(
            flops=2 * pairs * 4 * akl * WIDE * length,
            bytes_accessed=4 * got.size,
            transcendentals=0,
        ),
    )(got, *edges, table)


def on_device(
    adjoint_in,
    courant_lon,
    courant_lat,
    vertical_mix,
    sounding_values,
    sounding_dest,
    sounding_target,
    level_index,
):
    lat_size, lon_size = lax.axis_size("lat"), lax.axis_size("lon")
    n_tiles = lat_size * lon_size
    species, levels, cols, rows = adjoint_in.shape
    east_way = [(i, (i + 1) % lon_size) for i in range(lon_size)]
    west_way = [(j, i) for i, j in east_way]
    north_way = [(i, (i + 1) % lat_size) for i in range(lat_size)]
    south_way = [(j, i) for i, j in north_way]

    field = adjoint_in.transpose(0, 2, 1, 3)
    clon = courant_lon.transpose(1, 0, 2)
    clat = courant_lat.transpose(1, 0, 2)
    lat = lax.axis_index("lat").reshape(1)

    sent, *own = pack(sounding_dest, sounding_values, sounding_target, field, clon, clat, n_tiles)
    got = lax.all_to_all(sent, ("lat", "lon"), split_axis=0, concat_axis=0, tiled=True)

    def exchange(up, down, west, east):
        return (
            lax.ppermute(up, "lat", north_way),
            lax.ppermute(down, "lat", south_way),
            lax.ppermute(west, "lon", east_way),
            lax.ppermute(east, "lon", west_way),
        )

    halo = exchange(*own)
    weights = mix_weights(vertical_mix)
    table = (jnp.arange(levels, dtype=jnp.int32)[:, None] == level_index[None, :]).astype(bf16)
    table = jnp.concatenate([table] * 4, axis=1)
    plain, *edges = step(field, clon, clat, weights, lat_size)
    total, *edges = add_soundings(got, edges, table, cols)
    *edges, lanes, column_start, column_end = left_out(lat, own, halo, weights, edges, cols, lat_size)
    south, north, west, east = exchange(*edges)
    more = dict(
        lat=lat,
        south=south,
        north=north,
        west_col=west,
        east_col=east,
        clon_col=halo[2],
        clat_south=halo[0],
        total=total,
        table=table,
        lanes=lanes,
        column_start=column_start,
        column_end=column_end,
    )
    out, flux = step(plain, clon, clat, weights, lat_size, more)
    return out.transpose(0, 2, 1, 3), flux


def solution(mesh):
    return jax.shard_map(
        on_device,
        mesh=mesh,
        in_specs=(
            P(None, None, "lon", "lat"),
            P(None, "lon", "lat"),
            P(None, "lon", "lat"),
            P(),
            P(None, ("lat", "lon")),
            P(("lat", "lon"), None),
            P(("lat", "lon")),
            P(),
        ),
        out_specs=(P(None, None, "lon", "lat"), P(None, "lon", "lat")),
        check_vma=False,
    )
```

```python
import functools

import jax
import jax.numpy as jnp
from jax import lax
from jax.experimental import pallas as pl
from jax.experimental.pallas import tpu as pltpu
from jax.sharding import PartitionSpec as P

kappa_mix = 0.05
LANES = 128
WIDE = 256
TILE = 16
f32 = jnp.float32
bf16 = jnp.bfloat16
BLOCK = 15
VMEM_LIMIT = 52 * 2**20
PACK_LIMIT = 58 * 2**20
SMALL_LIMIT = 48 * 2**20
ADD_LIMIT = 49 * 2**20


def split(value):
    high = value.astype(bf16).astype(f32)
    return high, value - high


def nt_dot(a, b):
    return lax.dot_general(a, b, (((1,), (1,)), ((), ())), preferred_element_type=f32)


def onehot_product(parts, keys, tiles, spot, total, groups, step, together, depth, begin, end, onto=False, beside=None):
    rows = parts.shape[0]
    chunks = (end - begin) // depth

    def chunk(g, c):
        at = pl.ds(pl.multiple_of(begin + c * depth, LANES), depth)
        key = [k[:, at] for k in keys]
        held = [parts[TILE * q : TILE * (q + 1), at] for q in range(len(tiles))]
        none = jnp.zeros_like(held[0])
        left = []
        for i in range(together):
            hit = {}
            for kind in tiles:
                if kind not in hit:
                    which, offset = kind
                    number = jnp.asarray((g * together + i) * step + offset, jnp.int32).astype(f32).astype(bf16)
                    hit[kind] = key[which] == number
            left += [jnp.where(hit[kind], part, none) for kind, part in zip(tiles, held)]
        return nt_dot(jnp.concatenate(left, axis=0), spot[:, at])

    def of_group(g, carry):
        to = pl.ds(pl.multiple_of(g * (together * rows), together * rows), together * rows)
        if beside is not None:
            beside(g)
        if not onto:
            total[to, :] = chunk(g, 0)

        def of_chunk(c, carry):
            total[to, :] += chunk(g, c)
            return carry

        return lax.fori_loop(0 if onto else 1, chunks, of_chunk, carry)

    lax.fori_loop(groups[0] // together, groups[1] // together, of_group, 0)


def mark(spot, at, row):
    row = jnp.broadcast_to(row.astype(f32), (TILE, row.shape[1])).astype(bf16)
    base = lax.broadcasted_iota(jnp.int32, row.shape, 0).astype(f32).astype(bf16)
    one, none = jnp.ones_like(row), jnp.zeros_like(row)
    for q in range(WIDE // TILE):
        spot[TILE * q : TILE * (q + 1), at] = jnp.where(row - jnp.asarray(TILE * q, bf16) == base, one, none)


def edge_lanes(columns, kept, first, up, share=None):
    rows = kept.shape[1]
    lane = lax.broadcasted_iota(jnp.int32, kept.shape, 1)
    own = jnp.zeros_like(kept)
    for i, v in enumerate(columns):
        if up:
            own = jnp.where(lane == 2 * i, pltpu.roll(v, 2 * i + 1, 1), own)
        else:
            own = jnp.where(lane == 2 * i + 1, pltpu.roll(v, 2 * i + 1, 1), own)
    if share is not None:
        own = own * share
    turn = 2 * first if up else lax.rem(2 * first + rows - 2, rows)
    return kept + pltpu.roll(own, turn, 1)


PACK = (16, 8192)


def whole_part(value, divisor):
    return ((value.astype(f32) + 0.5) * (1.0 / divisor)).astype(jnp.int32)


def half_segment(columns):
    return -(-columns // 4) // 2 * 2 * WIDE


def pack_kernel(
    dest,
    values,
    target,
    field_at,
    clon_at,
    clat_at,
    out,
    up,
    down,
    west,
    east,
    parts,
    group,
    spot,
    total,
    field,
    clat,
    sems,
):
    n_tiles, held, _ = out.shape
    species, cols, _, rows = field.shape
    copies = [(field_at, field), (clat_at, clat), (clon_at.at[cols - 1], west.at[species])]
    for s in range(species):
        copies += [(field_at.at[s, cols - 1], west.at[s]), (field_at.at[s, 0], east.at[s])]
    copies = [pltpu.make_async_copy(*pair, sems.at[i]) for i, pair in enumerate(copies)]
    for copy in copies:
        copy.start()
    up[...] = jnp.zeros_like(up)
    down[...] = jnp.zeros_like(down)
    levels, length = values.shape
    iota_t = lax.broadcasted_iota(jnp.int32, (n_tiles, WIDE), 0)
    square = (WIDE, WIDE)
    upper = (
        lax.broadcasted_iota(jnp.int32, square, 0) < lax.broadcasted_iota(jnp.int32, square, 1)
    ).astype(f32).astype(bf16)

    halfway = half_segment(species * cols)

    def rank(at, base):
        d = dest[:, at]
        t = target[:, at]
        cell = whole_part(t, species)
        row_of = whole_part(cell, cols)
        segment = ((t - cell * species) * cols + cell - row_of * cols) * rows + row_of
        upper_half = segment >= halfway
        hot = iota_t == d
        hot_f = jnp.where(hot, jnp.where(upper_half, 256.0, 1.0), 0.0)
        earlier = jnp.dot(hot_f.astype(bf16), upper, preferred_element_type=f32) + base
        own = jnp.sum(jnp.where(hot, earlier, 0.0), axis=0, keepdims=True).astype(jnp.int32)
        slot = jnp.where(upper_half, LANES - 1 - (own >> 8), own & 255)
        low = slot + (d & 1) * LANES
        mark(spot, at, low)
        group[:, at] = jnp.broadcast_to((d >> 1).astype(f32), (TILE, WIDE)).astype(bf16)
        row = jnp.concatenate(
            [values[:, at], (segment + 1).astype(f32), jnp.zeros((held - levels - 1, WIDE), f32)], axis=0
        )
        parts[:, at] = jnp.concatenate(split(row), axis=0).astype(bf16)
        return base + jnp.sum(hot_f, axis=1, keepdims=True)

    def ranks(b, base):
        for i in range(4):
            base = rank(pl.ds(pl.multiple_of((4 * b + i) * WIDE, WIDE), WIDE), base)
        return base

    lax.fori_loop(0, length // (4 * WIDE), ranks, jnp.zeros((n_tiles, 1), f32))
    for copy in copies:
        copy.wait()
    blocks = cols // BLOCK

    def take_edges(g):
        first = jnp.minimum(g, blocks - 1) * BLOCK
        new = (g < blocks).astype(f32)
        for s in range(species + 1):
            columns = [field[s, first + i] if s < species else clat[first + i] for i in range(BLOCK)]
            up[s] = edge_lanes(columns, up[s], first, True, new)
            if s < species:
                down[s] = edge_lanes(columns, down[s], first, False, new)

    tiles = ((0, 0),) * (2 * held // TILE)
    onehot_product(
        parts, [group], tiles, spot, total, (0, n_tiles // 2), 1, *PACK, 0, length, beside=take_edges
    )

    def put(g, carry):
        for i in range(4):
            j = 4 * g + i
            at = pl.multiple_of(j * 2 * held, 2 * held)
            both = total[pl.ds(at, held), :] + total[pl.ds(at + held, held), :]
            out[2 * j] = both[:, :LANES]
            out[2 * j + 1] = both[:, LANES:]
        return carry

    lax.fori_loop(0, n_tiles // 8, put, 0)


def pack(dest, values, target, field, clon, clat, n_tiles):
    levels, length = values.shape
    species, cols, depth, rows = field.shape
    held = -(-(levels + 1) // 8) * 8
    four, three = (species + 1, depth, rows), (species, depth, rows)
    vmem, hbm = pl.BlockSpec(memory_space=pltpu.VMEM), pl.BlockSpec(memory_space=pl.ANY)
    return pl.pallas_call(
        pack_kernel,
        out_shape=tuple(
            jax.ShapeDtypeStruct(shape, f32) for shape in ((n_tiles, held, LANES), four, three, four, three)
        ),
        in_specs=[vmem, vmem, vmem, hbm, hbm, hbm],
        out_specs=(vmem,) * 5,
        scratch_shapes=(
            pltpu.VMEM((2 * held, length), bf16),
            pltpu.VMEM((TILE, length), bf16),
            pltpu.VMEM((WIDE, length), bf16),
            pltpu.VMEM((n_tiles // 2 * 2 * held, WIDE), f32),
            pltpu.VMEM(field.shape, f32),
            pltpu.VMEM(clat.shape, f32),
            pltpu.SemaphoreType.DMA((3 + 2 * species,)),
        ),
        compiler_params=pltpu.CompilerParams(vmem_limit_bytes=PACK_LIMIT),
        cost_estimate=pl.CostEstimate(
            flops=2 * length * n_tiles * LANES * 2 * held,
            bytes_accessed=4 * (length * 22 + n_tiles * held * LANES + field.size),
            transcendentals=0,
        ),
    )(dest.reshape(1, length), values, target.reshape(1, length), field, clon, clat)


def mix_weights(vertical_mix):
    levels = vertical_mix.shape[0]
    matrix = (jnp.eye(levels, dtype=f32) + vertical_mix).T
    high = lax.reduce_precision(matrix, 8, 7)
    return jnp.concatenate([high, high, matrix - high], axis=1).astype(bf16)


def step_kernel(*refs, names, lat_size):
    ref = dict(zip(names, refs))
    second = "total" in ref
    field, clon, clat, out = ref["field"], ref["clon"], ref["clat"], ref["out"]
    species, block, levels, rows = field.shape
    lane = lax.broadcasted_iota(jnp.int32, (levels, rows), 1)
    first, last = lane == 0, lane == rows - 1
    here = pl.program_id(0)
    at_start, at_end = here == 0, here == pl.num_programs(0) - 1
    start = here * block
    w = ref["weights"][...]
    waiting = []

    def back(v, i):
        return pltpu.roll(v, (rows - 2 * i) % rows, 1) if i else v

    if second:
        lat = ref["lat"][0]
        below = jnp.where(jnp.logical_and(first, lat == 0), 0.0, 1.0)
        inside = jnp.where(jnp.logical_and(last, lat == lat_size - 1), 0.0, 1.0)
        turn = lax.rem(rows - 2 * start, rows)
        even = lane % 2 == 0
        ends = jnp.logical_or(first, last)
        halos = [
            pltpu.roll(jnp.where(even, ref["south"][s], ref["north"][s]), turn, 1) for s in range(species)
        ]
        left_out = [pltpu.roll(ref["lanes"][s], turn, 1) for s in range(species)]
        courant_south = pltpu.roll(ref["clat_south"][0], turn, 1)
        t = ref["table"][...]
        cols = pl.num_programs(0) * block
        wanted = []
        made = {}

        def make(ready):
            forcing = jnp.dot(t, jnp.concatenate([p for _, _, p in ready], axis=1), preferred_element_type=f32)
            for k, ((s, i), v, _) in enumerate(ready):
                v = v + forcing[:, k * rows : (k + 1) * rows] + jnp.where(ends, back(left_out[s], i), 0.0)
                if i == 0:
                    v = v + jnp.where(at_start, ref["column_start"][s], 0.0)
                if i == block - 1:
                    v = v + jnp.where(at_end, ref["column_end"][s], 0.0)
                made[s, i] = v

        for i in range(-1, block + 1):
            x = jnp.clip(start + i, 0, cols - 1)
            for s in range(species):
                v = ref["field_west"][s, 0] if i < 0 else ref["field_east"][s, 0] if i == block else field[s, i]
                wanted.append(((s, i), v, spread(ref["total"], s * cols + x, rows, t.shape[1] // 4)))
                if len(wanted) == 2:
                    make(wanted)
                    wanted.clear()
        if wanted:
            make(wanted)

        def at_column(s, i):
            return made[s, i]
    else:
        below, inside = jnp.where(first, 0.0, 1.0), jnp.where(last, 0.0, 1.0)
        finished = [[None] * block for _ in range(species)]

        def at_column(s, i):
            return ref["field_west"][s, 0] if i < 0 else ref["field_east"][s, 0] if i == block else field[s, i]

    def mix(ready):
        mixed = jnp.dot(
            w, jnp.concatenate([r for _, _, r in ready], axis=1), preferred_element_type=f32
        )
        for k, (s, i, _) in enumerate(ready):
            m = mixed[:, k * rows : (k + 1) * rows]
            out[s, i] = m
            if second:
                ref["flux"][s, pl.ds(start + i, 1), :] = at_column(s, i)[0:1] + m[0:1]
            else:
                finished[s][i] = m

    for i in range(block):
        cl, cw = clon[i], clat[i]
        cl_west = clon[i - 1] if i else ref["clon_before"][0]
        if i == 0 and second:
            cl_west = jnp.where(at_start, ref["clon_col"][0], cl_west)
        e = jnp.maximum(cl, 0.0) + kappa_mix
        w_ = kappa_mix - jnp.minimum(cl_west, 0.0)
        if not second and i == 0:
            w_ = jnp.where(at_start, 0.0, w_)
        if not second and i == block - 1:
            e = jnp.where(at_end, 0.0, e)
        n = (jnp.maximum(cw, 0.0) + kappa_mix) * inside
        cs = pltpu.roll(cw, 1, 1)
        if second:
            cs = jnp.where(first, back(courant_south, i), cs)
        s_ = (kappa_mix - jnp.minimum(cs, 0.0)) * below
        centre = 1.0 - (e + w_ + n + s_)
        for s in range(species):
            v, v_w, v_e = at_column(s, i), at_column(s, i - 1), at_column(s, i + 1)
            v_n, v_s = pltpu.roll(v, rows - 1, 1), pltpu.roll(v, 1, 1)
            if second:
                if i == 0:
                    v_w = jnp.where(at_start, ref["west_col"][s], v_w)
                if i == block - 1:
                    v_e = jnp.where(at_end, ref["east_col"][s], v_e)
                halo = back(halos[s], i)
                v_n, v_s = jnp.where(last, halo, v_n), jnp.where(first, halo, v_s)
            h = centre * v + e * v_e + w_ * v_w + n * v_n + s_ * v_s
            waiting.append((s, i, mix_parts(h)))
            if len(waiting) == 2:
                mix(waiting)
                waiting.clear()
    if waiting:
        mix(waiting)
    if not second:
        up, down, west, east = ref["up"], ref["down"], ref["west"], ref["east"]

        @pl.when(at_start)
        def _():
            up[...] = jnp.zeros_like(up)
            down[...] = jnp.zeros_like(down)
            for s in range(species):
                east[s] = out[s, 0]

        @pl.when(at_end)
        def _():
            for s in range(species):
                west[s] = out[s, block - 1]

        for s in range(species):
            up[s] = edge_lanes(finished[s], up[s], start, True)
            down[s] = edge_lanes(finished[s], down[s], start, False)


def mix_parts(h):
    high, low = split(h)
    return jnp.concatenate([high, low, high], axis=0).astype(bf16)


def left_out_kernel(
    lat_ref,
    up_own,
    down_own,
    west_own,
    east_own,
    south,
    north,
    west,
    east,
    weights,
    up_in,
    down_in,
    west_in,
    east_in,
    up,
    down,
    west_out,
    east_out,
    lanes,
    column_start,
    column_end,
    *,
    cols,
    lat_size,
):
    species, levels, rows = up_in.shape
    lane = lax.broadcasted_iota(jnp.int32, (levels, rows), 1)
    even = lane % 2 == 0
    ends = jnp.logical_or(lane == 0, lane == rows - 1)
    lat = lat_ref[0]
    below = jnp.where(lat == 0, 0.0, 1.0)
    inside = jnp.where(lat == lat_size - 1, 0.0, 1.0)
    far = 2 * (cols - 1)

    def later(v):
        return pltpu.roll(v, 1, 1)

    def sooner(v):
        return pltpu.roll(v, rows - 1, 1)

    n = (jnp.maximum(sooner(up_own[species]), 0.0) + kappa_mix) * inside
    s_ = (kappa_mix - jnp.minimum(south[species], 0.0)) * below
    w_ = kappa_mix - jnp.minimum(west[species], 0.0)
    e = jnp.maximum(west_own[species], 0.0) + kappa_mix
    w = weights[...]
    for s in range(species):
        rim = jnp.where(even, s_ * (south[s] - later(down_own[s])), n * (north[s] - sooner(up_own[s])))
        terms = [rim, w_ * (west[s] - east_own[s]), e * (east[s] - west_own[s])]
        mixed = jnp.dot(w, jnp.concatenate([mix_parts(h) for h in terms], axis=1), preferred_element_type=f32)
        c, c_start, c_end = [mixed[:, k * rows : (k + 1) * rows] for k in range(3)]
        lanes[s], column_start[s], column_end[s] = c, c_start, c_end
        up[s] = (
            up_in[s]
            + jnp.where(even, later(c), 0.0)
            + jnp.where(lane == 0, later(c_start), 0.0)
            + jnp.where(lane == far, pltpu.roll(c_end, far + 1, 1), 0.0)
        )
        down[s] = (
            down_in[s]
            + jnp.where(even, 0.0, sooner(c))
            + jnp.where(lane == rows - 1, sooner(c_start), 0.0)
            + jnp.where(lane == far - 1, pltpu.roll(c_end, far - 1, 1), 0.0)
        )
        west_out[s] = west_in[s] + c_end + jnp.where(ends, pltpu.roll(c, rows - far, 1), 0.0)
        east_out[s] = east_in[s] + c_start + jnp.where(ends, c, 0.0)


def left_out(lat, own, halo, weights, edges, cols, lat_size):
    shape = jax.ShapeDtypeStruct(edges[0].shape, f32)
    vmem = pl.BlockSpec(memory_space=pltpu.VMEM)
    return pl.pallas_call(
        functools.partial(left_out_kernel, cols=cols, lat_size=lat_size),
        out_shape=(shape,) * 7,
        in_specs=[pl.BlockSpec(memory_space=pltpu.SMEM)] + [vmem] * 13,
        out_specs=(vmem,) * 7,
        compiler_params=pltpu.CompilerParams(vmem_limit_bytes=SMALL_LIMIT),
        cost_estimate=pl.CostEstimate(flops=shape.size * 3000, bytes_accessed=shape.size * 100, transcendentals=0),
    )(lat, *own, *halo, weights, *edges)


def spread(total, sx, rows, akl):
    pair = total[
        pl.ds(pl.multiple_of((sx >> 1) * 2 * akl, 8), 2 * akl),
        pl.ds(pl.multiple_of((sx & 1) * rows, rows), rows),
    ]
    return jnp.concatenate(split(pair), axis=0).astype(bf16)


def step(field, clon, clat, weights, lat_size, more=None):
    species, cols, levels, rows = field.shape
    columns = pl.BlockSpec((species, BLOCK, levels, rows), lambda i: (0, i, 0, 0))
    courant = pl.BlockSpec((BLOCK, levels, rows), lambda i: (i, 0, 0))
    whole = lambda shape: pl.BlockSpec(shape, lambda i: (0,) * len(shape))
    part = lambda at: pl.BlockSpec((1, levels, rows), lambda i: (at, 0, 0))
    three = (species, levels, rows)
    given = {
        "field": (field, columns),
        "field_west": (
            field,
            pl.BlockSpec((species, 1, levels, rows), lambda i: (0, jnp.maximum(i * BLOCK - 1, 0), 0, 0)),
        ),
        "field_east": (
            field,
            pl.BlockSpec((species, 1, levels, rows), lambda i: (0, jnp.minimum(i * BLOCK + BLOCK, cols - 1), 0, 0)),
        ),
        "clon": (clon, courant),
        "clon_before": (clon, pl.BlockSpec((1, levels, rows), lambda i: (jnp.maximum(i * BLOCK - 1, 0), 0, 0))),
        "clat": (clat, courant),
        "weights": (weights, whole(weights.shape)),
    }
    if more is None:
        made = dict(up=three, down=three, west=three, east=three)
    else:
        made = dict(flux=(species, cols, rows))
        for name, value in more.items():
            spec = whole(value.shape)
            if name == "lat":
                spec = pl.BlockSpec(memory_space=pltpu.SMEM)
            elif name in ("clon_col", "clat_south"):
                spec = part(species)
            given[name] = (value, spec)
    return pl.pallas_call(
        functools.partial(step_kernel, names=(*given, "out", *made), lat_size=lat_size),
        out_shape=[pltpu.HBM(field.shape, f32)] + [jax.ShapeDtypeStruct(shape, f32) for shape in made.values()],
        grid=(cols // BLOCK,),
        in_specs=[spec for _, spec in given.values()],
        out_specs=[columns] + [whole(shape) for shape in made.values()],
        compiler_params=pltpu.CompilerParams(vmem_limit_bytes=VMEM_LIMIT),
        cost_estimate=pl.CostEstimate(
            flops=field.size * levels * 6, bytes_accessed=field.size * 12, transcendentals=0
        ),
    )(*[value for value, _ in given.values()])


def add_kernel(
    got_at,
    plain_up,
    plain_down,
    plain_west,
    plain_east,
    table,
    total,
    up,
    down,
    west,
    east,
    got,
    parts,
    group,
    middle,
    spot,
    parts_b,
    group_b,
    middle_b,
    spot_b,
    bounds,
    sem_got,
    *,
    cols,
):
    sources, held, slots = got_at.shape
    species, levels, rows = plain_up.shape
    akl = table.shape[1] // 4
    quarters = sem_got.shape[0]
    quarter = sources // quarters
    came = [
        pltpu.make_async_copy(got_at.at[pl.ds(q * quarter, quarter)], got.at[pl.ds(q * quarter, quarter)], sem_got.at[q])
        for q in range(quarters)
    ]
    for copy in came:
        copy.start()
    second = (lax.broadcasted_iota(jnp.int32, (TILE, WIDE), 0) >= TILE // 2).astype(f32)
    quarter_of = lax.broadcasted_iota(jnp.int32, (held, slots), 1) // (slots // 4)
    length = sources * slots // 2
    outer = length // 4
    halfway = half_segment(species * cols)
    halves = ((parts, group, middle, spot), (parts_b, group_b, middle_b, spot_b))

    def put(to, row, at):
        to_parts, to_group, to_middle, to_spot = to
        at = pl.ds(at if isinstance(at, int) else pl.multiple_of(at, LANES), WIDE)
        segment = row[akl : akl + 1].astype(jnp.int32) - 1
        mark(to_spot, at, segment & (WIDE - 1))
        pair = jnp.broadcast_to((segment >> 8).astype(f32), (TILE, WIDE))
        to_group[:, at] = pair.astype(bf16)
        to_middle[:, at] = (pair - second).astype(bf16)
        high, low = split(row[:akl])
        both = jnp.concatenate([high, low], axis=0)
        to_parts[:, at] = jnp.concatenate([both, both], axis=0).astype(bf16)
        return segment

    def prepare(half, g):
        fours = []
        for b in range(2):
            turned = [got[half * (sources // 2) + 8 * g + 4 * b + k] for k in range(4)]
            turned = [pltpu.roll(v, k * (slots // 4), 1) if k else v for k, v in enumerate(turned)]
            rows_of = []
            for q in range(4):
                row = turned[0]
                for k in range(1, 4):
                    row = jnp.where(quarter_of == (q + k) % 4, turned[k], row)
                rows_of.append(row)
            fours.append(rows_of)
        row = [jnp.concatenate([fours[0][q], fours[1][q]], axis=1) for q in range(4)]
        to = halves[half]
        segment = put(to, row[0], g * WIDE)
        bounds[0:1] = jnp.maximum(bounds[0:1], segment)
        put(to, row[1], outer + 2 * g * WIDE)
        put(to, row[2], outer + (2 * g + 1) * WIDE)
        segment = put(to, row[3], 3 * outer + g * WIDE)
        bounds[1:2] = jnp.minimum(bounds[1:2], jnp.where(segment < 0, 2 * halfway, segment))

    def prepare_one(g, carry):
        prepare(0, g)
        return carry

    bounds[0:1] = jnp.full((1, WIDE), -1, jnp.int32)
    bounds[1:2] = jnp.full((1, WIDE), 2 * halfway, jnp.int32)
    steps = sources // 16
    for q, copy in enumerate(came):
        copy.wait()
        if q < 2:
            lax.fori_loop(q * steps // 2, (q + 1) * steps // 2, prepare_one, 0)

    tiles = ((0, 0), (0, 0), (1, 0), (0, 1), (0, 1))
    groups = total.shape[0] // (4 * akl)
    lower, higher = (0, groups // 2), (groups // 2, groups)

    def add(half, of, depth, begin, end, **how):
        held_parts, held_group, held_middle, held_spot = halves[half]
        onehot_product(
            held_parts, [held_group, held_middle], tiles, held_spot, total, of, 2, groups // 2, depth, begin, end, **how
        )

    def beside(steps_now):
        def run(_):
            for g in steps_now:
                prepare(1, g)

        return run

    add(0, lower, 3 * outer, 0, 3 * outer, beside=beside(range(steps // 2)))
    add(0, higher, 3 * outer, outer, length, beside=beside(range(steps // 2, steps)))
    add(1, lower, 3 * outer, 0, 3 * outer, onto=True)
    add(1, higher, 3 * outer, outer, length, onto=True)
    highest, lowest = jnp.max(bounds[0:1]), jnp.min(bounds[1:2])

    @pl.when(highest >= halfway)
    def _():
        for half in range(2):
            add(half, higher, outer, 0, outer, onto=True)

    @pl.when(lowest < halfway)
    def _():
        for half in range(2):
            add(half, lower, outer, 3 * outer, length, onto=True)

    t = table[...]

    def forced(parts_of, before):
        return before + jnp.dot(t, parts_of, preferred_element_type=f32)

    for s in range(species):
        east[s] = forced(spread(total, s * cols, rows, akl), plain_east[s])
        west[s] = forced(spread(total, s * cols + cols - 1, rows, akl), plain_west[s])

        def of_block(b, carry):
            columns = []
            for i in range(BLOCK):
                sx = s * cols + b * BLOCK + i
                columns.append(
                    total[
                        pl.ds(pl.multiple_of((sx >> 1) * 2 * akl, 8), 2 * akl),
                        pl.ds(pl.multiple_of((sx & 1) * rows, rows), rows),
                    ]
                )
            return tuple(edge_lanes(columns, kept, b * BLOCK, k == 0) for k, kept in enumerate(carry))

        none = jnp.zeros((2 * akl, rows), f32)
        ends = lax.fori_loop(0, cols // BLOCK, of_block, (none, none))
        for end, before, after in zip(ends, (plain_up, plain_down), (up, down)):
            after[s] = forced(jnp.concatenate(split(end), axis=0).astype(bf16), before[s])


def add_soundings(got, edges, table, cols):
    sources, held, slots = got.shape
    species, levels, rows = edges[0].shape
    akl = table.shape[1] // 4
    length = sources * slots
    pairs = -(-species * cols // 4)
    halves = [pltpu.VMEM((rows_held, length // 2), bf16) for rows_held in (4 * akl, TILE, TILE, WIDE)]
    edge = jax.ShapeDtypeStruct((species, levels, rows), f32)
    vmem, hbm = pl.BlockSpec(memory_space=pltpu.VMEM), pl.BlockSpec(memory_space=pl.ANY)
    return pl.pallas_call(
        functools.partial(add_kernel, cols=cols),
        out_shape=(jax.ShapeDtypeStruct((pairs * 4 * akl, WIDE), f32), edge, edge, edge, edge),
        in_specs=[hbm] + [vmem] * 5,
        out_specs=(vmem,) * 5,
        scratch_shapes=(
            pltpu.VMEM(got.shape, f32),
            *halves,
            *halves,
            pltpu.VMEM((2, WIDE), jnp.int32),
            pltpu.SemaphoreType.DMA((4,)),
        ),
        compiler_params=pltpu.CompilerParams(vmem_limit_bytes=ADD_LIMIT),
        cost_estimate=pl.CostEstimate(
            flops=2 * pairs * 4 * akl * WIDE * length,
            bytes_accessed=4 * got.size,
            transcendentals=0,
        ),
    )(got, *edges, table)


def on_device(
    adjoint_in,
    courant_lon,
    courant_lat,
    vertical_mix,
    sounding_values,
    sounding_dest,
    sounding_target,
    level_index,
):
    lat_size, lon_size = lax.axis_size("lat"), lax.axis_size("lon")
    n_tiles = lat_size * lon_size
    species, levels, cols, rows = adjoint_in.shape
    east_way = [(i, (i + 1) % lon_size) for i in range(lon_size)]
    west_way = [(j, i) for i, j in east_way]
    north_way = [(i, (i + 1) % lat_size) for i in range(lat_size)]
    south_way = [(j, i) for i, j in north_way]

    field = adjoint_in.transpose(0, 2, 1, 3)
    clon = courant_lon.transpose(1, 0, 2)
    clat = courant_lat.transpose(1, 0, 2)
    lat = lax.axis_index("lat").reshape(1)

    sent, *own = pack(sounding_dest, sounding_values, sounding_target, field, clon, clat, n_tiles)
    got = lax.all_to_all(sent, ("lat", "lon"), split_axis=0, concat_axis=0, tiled=True)

    def exchange(up, down, west, east):
        return (
            lax.ppermute(up, "lat", north_way),
            lax.ppermute(down, "lat", south_way),
            lax.ppermute(west, "lon", east_way),
            lax.ppermute(east, "lon", west_way),
        )

    halo = exchange(*own)
    weights = mix_weights(vertical_mix)
    table = (jnp.arange(levels, dtype=jnp.int32)[:, None] == level_index[None, :]).astype(bf16)
    table = jnp.concatenate([table] * 4, axis=1)
    plain, *edges = step(field, clon, clat, weights, lat_size)
    total, *edges = add_soundings(got, edges, table, cols)
    *edges, lanes, column_start, column_end = left_out(lat, own, halo, weights, edges, cols, lat_size)
    south, north, west, east = exchange(*edges)
    more = dict(
        lat=lat,
        south=south,
        north=north,
        west_col=west,
        east_col=east,
        clon_col=halo[2],
        clat_south=halo[0],
        total=total,
        table=table,
        lanes=lanes,
        column_start=column_start,
        column_end=column_end,
    )
    out, flux = step(plain, clon, clat, weights, lat_size, more)
    return out.transpose(0, 2, 1, 3), flux


def solution(mesh):
    return jax.shard_map(
        on_device,
        mesh=mesh,
        in_specs=(
            P(None, None, "lon", "lat"),
            P(None, "lon", "lat"),
            P(None, "lon", "lat"),
            P(),
            P(None, ("lat", "lon")),
            P(("lat", "lon"), None),
            P(("lat", "lon")),
            P(),
        ),
        out_specs=(P(None, None, "lon", "lat"), P(None, "lon", "lat")),
        check_vma=False,
    )
```

```python
import functools

import jax
import jax.numpy as jnp
from jax import lax
from jax.experimental import pallas as pl
from jax.experimental.pallas import tpu as pltpu
from jax.sharding import PartitionSpec as P

kappa_mix = 0.05
LANES = 128
WIDE = 256
TILE = 16
f32 = jnp.float32
bf16 = jnp.bfloat16
BLOCK = 15
VMEM_LIMIT = 52 * 2**20
PACK_LIMIT = 58 * 2**20
SMALL_LIMIT = 48 * 2**20
ADD_LIMIT = 49 * 2**20


def split(value):
    high = value.astype(bf16).astype(f32)
    return high, value - high


def nt_dot(a, b):
    return lax.dot_general(a, b, (((1,), (1,)), ((), ())), preferred_element_type=f32)


def onehot_product(parts, keys, tiles, spot, total, groups, step, together, depth, begin, end, onto=False, beside=None):
    rows = parts.shape[0]
    chunks = (end - begin) // depth

    def chunk(g, c):
        at = pl.ds(pl.multiple_of(begin + c * depth, LANES), depth)
        key = [k[:, at] for k in keys]
        held = [parts[TILE * q : TILE * (q + 1), at] for q in range(len(tiles))]
        none = jnp.zeros_like(held[0])
        left = []
        for i in range(together):
            hit = {}
            for kind in tiles:
                if kind not in hit:
                    which, offset = kind
                    number = jnp.asarray((g * together + i) * step + offset, jnp.int32).astype(f32).astype(bf16)
                    hit[kind] = key[which] == number
            left += [jnp.where(hit[kind], part, none) for kind, part in zip(tiles, held)]
        return nt_dot(jnp.concatenate(left, axis=0), spot[:, at])

    def of_group(g, carry):
        to = pl.ds(pl.multiple_of(g * (together * rows), together * rows), together * rows)
        if beside is not None:
            beside(g)
        if not onto:
            total[to, :] = chunk(g, 0)

        def of_chunk(c, carry):
            total[to, :] += chunk(g, c)
            return carry

        return lax.fori_loop(0 if onto else 1, chunks, of_chunk, carry)

    lax.fori_loop(groups[0] // together, groups[1] // together, of_group, 0)


def mark(spot, at, row):
    row = jnp.broadcast_to(row.astype(f32), (TILE, row.shape[1])).astype(bf16)
    base = lax.broadcasted_iota(jnp.int32, row.shape, 0).astype(f32).astype(bf16)
    one, none = jnp.ones_like(row), jnp.zeros_like(row)
    for q in range(WIDE // TILE):
        spot[TILE * q : TILE * (q + 1), at] = jnp.where(row - jnp.asarray(TILE * q, bf16) == base, one, none)


def turn(v, by):
    return pltpu.roll(v, by % v.shape[1], 1)


def is_even(shape):
    return lax.broadcasted_iota(jnp.int32, shape, 1) % 2 == 0


def interleave(values, to, first_even):
    even = is_even(values[0].shape)
    mine = even if first_even else jnp.logical_not(even)
    for k in range(0, len(values), 2):
        both = values[k]
        if k + 1 < len(values):
            both = jnp.where(mine, both, turn(values[k + 1], 1 if first_even else -1))
        to[k // 2] = both


def apart(held, s, first_even):
    return held[s // 2] if s % 2 == 0 else turn(held[s // 2], -1 if first_even else 1)


def edge_lanes(columns, kept, first, up, share=None):
    rows = kept.shape[1]
    lane = lax.broadcasted_iota(jnp.int32, kept.shape, 1)
    own = jnp.zeros_like(kept)
    for i, v in enumerate(columns):
        if up:
            own = jnp.where(lane == 2 * i, pltpu.roll(v, 2 * i + 1, 1), own)
        else:
            own = jnp.where(lane == 2 * i + 1, pltpu.roll(v, 2 * i + 1, 1), own)
    if share is not None:
        own = own * share
    turn = 2 * first if up else lax.rem(2 * first + rows - 2, rows)
    return kept + pltpu.roll(own, turn, 1)


PACK = (16, 8192)


def whole_part(value, divisor):
    return ((value.astype(f32) + 0.5) * (1.0 / divisor)).astype(jnp.int32)


def half_segment(columns):
    return -(-columns // 4) // 2 * 2 * WIDE


def pack_kernel(
    dest,
    values,
    target,
    field_at,
    clon_at,
    clat_at,
    out,
    up_sent,
    down_sent,
    west,
    east,
    parts,
    group,
    spot,
    total,
    field,
    clat,
    up,
    down,
    sems,
):
    n_tiles, held, _ = out.shape
    species, cols, _, rows = field.shape
    copies = [(field_at, field), (clat_at, clat), (clon_at.at[cols - 1], west.at[species])]
    for s in range(species):
        copies += [(field_at.at[s, cols - 1], west.at[s]), (field_at.at[s, 0], east.at[s])]
    copies = [pltpu.make_async_copy(*pair, sems.at[i]) for i, pair in enumerate(copies)]
    for copy in copies:
        copy.start()
    up[...] = jnp.zeros_like(up)
    down[...] = jnp.zeros_like(down)
    levels, length = values.shape
    iota_t = lax.broadcasted_iota(jnp.int32, (n_tiles, WIDE), 0)
    square = (WIDE, WIDE)
    upper = (
        lax.broadcasted_iota(jnp.int32, square, 0) < lax.broadcasted_iota(jnp.int32, square, 1)
    ).astype(f32).astype(bf16)

    halfway = half_segment(species * cols)

    def rank(at, base):
        d = dest[:, at]
        t = target[:, at]
        cell = whole_part(t, species)
        row_of = whole_part(cell, cols)
        segment = ((t - cell * species) * cols + cell - row_of * cols) * rows + row_of
        upper_half = segment >= halfway
        hot = iota_t == d
        hot_f = jnp.where(hot, jnp.where(upper_half, 256.0, 1.0), 0.0)
        earlier = jnp.dot(hot_f.astype(bf16), upper, preferred_element_type=f32) + base
        own = jnp.sum(jnp.where(hot, earlier, 0.0), axis=0, keepdims=True).astype(jnp.int32)
        slot = jnp.where(upper_half, LANES - 1 - (own >> 8), own & 255)
        low = slot + (d & 1) * LANES
        mark(spot, at, low)
        group[:, at] = jnp.broadcast_to((d >> 1).astype(f32), (TILE, WIDE)).astype(bf16)
        row = jnp.concatenate(
            [values[:, at], (segment + 1).astype(f32), jnp.zeros((held - levels - 1, WIDE), f32)], axis=0
        )
        parts[:, at] = jnp.concatenate(split(row), axis=0).astype(bf16)
        return base + jnp.sum(hot_f, axis=1, keepdims=True)

    def ranks(b, base):
        for i in range(4):
            base = rank(pl.ds(pl.multiple_of((4 * b + i) * WIDE, WIDE), WIDE), base)
        return base

    lax.fori_loop(0, length // (4 * WIDE), ranks, jnp.zeros((n_tiles, 1), f32))
    for copy in copies:
        copy.wait()
    blocks = cols // BLOCK

    def take_edges(g):
        first = jnp.minimum(g, blocks - 1) * BLOCK
        new = (g < blocks).astype(f32)
        for s in range(species + 1):
            columns = [field[s, first + i] if s < species else clat[first + i] for i in range(BLOCK)]
            up[s] = edge_lanes(columns, up[s], first, True, new)
            if s < species:
                down[s] = edge_lanes(columns, down[s], first, False, new)

    tiles = ((0, 0),) * (2 * held // TILE)
    onehot_product(
        parts, [group], tiles, spot, total, (0, n_tiles // 2), 1, *PACK, 0, length, beside=take_edges
    )
    interleave([up[s] for s in range(species + 1)], up_sent, True)
    interleave([down[s] for s in range(species)], down_sent, False)

    def put(g, carry):
        for i in range(4):
            j = 4 * g + i
            at = pl.multiple_of(j * 2 * held, 2 * held)
            both = total[pl.ds(at, held), :] + total[pl.ds(at + held, held), :]
            out[2 * j] = both[:, :LANES]
            out[2 * j + 1] = both[:, LANES:]
        return carry

    lax.fori_loop(0, n_tiles // 8, put, 0)


def pack(dest, values, target, field, clon, clat, n_tiles):
    levels, length = values.shape
    species, cols, depth, rows = field.shape
    held = -(-(levels + 1) // 8) * 8
    four, three = (species + 1, depth, rows), (species, depth, rows)
    up, down = ((species + 2) // 2, depth, rows), ((species + 1) // 2, depth, rows)
    vmem, hbm = pl.BlockSpec(memory_space=pltpu.VMEM), pl.BlockSpec(memory_space=pl.ANY)
    return pl.pallas_call(
        pack_kernel,
        out_shape=tuple(
            jax.ShapeDtypeStruct(shape, f32) for shape in ((n_tiles, held, LANES), up, down, four, three)
        ),
        in_specs=[vmem, vmem, vmem, hbm, hbm, hbm],
        out_specs=(vmem,) * 5,
        scratch_shapes=(
            pltpu.VMEM((2 * held, length), bf16),
            pltpu.VMEM((TILE, length), bf16),
            pltpu.VMEM((WIDE, length), bf16),
            pltpu.VMEM((n_tiles // 2 * 2 * held, WIDE), f32),
            pltpu.VMEM(field.shape, f32),
            pltpu.VMEM(clat.shape, f32),
            pltpu.VMEM(four, f32),
            pltpu.VMEM(three, f32),
            pltpu.SemaphoreType.DMA((3 + 2 * species,)),
        ),
        compiler_params=pltpu.CompilerParams(vmem_limit_bytes=PACK_LIMIT),
        cost_estimate=pl.CostEstimate(
            flops=2 * length * n_tiles * LANES * 2 * held,
            bytes_accessed=4 * (length * 22 + n_tiles * held * LANES + field.size),
            transcendentals=0,
        ),
    )(dest.reshape(1, length), values, target.reshape(1, length), field, clon, clat)


def mix_weights(vertical_mix):
    levels = vertical_mix.shape[0]
    matrix = (jnp.eye(levels, dtype=f32) + vertical_mix).T
    high = lax.reduce_precision(matrix, 8, 7)
    return jnp.concatenate([high, high, matrix - high], axis=1).astype(bf16)


def step_kernel(*refs, names, lat_size):
    ref = dict(zip(names, refs))
    second = "total" in ref
    field, clon, clat, out = ref["field"], ref["clon"], ref["clat"], ref["out"]
    species, block, levels, rows = field.shape
    lane = lax.broadcasted_iota(jnp.int32, (levels, rows), 1)
    first, last = lane == 0, lane == rows - 1
    here = pl.program_id(0)
    at_start, at_end = here == 0, here == pl.num_programs(0) - 1
    start = here * block
    w = ref["weights"][...]
    waiting = []

    def back(v, i):
        return pltpu.roll(v, (rows - 2 * i) % rows, 1) if i else v

    if second:
        lat = ref["lat"][0]
        below = jnp.where(jnp.logical_and(first, lat == 0), 0.0, 1.0)
        inside = jnp.where(jnp.logical_and(last, lat == lat_size - 1), 0.0, 1.0)
        back_to_start = lax.rem(rows - 2 * start, rows)
        even = lane % 2 == 0
        ends = jnp.logical_or(first, last)
        halos = [
            pltpu.roll(
                jnp.where(even, apart(ref["south"], s, True), apart(ref["north"], s, False)), back_to_start, 1
            )
            for s in range(species)
        ]
        left_out = [pltpu.roll(ref["lanes"][s], back_to_start, 1) for s in range(species)]
        courant_south = pltpu.roll(apart(ref["clat_south"], species, True), back_to_start, 1)
        t = ref["table"][...]
        cols = pl.num_programs(0) * block
        wanted = []
        made = {}

        def make(ready):
            forcing = jnp.dot(t, jnp.concatenate([p for _, _, p in ready], axis=1), preferred_element_type=f32)
            for k, ((s, i), v, _) in enumerate(ready):
                v = v + forcing[:, k * rows : (k + 1) * rows] + jnp.where(ends, back(left_out[s], i), 0.0)
                if i == 0:
                    v = v + jnp.where(at_start, ref["column_start"][s], 0.0)
                if i == block - 1:
                    v = v + jnp.where(at_end, ref["column_end"][s], 0.0)
                made[s, i] = v

        for i in range(-1, block + 1):
            x = jnp.clip(start + i, 0, cols - 1)
            for s in range(species):
                v = ref["field_west"][s, 0] if i < 0 else ref["field_east"][s, 0] if i == block else field[s, i]
                wanted.append(((s, i), v, spread(ref["total"], s * cols + x, rows, t.shape[1] // 4)))
                if len(wanted) == 2:
                    make(wanted)
                    wanted.clear()
        if wanted:
            make(wanted)

        def at_column(s, i):
            return made[s, i]
    else:
        below, inside = jnp.where(first, 0.0, 1.0), jnp.where(last, 0.0, 1.0)
        finished = [[None] * block for _ in range(species)]

        def at_column(s, i):
            return ref["field_west"][s, 0] if i < 0 else ref["field_east"][s, 0] if i == block else field[s, i]

    def mix(ready):
        mixed = jnp.dot(
            w, jnp.concatenate([r for _, _, r in ready], axis=1), preferred_element_type=f32
        )
        for k, (s, i, _) in enumerate(ready):
            m = mixed[:, k * rows : (k + 1) * rows]
            out[s, i] = m
            if second:
                ref["flux"][s, pl.ds(start + i, 1), :] = at_column(s, i)[0:1] + m[0:1]
            else:
                finished[s][i] = m

    for i in range(block):
        cl, cw = clon[i], clat[i]
        cl_west = clon[i - 1] if i else ref["clon_before"][0]
        if i == 0 and second:
            cl_west = jnp.where(at_start, ref["clon_col"][0], cl_west)
        e = jnp.maximum(cl, 0.0) + kappa_mix
        w_ = kappa_mix - jnp.minimum(cl_west, 0.0)
        if not second and i == 0:
            w_ = jnp.where(at_start, 0.0, w_)
        if not second and i == block - 1:
            e = jnp.where(at_end, 0.0, e)
        n = (jnp.maximum(cw, 0.0) + kappa_mix) * inside
        cs = pltpu.roll(cw, 1, 1)
        if second:
            cs = jnp.where(first, back(courant_south, i), cs)
        s_ = (kappa_mix - jnp.minimum(cs, 0.0)) * below
        centre = 1.0 - (e + w_ + n + s_)
        for s in range(species):
            v, v_w, v_e = at_column(s, i), at_column(s, i - 1), at_column(s, i + 1)
            v_n, v_s = pltpu.roll(v, rows - 1, 1), pltpu.roll(v, 1, 1)
            if second:
                if i == 0:
                    v_w = jnp.where(at_start, ref["west_col"][s], v_w)
                if i == block - 1:
                    v_e = jnp.where(at_end, ref["east_col"][s], v_e)
                halo = back(halos[s], i)
                v_n, v_s = jnp.where(last, halo, v_n), jnp.where(first, halo, v_s)
            h = centre * v + e * v_e + w_ * v_w + n * v_n + s_ * v_s
            waiting.append((s, i, mix_parts(h)))
            if len(waiting) == 2:
                mix(waiting)
                waiting.clear()
    if waiting:
        mix(waiting)
    if not second:
        up, down, west, east = ref["up"], ref["down"], ref["west"], ref["east"]

        @pl.when(at_start)
        def _():
            up[...] = jnp.zeros_like(up)
            down[...] = jnp.zeros_like(down)
            for s in range(species):
                east[s] = out[s, 0]

        @pl.when(at_end)
        def _():
            for s in range(species):
                west[s] = out[s, block - 1]

        for s in range(species):
            up[s] = edge_lanes(finished[s], up[s], start, True)
            down[s] = edge_lanes(finished[s], down[s], start, False)


def mix_parts(h):
    high, low = split(h)
    return jnp.concatenate([high, low, high], axis=0).astype(bf16)


def left_out_kernel(
    lat_ref,
    up_own,
    down_own,
    west_own,
    east_own,
    south,
    north,
    west,
    east,
    weights,
    up_in,
    down_in,
    west_in,
    east_in,
    up,
    down,
    west_out,
    east_out,
    lanes,
    column_start,
    column_end,
    *,
    cols,
    lat_size,
):
    species, levels, rows = up_in.shape
    lane = lax.broadcasted_iota(jnp.int32, (levels, rows), 1)
    even = lane % 2 == 0
    ends = jnp.logical_or(lane == 0, lane == rows - 1)
    lat = lat_ref[0]
    below = jnp.where(lat == 0, 0.0, 1.0)
    inside = jnp.where(lat == lat_size - 1, 0.0, 1.0)
    far = 2 * (cols - 1)

    def later(v):
        return pltpu.roll(v, 1, 1)

    def sooner(v):
        return pltpu.roll(v, rows - 1, 1)

    ups, downs = [], []
    n = (jnp.maximum(sooner(apart(up_own, species, True)), 0.0) + kappa_mix) * inside
    s_ = (kappa_mix - jnp.minimum(apart(south, species, True), 0.0)) * below
    w_ = kappa_mix - jnp.minimum(west[species], 0.0)
    e = jnp.maximum(west_own[species], 0.0) + kappa_mix
    w = weights[...]
    for s in range(species):
        from_south = s_ * (apart(south, s, True) - later(apart(down_own, s, False)))
        from_north = n * (apart(north, s, False) - sooner(apart(up_own, s, True)))
        rim = jnp.where(even, from_south, from_north)
        terms = [rim, w_ * (west[s] - east_own[s]), e * (east[s] - west_own[s])]
        mixed = jnp.dot(w, jnp.concatenate([mix_parts(h) for h in terms], axis=1), preferred_element_type=f32)
        c, c_start, c_end = [mixed[:, k * rows : (k + 1) * rows] for k in range(3)]
        lanes[s], column_start[s], column_end[s] = c, c_start, c_end
        ups.append(
            up_in[s]
            + jnp.where(even, later(c), 0.0)
            + jnp.where(lane == 0, later(c_start), 0.0)
            + jnp.where(lane == far, pltpu.roll(c_end, far + 1, 1), 0.0)
        )
        downs.append(
            down_in[s]
            + jnp.where(even, 0.0, sooner(c))
            + jnp.where(lane == rows - 1, sooner(c_start), 0.0)
            + jnp.where(lane == far - 1, pltpu.roll(c_end, far - 1, 1), 0.0)
        )
        west_out[s] = west_in[s] + c_end + jnp.where(ends, pltpu.roll(c, rows - far, 1), 0.0)
        east_out[s] = east_in[s] + c_start + jnp.where(ends, c, 0.0)
    interleave(ups, up, True)
    interleave(downs, down, False)


def left_out(lat, own, halo, weights, edges, cols, lat_size):
    shape = jax.ShapeDtypeStruct(edges[0].shape, f32)
    vmem = pl.BlockSpec(memory_space=pltpu.VMEM)
    return pl.pallas_call(
        functools.partial(left_out_kernel, cols=cols, lat_size=lat_size),
        out_shape=(jax.ShapeDtypeStruct(((len(edges[0]) + 1) // 2, *shape.shape[1:]), f32),) * 2 + (shape,) * 5,
        in_specs=[pl.BlockSpec(memory_space=pltpu.SMEM)] + [vmem] * 13,
        out_specs=(vmem,) * 7,
        compiler_params=pltpu.CompilerParams(vmem_limit_bytes=SMALL_LIMIT),
        cost_estimate=pl.CostEstimate(flops=shape.size * 3000, bytes_accessed=shape.size * 100, transcendentals=0),
    )(lat, *own, *halo, weights, *edges)


def spread(total, sx, rows, akl):
    pair = total[
        pl.ds(pl.multiple_of((sx >> 1) * 2 * akl, 8), 2 * akl),
        pl.ds(pl.multiple_of((sx & 1) * rows, rows), rows),
    ]
    return jnp.concatenate(split(pair), axis=0).astype(bf16)


def step(field, clon, clat, weights, lat_size, more=None):
    species, cols, levels, rows = field.shape
    columns = pl.BlockSpec((species, BLOCK, levels, rows), lambda i: (0, i, 0, 0))
    courant = pl.BlockSpec((BLOCK, levels, rows), lambda i: (i, 0, 0))
    whole = lambda shape: pl.BlockSpec(shape, lambda i: (0,) * len(shape))
    part = lambda at: pl.BlockSpec((1, levels, rows), lambda i: (at, 0, 0))
    three = (species, levels, rows)
    given = {
        "field": (field, columns),
        "field_west": (
            field,
            pl.BlockSpec((species, 1, levels, rows), lambda i: (0, jnp.maximum(i * BLOCK - 1, 0), 0, 0)),
        ),
        "field_east": (
            field,
            pl.BlockSpec((species, 1, levels, rows), lambda i: (0, jnp.minimum(i * BLOCK + BLOCK, cols - 1), 0, 0)),
        ),
        "clon": (clon, courant),
        "clon_before": (clon, pl.BlockSpec((1, levels, rows), lambda i: (jnp.maximum(i * BLOCK - 1, 0), 0, 0))),
        "clat": (clat, courant),
        "weights": (weights, whole(weights.shape)),
    }
    if more is None:
        made = dict(up=three, down=three, west=three, east=three)
    else:
        made = dict(flux=(species, cols, rows))
        for name, value in more.items():
            spec = whole(value.shape)
            if name == "lat":
                spec = pl.BlockSpec(memory_space=pltpu.SMEM)
            elif name == "clon_col":
                spec = part(species)
            given[name] = (value, spec)
    return pl.pallas_call(
        functools.partial(step_kernel, names=(*given, "out", *made), lat_size=lat_size),
        out_shape=[pltpu.HBM(field.shape, f32)] + [jax.ShapeDtypeStruct(shape, f32) for shape in made.values()],
        grid=(cols // BLOCK,),
        in_specs=[spec for _, spec in given.values()],
        out_specs=[columns] + [whole(shape) for shape in made.values()],
        compiler_params=pltpu.CompilerParams(vmem_limit_bytes=VMEM_LIMIT),
        cost_estimate=pl.CostEstimate(
            flops=field.size * levels * 6, bytes_accessed=field.size * 12, transcendentals=0
        ),
    )(*[value for value, _ in given.values()])


def add_kernel(
    got_at,
    plain_up,
    plain_down,
    plain_west,
    plain_east,
    table,
    total,
    up,
    down,
    west,
    east,
    got,
    parts,
    group,
    middle,
    spot,
    parts_b,
    group_b,
    middle_b,
    spot_b,
    bounds,
    sem_got,
    *,
    cols,
):
    sources, held, slots = got_at.shape
    species, levels, rows = plain_up.shape
    akl = table.shape[1] // 4
    quarters = sem_got.shape[0]
    quarter = sources // quarters
    came = [
        pltpu.make_async_copy(got_at.at[pl.ds(q * quarter, quarter)], got.at[pl.ds(q * quarter, quarter)], sem_got.at[q])
        for q in range(quarters)
    ]
    for copy in came:
        copy.start()
    second = (lax.broadcasted_iota(jnp.int32, (TILE, WIDE), 0) >= TILE // 2).astype(f32)
    quarter_of = lax.broadcasted_iota(jnp.int32, (held, slots), 1) // (slots // 4)
    length = sources * slots // 2
    outer = length // 4
    halfway = half_segment(species * cols)
    halves = ((parts, group, middle, spot), (parts_b, group_b, middle_b, spot_b))

    def put(to, row, at):
        to_parts, to_group, to_middle, to_spot = to
        at = pl.ds(at if isinstance(at, int) else pl.multiple_of(at, LANES), WIDE)
        segment = row[akl : akl + 1].astype(jnp.int32) - 1
        mark(to_spot, at, segment & (WIDE - 1))
        pair = jnp.broadcast_to((segment >> 8).astype(f32), (TILE, WIDE))
        to_group[:, at] = pair.astype(bf16)
        to_middle[:, at] = (pair - second).astype(bf16)
        high, low = split(row[:akl])
        both = jnp.concatenate([high, low], axis=0)
        to_parts[:, at] = jnp.concatenate([both, both], axis=0).astype(bf16)
        return segment

    def prepare(half, g):
        fours = []
        for b in range(2):
            turned = [got[half * (sources // 2) + 8 * g + 4 * b + k] for k in range(4)]
            turned = [pltpu.roll(v, k * (slots // 4), 1) if k else v for k, v in enumerate(turned)]
            rows_of = []
            for q in range(4):
                row = turned[0]
                for k in range(1, 4):
                    row = jnp.where(quarter_of == (q + k) % 4, turned[k], row)
                rows_of.append(row)
            fours.append(rows_of)
        row = [jnp.concatenate([fours[0][q], fours[1][q]], axis=1) for q in range(4)]
        to = halves[half]
        segment = put(to, row[0], g * WIDE)
        bounds[0:1] = jnp.maximum(bounds[0:1], segment)
        put(to, row[1], outer + 2 * g * WIDE)
        put(to, row[2], outer + (2 * g + 1) * WIDE)
        segment = put(to, row[3], 3 * outer + g * WIDE)
        bounds[1:2] = jnp.minimum(bounds[1:2], jnp.where(segment < 0, 2 * halfway, segment))

    def prepare_one(g, carry):
        prepare(0, g)
        return carry

    bounds[0:1] = jnp.full((1, WIDE), -1, jnp.int32)
    bounds[1:2] = jnp.full((1, WIDE), 2 * halfway, jnp.int32)
    steps = sources // 16
    for q, copy in enumerate(came):
        copy.wait()
        if q < 2:
            lax.fori_loop(q * steps // 2, (q + 1) * steps // 2, prepare_one, 0)

    tiles = ((0, 0), (0, 0), (1, 0), (0, 1), (0, 1))
    groups = total.shape[0] // (4 * akl)
    lower, higher = (0, groups // 2), (groups // 2, groups)

    def add(half, of, depth, begin, end, **how):
        held_parts, held_group, held_middle, held_spot = halves[half]
        onehot_product(
            held_parts, [held_group, held_middle], tiles, held_spot, total, of, 2, groups // 2, depth, begin, end, **how
        )

    def beside(steps_now):
        def run(_):
            for g in steps_now:
                prepare(1, g)

        return run

    add(0, lower, 3 * outer, 0, 3 * outer, beside=beside(range(steps // 2)))
    add(0, higher, 3 * outer, outer, length, beside=beside(range(steps // 2, steps)))
    add(1, lower, 3 * outer, 0, 3 * outer, onto=True)
    add(1, higher, 3 * outer, outer, length, onto=True)
    highest, lowest = jnp.max(bounds[0:1]), jnp.min(bounds[1:2])

    @pl.when(highest >= halfway)
    def _():
        for half in range(2):
            add(half, higher, outer, 0, outer, onto=True)

    @pl.when(lowest < halfway)
    def _():
        for half in range(2):
            add(half, lower, outer, 3 * outer, length, onto=True)

    t = table[...]

    def forced(parts_of, before):
        return before + jnp.dot(t, parts_of, preferred_element_type=f32)

    for s in range(species):
        east[s] = forced(spread(total, s * cols, rows, akl), plain_east[s])
        west[s] = forced(spread(total, s * cols + cols - 1, rows, akl), plain_west[s])

        def of_block(b, carry):
            columns = []
            for i in range(BLOCK):
                sx = s * cols + b * BLOCK + i
                columns.append(
                    total[
                        pl.ds(pl.multiple_of((sx >> 1) * 2 * akl, 8), 2 * akl),
                        pl.ds(pl.multiple_of((sx & 1) * rows, rows), rows),
                    ]
                )
            return tuple(edge_lanes(columns, kept, b * BLOCK, k == 0) for k, kept in enumerate(carry))

        none = jnp.zeros((2 * akl, rows), f32)
        ends = lax.fori_loop(0, cols // BLOCK, of_block, (none, none))
        for end, before, after in zip(ends, (plain_up, plain_down), (up, down)):
            after[s] = forced(jnp.concatenate(split(end), axis=0).astype(bf16), before[s])


def add_soundings(got, edges, table, cols):
    sources, held, slots = got.shape
    species, levels, rows = edges[0].shape
    akl = table.shape[1] // 4
    length = sources * slots
    pairs = -(-species * cols // 4)
    halves = [pltpu.VMEM((rows_held, length // 2), bf16) for rows_held in (4 * akl, TILE, TILE, WIDE)]
    edge = jax.ShapeDtypeStruct((species, levels, rows), f32)
    vmem, hbm = pl.BlockSpec(memory_space=pltpu.VMEM), pl.BlockSpec(memory_space=pl.ANY)
    return pl.pallas_call(
        functools.partial(add_kernel, cols=cols),
        out_shape=(jax.ShapeDtypeStruct((pairs * 4 * akl, WIDE), f32), edge, edge, edge, edge),
        in_specs=[hbm] + [vmem] * 5,
        out_specs=(vmem,) * 5,
        scratch_shapes=(
            pltpu.VMEM(got.shape, f32),
            *halves,
            *halves,
            pltpu.VMEM((2, WIDE), jnp.int32),
            pltpu.SemaphoreType.DMA((4,)),
        ),
        compiler_params=pltpu.CompilerParams(vmem_limit_bytes=ADD_LIMIT),
        cost_estimate=pl.CostEstimate(
            flops=2 * pairs * 4 * akl * WIDE * length,
            bytes_accessed=4 * got.size,
            transcendentals=0,
        ),
    )(got, *edges, table)


def on_device(
    adjoint_in,
    courant_lon,
    courant_lat,
    vertical_mix,
    sounding_values,
    sounding_dest,
    sounding_target,
    level_index,
):
    lat_size, lon_size = lax.axis_size("lat"), lax.axis_size("lon")
    n_tiles = lat_size * lon_size
    species, levels, cols, rows = adjoint_in.shape
    east_way = [(i, (i + 1) % lon_size) for i in range(lon_size)]
    west_way = [(j, i) for i, j in east_way]
    north_way = [(i, (i + 1) % lat_size) for i in range(lat_size)]
    south_way = [(j, i) for i, j in north_way]

    field = adjoint_in.transpose(0, 2, 1, 3)
    clon = courant_lon.transpose(1, 0, 2)
    clat = courant_lat.transpose(1, 0, 2)
    lat = lax.axis_index("lat").reshape(1)

    sent, *own = pack(sounding_dest, sounding_values, sounding_target, field, clon, clat, n_tiles)
    got = lax.all_to_all(sent, ("lat", "lon"), split_axis=0, concat_axis=0, tiled=True)

    def exchange(up, down, west, east):
        return (
            lax.ppermute(up, "lat", north_way),
            lax.ppermute(down, "lat", south_way),
            lax.ppermute(west, "lon", east_way),
            lax.ppermute(east, "lon", west_way),
        )

    halo = exchange(*own)
    weights = mix_weights(vertical_mix)
    table = (jnp.arange(levels, dtype=jnp.int32)[:, None] == level_index[None, :]).astype(bf16)
    table = jnp.concatenate([table] * 4, axis=1)
    plain, *edges = step(field, clon, clat, weights, lat_size)
    total, *edges = add_soundings(got, edges, table, cols)
    *edges, lanes, column_start, column_end = left_out(lat, own, halo, weights, edges, cols, lat_size)
    south, north, west, east = exchange(*edges)
    more = dict(
        lat=lat,
        south=south,
        north=north,
        west_col=west,
        east_col=east,
        clon_col=halo[2],
        clat_south=halo[0],
        total=total,
        table=table,
        lanes=lanes,
        column_start=column_start,
        column_end=column_end,
    )
    out, flux = step(plain, clon, clat, weights, lat_size, more)
    return out.transpose(0, 2, 1, 3), flux


def solution(mesh):
    return jax.shard_map(
        on_device,
        mesh=mesh,
        in_specs=(
            P(None, None, "lon", "lat"),
            P(None, "lon", "lat"),
            P(None, "lon", "lat"),
            P(),
            P(None, ("lat", "lon")),
            P(("lat", "lon"), None),
            P(("lat", "lon")),
            P(),
        ),
        out_specs=(P(None, None, "lon", "lat"), P(None, "lon", "lat")),
        check_vma=False,
    )
```

```python
import functools

import jax
import jax.numpy as jnp
from jax import lax
from jax.experimental import pallas as pl
from jax.experimental.pallas import tpu as pltpu
from jax.sharding import PartitionSpec as P

kappa_mix = 0.05
LANES = 128
WIDE = 256
TILE = 16
f32 = jnp.float32
bf16 = jnp.bfloat16
BLOCK = 15
VMEM_LIMIT = 52 * 2**20
PACK_LIMIT = 58 * 2**20
SMALL_LIMIT = 48 * 2**20
ADD_LIMIT = 49 * 2**20


def split(value):
    high = value.astype(bf16).astype(f32)
    return high, value - high


def nt_dot(a, b):
    return lax.dot_general(a, b, (((1,), (1,)), ((), ())), preferred_element_type=f32)


def onehot_product(parts, keys, tiles, spot, total, groups, step, together, depth, begin, end, onto=False, beside=None):
    rows = parts.shape[0]
    chunks = (end - begin) // depth

    def chunk(g, c):
        at = pl.ds(pl.multiple_of(begin + c * depth, LANES), depth)
        key = [k[:, at] for k in keys]
        held = [parts[TILE * q : TILE * (q + 1), at] for q in range(len(tiles))]
        none = jnp.zeros_like(held[0])
        left = []
        for i in range(together):
            hit = {}
            for kind in tiles:
                if kind not in hit:
                    which, offset = kind
                    number = jnp.asarray((g * together + i) * step + offset, jnp.int32).astype(f32).astype(bf16)
                    hit[kind] = key[which] == number
            left += [jnp.where(hit[kind], part, none) for kind, part in zip(tiles, held)]
        return nt_dot(jnp.concatenate(left, axis=0), spot[:, at])

    def of_group(g, carry):
        to = pl.ds(pl.multiple_of(g * (together * rows), together * rows), together * rows)
        if beside is not None:
            beside(g)
        if not onto:
            total[to, :] = chunk(g, 0)

        def of_chunk(c, carry):
            total[to, :] += chunk(g, c)
            return carry

        return lax.fori_loop(0 if onto else 1, chunks, of_chunk, carry)

    lax.fori_loop(groups[0] // together, groups[1] // together, of_group, 0)


def mark(spot, at, row):
    row = jnp.broadcast_to(row.astype(f32), (TILE, row.shape[1])).astype(bf16)
    base = lax.broadcasted_iota(jnp.int32, row.shape, 0).astype(f32).astype(bf16)
    one, none = jnp.ones_like(row), jnp.zeros_like(row)
    for q in range(WIDE // TILE):
        spot[TILE * q : TILE * (q + 1), at] = jnp.where(row - jnp.asarray(TILE * q, bf16) == base, one, none)


def edge_lanes(columns, kept, first, up, share=None):
    rows = kept.shape[1]
    lane = lax.broadcasted_iota(jnp.int32, kept.shape, 1)
    own = jnp.zeros_like(kept)
    for i, v in enumerate(columns):
        if up:
            own = jnp.where(lane == 2 * i, pltpu.roll(v, 2 * i + 1, 1), own)
        else:
            own = jnp.where(lane == 2 * i + 1, pltpu.roll(v, 2 * i + 1, 1), own)
    if share is not None:
        own = own * share
    turn = 2 * first if up else lax.rem(2 * first + rows - 2, rows)
    return kept + pltpu.roll(own, turn, 1)


PACK = (16, 8192)


def whole_part(value, divisor):
    return ((value.astype(f32) + 0.5) * (1.0 / divisor)).astype(jnp.int32)


def half_segment(columns):
    return -(-columns // 4) // 2 * 2 * WIDE


def pack_kernel(
    dest,
    values,
    target,
    field_at,
    clon_at,
    clat_at,
    out,
    up,
    down,
    west,
    east,
    parts,
    group,
    spot,
    total,
    field,
    clat,
    sems,
):
    n_tiles, held, _ = out.shape
    species, cols, _, rows = field.shape
    copies = [(field_at, field), (clat_at, clat), (clon_at.at[cols - 1], west.at[species])]
    for s in range(species):
        copies += [(field_at.at[s, cols - 1], west.at[s]), (field_at.at[s, 0], east.at[s])]
    copies = [pltpu.make_async_copy(*pair, sems.at[i]) for i, pair in enumerate(copies)]
    for copy in copies:
        copy.start()
    up[...] = jnp.zeros_like(up)
    down[...] = jnp.zeros_like(down)
    levels, length = values.shape
    iota_t = lax.broadcasted_iota(jnp.int32, (n_tiles, WIDE), 0)
    square = (WIDE, WIDE)
    upper = (
        lax.broadcasted_iota(jnp.int32, square, 0) < lax.broadcasted_iota(jnp.int32, square, 1)
    ).astype(f32).astype(bf16)

    halfway = half_segment(species * cols)

    def rank(at, base):
        d = dest[:, at]
        t = target[:, at]
        cell = whole_part(t, species)
        row_of = whole_part(cell, cols)
        segment = ((t - cell * species) * cols + cell - row_of * cols) * rows + row_of
        upper_half = segment >= halfway
        hot = iota_t == d
        hot_f = jnp.where(hot, jnp.where(upper_half, 256.0, 1.0), 0.0)
        earlier = jnp.dot(hot_f.astype(bf16), upper, preferred_element_type=f32) + base
        own = jnp.sum(jnp.where(hot, earlier, 0.0), axis=0, keepdims=True).astype(jnp.int32)
        slot = jnp.where(upper_half, LANES - 1 - (own >> 8), own & 255)
        low = slot + (d & 1) * LANES
        mark(spot, at, low)
        group[:, at] = jnp.broadcast_to((d >> 1).astype(f32), (TILE, WIDE)).astype(bf16)
        row = jnp.concatenate(
            [values[:, at], (segment + 1).astype(f32), jnp.zeros((held - levels - 1, WIDE), f32)], axis=0
        )
        parts[:, at] = jnp.concatenate(split(row), axis=0).astype(bf16)
        return base + jnp.sum(hot_f, axis=1, keepdims=True)

    def ranks(b, base):
        for i in range(4):
            base = rank(pl.ds(pl.multiple_of((4 * b + i) * WIDE, WIDE), WIDE), base)
        return base

    lax.fori_loop(0, length // (4 * WIDE), ranks, jnp.zeros((n_tiles, 1), f32))
    for copy in copies:
        copy.wait()
    blocks = cols // BLOCK

    def take_edges(g):
        first = jnp.minimum(g, blocks - 1) * BLOCK
        new = (g < blocks).astype(f32)
        for s in range(species + 1):
            columns = [field[s, first + i] if s < species else clat[first + i] for i in range(BLOCK)]
            up[s] = edge_lanes(columns, up[s], first, True, new)
            if s < species:
                down[s] = edge_lanes(columns, down[s], first, False, new)

    tiles = ((0, 0),) * (2 * held // TILE)
    onehot_product(
        parts, [group], tiles, spot, total, (0, n_tiles // 2), 1, *PACK, 0, length, beside=take_edges
    )

    def put(g, carry):
        for i in range(4):
            j = 4 * g + i
            at = pl.multiple_of(j * 2 * held, 2 * held)
            both = total[pl.ds(at, held), :] + total[pl.ds(at + held, held), :]
            out[2 * j] = both[:, :LANES]
            out[2 * j + 1] = both[:, LANES:]
        return carry

    lax.fori_loop(0, n_tiles // 8, put, 0)


def pack(dest, values, target, field, clon, clat, n_tiles):
    levels, length = values.shape
    species, cols, depth, rows = field.shape
    held = -(-(levels + 1) // 8) * 8
    four, three = (species + 1, depth, rows), (species, depth, rows)
    vmem, hbm = pl.BlockSpec(memory_space=pltpu.VMEM), pl.BlockSpec(memory_space=pl.ANY)
    return pl.pallas_call(
        pack_kernel,
        out_shape=tuple(
            jax.ShapeDtypeStruct(shape, f32) for shape in ((n_tiles, held, LANES), four, three, four, three)
        ),
        in_specs=[vmem, vmem, vmem, hbm, hbm, hbm],
        out_specs=(vmem,) * 5,
        scratch_shapes=(
            pltpu.VMEM((2 * held, length), bf16),
            pltpu.VMEM((TILE, length), bf16),
            pltpu.VMEM((WIDE, length), bf16),
            pltpu.VMEM((n_tiles // 2 * 2 * held, WIDE), f32),
            pltpu.VMEM(field.shape, f32),
            pltpu.VMEM(clat.shape, f32),
            pltpu.SemaphoreType.DMA((3 + 2 * species,)),
        ),
        compiler_params=pltpu.CompilerParams(vmem_limit_bytes=PACK_LIMIT),
        cost_estimate=pl.CostEstimate(
            flops=2 * length * n_tiles * LANES * 2 * held,
            bytes_accessed=4 * (length * 22 + n_tiles * held * LANES + field.size),
            transcendentals=0,
        ),
    )(dest.reshape(1, length), values, target.reshape(1, length), field, clon, clat)


def mix_weights(vertical_mix):
    levels = vertical_mix.shape[0]
    matrix = (jnp.eye(levels, dtype=f32) + vertical_mix).T
    high = lax.reduce_precision(matrix, 8, 7)
    return jnp.concatenate([high, high, matrix - high], axis=1).astype(bf16)


def step_kernel(*refs, names, lat_size):
    ref = dict(zip(names, refs))
    second = "total" in ref
    field, clon, clat, out = ref["field"], ref["clon"], ref["clat"], ref["out"]
    species, block, levels, rows = field.shape
    lane = lax.broadcasted_iota(jnp.int32, (levels, rows), 1)
    first, last = lane == 0, lane == rows - 1
    here = pl.program_id(0)
    at_start, at_end = here == 0, here == pl.num_programs(0) - 1
    start = here * block
    w = ref["weights"][...]
    waiting = []

    def back(v, i):
        return pltpu.roll(v, (rows - 2 * i) % rows, 1) if i else v

    if second:
        lat = ref["lat"][0]
        below = jnp.where(jnp.logical_and(first, lat == 0), 0.0, 1.0)
        inside = jnp.where(jnp.logical_and(last, lat == lat_size - 1), 0.0, 1.0)
        turn = lax.rem(rows - 2 * start, rows)
        even = lane % 2 == 0
        ends = jnp.logical_or(first, last)
        halos = [
            pltpu.roll(jnp.where(even, ref["south"][s], ref["north"][s]), turn, 1) for s in range(species)
        ]
        left_out = [pltpu.roll(ref["lanes"][s], turn, 1) for s in range(species)]
        courant_south = pltpu.roll(ref["clat_south"][0], turn, 1)
        t = ref["table"][...]
        cols = pl.num_programs(0) * block
        wanted = []
        made = {}

        def make(ready):
            forcing = jnp.dot(t, jnp.concatenate([p for _, _, p in ready], axis=1), preferred_element_type=f32)
            for k, ((s, i), v, _) in enumerate(ready):
                v = v + forcing[:, k * rows : (k + 1) * rows] + jnp.where(ends, back(left_out[s], i), 0.0)
                if i == 0:
                    v = v + jnp.where(at_start, ref["column_start"][s], 0.0)
                if i == block - 1:
                    v = v + jnp.where(at_end, ref["column_end"][s], 0.0)
                made[s, i] = v

        for i in range(-1, block + 1):
            x = jnp.clip(start + i, 0, cols - 1)
            for s in range(species):
                v = ref["field_west"][s, 0] if i < 0 else ref["field_east"][s, 0] if i == block else field[s, i]
                wanted.append(((s, i), v, spread(ref["total"], s * cols + x, rows, t.shape[1] // 4)))
                if len(wanted) == 3:
                    make(wanted)
                    wanted.clear()
        if wanted:
            make(wanted)

        def at_column(s, i):
            return made[s, i]
    else:
        below, inside = jnp.where(first, 0.0, 1.0), jnp.where(last, 0.0, 1.0)
        finished = [[None] * block for _ in range(species)]

        def at_column(s, i):
            return ref["field_west"][s, 0] if i < 0 else ref["field_east"][s, 0] if i == block else field[s, i]

    def mix(ready):
        mixed = jnp.dot(
            w, jnp.concatenate([r for _, _, r in ready], axis=1), preferred_element_type=f32
        )
        for k, (s, i, _) in enumerate(ready):
            m = mixed[:, k * rows : (k + 1) * rows]
            out[s, i] = m
            if second:
                ref["flux"][s, pl.ds(start + i, 1), :] = at_column(s, i)[0:1] + m[0:1]
            else:
                finished[s][i] = m

    for i in range(block):
        cl, cw = clon[i], clat[i]
        cl_west = clon[i - 1] if i else ref["clon_before"][0]
        if i == 0 and second:
            cl_west = jnp.where(at_start, ref["clon_col"][0], cl_west)
        e = jnp.maximum(cl, 0.0) + kappa_mix
        w_ = kappa_mix - jnp.minimum(cl_west, 0.0)
        if not second and i == 0:
            w_ = jnp.where(at_start, 0.0, w_)
        if not second and i == block - 1:
            e = jnp.where(at_end, 0.0, e)
        n = (jnp.maximum(cw, 0.0) + kappa_mix) * inside
        cs = pltpu.roll(cw, 1, 1)
        if second:
            cs = jnp.where(first, back(courant_south, i), cs)
        s_ = (kappa_mix - jnp.minimum(cs, 0.0)) * below
        centre = 1.0 - (e + w_ + n + s_)
        for s in range(species):
            v, v_w, v_e = at_column(s, i), at_column(s, i - 1), at_column(s, i + 1)
            v_n, v_s = pltpu.roll(v, rows - 1, 1), pltpu.roll(v, 1, 1)
            if second:
                if i == 0:
                    v_w = jnp.where(at_start, ref["west_col"][s], v_w)
                if i == block - 1:
                    v_e = jnp.where(at_end, ref["east_col"][s], v_e)
                halo = back(halos[s], i)
                v_n, v_s = jnp.where(last, halo, v_n), jnp.where(first, halo, v_s)
            h = centre * v + e * v_e + w_ * v_w + n * v_n + s_ * v_s
            waiting.append((s, i, mix_parts(h)))
            if len(waiting) == 3:
                mix(waiting)
                waiting.clear()
    if waiting:
        mix(waiting)
    if not second:
        up, down, west, east = ref["up"], ref["down"], ref["west"], ref["east"]

        @pl.when(at_start)
        def _():
            up[...] = jnp.zeros_like(up)
            down[...] = jnp.zeros_like(down)
            for s in range(species):
                east[s] = out[s, 0]

        @pl.when(at_end)
        def _():
            for s in range(species):
                west[s] = out[s, block - 1]

        for s in range(species):
            up[s] = edge_lanes(finished[s], up[s], start, True)
            down[s] = edge_lanes(finished[s], down[s], start, False)


def mix_parts(h):
    high, low = split(h)
    return jnp.concatenate([high, low, high], axis=0).astype(bf16)


def left_out_kernel(
    lat_ref,
    up_own,
    down_own,
    west_own,
    east_own,
    south,
    north,
    west,
    east,
    weights,
    up_in,
    down_in,
    west_in,
    east_in,
    up,
    down,
    west_out,
    east_out,
    lanes,
    column_start,
    column_end,
    *,
    cols,
    lat_size,
):
    species, levels, rows = up_in.shape
    lane = lax.broadcasted_iota(jnp.int32, (levels, rows), 1)
    even = lane % 2 == 0
    ends = jnp.logical_or(lane == 0, lane == rows - 1)
    lat = lat_ref[0]
    below = jnp.where(lat == 0, 0.0, 1.0)
    inside = jnp.where(lat == lat_size - 1, 0.0, 1.0)
    far = 2 * (cols - 1)

    def later(v):
        return pltpu.roll(v, 1, 1)

    def sooner(v):
        return pltpu.roll(v, rows - 1, 1)

    n = (jnp.maximum(sooner(up_own[species]), 0.0) + kappa_mix) * inside
    s_ = (kappa_mix - jnp.minimum(south[species], 0.0)) * below
    w_ = kappa_mix - jnp.minimum(west[species], 0.0)
    e = jnp.maximum(west_own[species], 0.0) + kappa_mix
    w = weights[...]
    for s in range(species):
        rim = jnp.where(even, s_ * (south[s] - later(down_own[s])), n * (north[s] - sooner(up_own[s])))
        terms = [rim, w_ * (west[s] - east_own[s]), e * (east[s] - west_own[s])]
        mixed = jnp.dot(w, jnp.concatenate([mix_parts(h) for h in terms], axis=1), preferred_element_type=f32)
        c, c_start, c_end = [mixed[:, k * rows : (k + 1) * rows] for k in range(3)]
        lanes[s], column_start[s], column_end[s] = c, c_start, c_end
        up[s] = (
            up_in[s]
            + jnp.where(even, later(c), 0.0)
            + jnp.where(lane == 0, later(c_start), 0.0)
            + jnp.where(lane == far, pltpu.roll(c_end, far + 1, 1), 0.0)
        )
        down[s] = (
            down_in[s]
            + jnp.where(even, 0.0, sooner(c))
            + jnp.where(lane == rows - 1, sooner(c_start), 0.0)
            + jnp.where(lane == far - 1, pltpu.roll(c_end, far - 1, 1), 0.0)
        )
        west_out[s] = west_in[s] + c_end + jnp.where(ends, pltpu.roll(c, rows - far, 1), 0.0)
        east_out[s] = east_in[s] + c_start + jnp.where(ends, c, 0.0)


def left_out(lat, own, halo, weights, edges, cols, lat_size):
    shape = jax.ShapeDtypeStruct(edges[0].shape, f32)
    vmem = pl.BlockSpec(memory_space=pltpu.VMEM)
    return pl.pallas_call(
        functools.partial(left_out_kernel, cols=cols, lat_size=lat_size),
        out_shape=(shape,) * 7,
        in_specs=[pl.BlockSpec(memory_space=pltpu.SMEM)] + [vmem] * 13,
        out_specs=(vmem,) * 7,
        compiler_params=pltpu.CompilerParams(vmem_limit_bytes=SMALL_LIMIT),
        cost_estimate=pl.CostEstimate(flops=shape.size * 3000, bytes_accessed=shape.size * 100, transcendentals=0),
    )(lat, *own, *halo, weights, *edges)


def spread(total, sx, rows, akl):
    pair = total[
        pl.ds(pl.multiple_of((sx >> 1) * 2 * akl, 8), 2 * akl),
        pl.ds(pl.multiple_of((sx & 1) * rows, rows), rows),
    ]
    return jnp.concatenate(split(pair), axis=0).astype(bf16)


def step(field, clon, clat, weights, lat_size, more=None):
    species, cols, levels, rows = field.shape
    columns = pl.BlockSpec((species, BLOCK, levels, rows), lambda i: (0, i, 0, 0))
    courant = pl.BlockSpec((BLOCK, levels, rows), lambda i: (i, 0, 0))
    whole = lambda shape: pl.BlockSpec(shape, lambda i: (0,) * len(shape))
    part = lambda at: pl.BlockSpec((1, levels, rows), lambda i: (at, 0, 0))
    three = (species, levels, rows)
    given = {
        "field": (field, columns),
        "field_west": (
            field,
            pl.BlockSpec((species, 1, levels, rows), lambda i: (0, jnp.maximum(i * BLOCK - 1, 0), 0, 0)),
        ),
        "field_east": (
            field,
            pl.BlockSpec((species, 1, levels, rows), lambda i: (0, jnp.minimum(i * BLOCK + BLOCK, cols - 1), 0, 0)),
        ),
        "clon": (clon, courant),
        "clon_before": (clon, pl.BlockSpec((1, levels, rows), lambda i: (jnp.maximum(i * BLOCK - 1, 0), 0, 0))),
        "clat": (clat, courant),
        "weights": (weights, whole(weights.shape)),
    }
    if more is None:
        made = dict(up=three, down=three, west=three, east=three)
    else:
        made = dict(flux=(species, cols, rows))
        for name, value in more.items():
            spec = whole(value.shape)
            if name == "lat":
                spec = pl.BlockSpec(memory_space=pltpu.SMEM)
            elif name in ("clon_col", "clat_south"):
                spec = part(species)
            given[name] = (value, spec)
    return pl.pallas_call(
        functools.partial(step_kernel, names=(*given, "out", *made), lat_size=lat_size),
        out_shape=[pltpu.HBM(field.shape, f32)] + [jax.ShapeDtypeStruct(shape, f32) for shape in made.values()],
        grid=(cols // BLOCK,),
        in_specs=[spec for _, spec in given.values()],
        out_specs=[columns] + [whole(shape) for shape in made.values()],
        compiler_params=pltpu.CompilerParams(vmem_limit_bytes=VMEM_LIMIT),
        cost_estimate=pl.CostEstimate(
            flops=field.size * levels * 6, bytes_accessed=field.size * 12, transcendentals=0
        ),
    )(*[value for value, _ in given.values()])


def add_kernel(
    got_at,
    plain_up,
    plain_down,
    plain_west,
    plain_east,
    table,
    total,
    up,
    down,
    west,
    east,
    got,
    parts,
    group,
    middle,
    spot,
    parts_b,
    group_b,
    middle_b,
    spot_b,
    bounds,
    sem_got,
    *,
    cols,
):
    sources, held, slots = got_at.shape
    species, levels, rows = plain_up.shape
    akl = table.shape[1] // 4
    quarters = sem_got.shape[0]
    quarter = sources // quarters
    came = [
        pltpu.make_async_copy(got_at.at[pl.ds(q * quarter, quarter)], got.at[pl.ds(q * quarter, quarter)], sem_got.at[q])
        for q in range(quarters)
    ]
    for copy in came:
        copy.start()
    second = (lax.broadcasted_iota(jnp.int32, (TILE, WIDE), 0) >= TILE // 2).astype(f32)
    quarter_of = lax.broadcasted_iota(jnp.int32, (held, slots), 1) // (slots // 4)
    length = sources * slots // 2
    outer = length // 4
    halfway = half_segment(species * cols)
    halves = ((parts, group, middle, spot), (parts_b, group_b, middle_b, spot_b))

    def put(to, row, at):
        to_parts, to_group, to_middle, to_spot = to
        at = pl.ds(at if isinstance(at, int) else pl.multiple_of(at, LANES), WIDE)
        segment = row[akl : akl + 1].astype(jnp.int32) - 1
        mark(to_spot, at, segment & (WIDE - 1))
        pair = jnp.broadcast_to((segment >> 8).astype(f32), (TILE, WIDE))
        to_group[:, at] = pair.astype(bf16)
        to_middle[:, at] = (pair - second).astype(bf16)
        high, low = split(row[:akl])
        both = jnp.concatenate([high, low], axis=0)
        to_parts[:, at] = jnp.concatenate([both, both], axis=0).astype(bf16)
        return segment

    def prepare(half, g):
        fours = []
        for b in range(2):
            turned = [got[half * (sources // 2) + 8 * g + 4 * b + k] for k in range(4)]
            turned = [pltpu.roll(v, k * (slots // 4), 1) if k else v for k, v in enumerate(turned)]
            rows_of = []
            for q in range(4):
                row = turned[0]
                for k in range(1, 4):
                    row = jnp.where(quarter_of == (q + k) % 4, turned[k], row)
                rows_of.append(row)
            fours.append(rows_of)
        row = [jnp.concatenate([fours[0][q], fours[1][q]], axis=1) for q in range(4)]
        to = halves[half]
        segment = put(to, row[0], g * WIDE)
        bounds[0:1] = jnp.maximum(bounds[0:1], segment)
        put(to, row[1], outer + 2 * g * WIDE)
        put(to, row[2], outer + (2 * g + 1) * WIDE)
        segment = put(to, row[3], 3 * outer + g * WIDE)
        bounds[1:2] = jnp.minimum(bounds[1:2], jnp.where(segment < 0, 2 * halfway, segment))

    def prepare_one(g, carry):
        prepare(0, g)
        return carry

    bounds[0:1] = jnp.full((1, WIDE), -1, jnp.int32)
    bounds[1:2] = jnp.full((1, WIDE), 2 * halfway, jnp.int32)
    steps = sources // 16
    for q, copy in enumerate(came):
        copy.wait()
        if q < 2:
            lax.fori_loop(q * steps // 2, (q + 1) * steps // 2, prepare_one, 0)

    tiles = ((0, 0), (0, 0), (1, 0), (0, 1), (0, 1))
    groups = total.shape[0] // (4 * akl)
    lower, higher = (0, groups // 2), (groups // 2, groups)

    def add(half, of, depth, begin, end, **how):
        held_parts, held_group, held_middle, held_spot = halves[half]
        onehot_product(
            held_parts, [held_group, held_middle], tiles, held_spot, total, of, 2, groups // 2, depth, begin, end, **how
        )

    def beside(steps_now):
        def run(_):
            for g in steps_now:
                prepare(1, g)

        return run

    add(0, lower, 3 * outer, 0, 3 * outer, beside=beside(range(steps // 2)))
    add(0, higher, 3 * outer, outer, length, beside=beside(range(steps // 2, steps)))
    add(1, lower, 3 * outer, 0, 3 * outer, onto=True)
    add(1, higher, 3 * outer, outer, length, onto=True)
    highest, lowest = jnp.max(bounds[0:1]), jnp.min(bounds[1:2])

    @pl.when(highest >= halfway)
    def _():
        for half in range(2):
            add(half, higher, outer, 0, outer, onto=True)

    @pl.when(lowest < halfway)
    def _():
        for half in range(2):
            add(half, lower, outer, 3 * outer, length, onto=True)

    t = table[...]

    def forced(parts_of, before):
        return before + jnp.dot(t, parts_of, preferred_element_type=f32)

    for s in range(species):
        east[s] = forced(spread(total, s * cols, rows, akl), plain_east[s])
        west[s] = forced(spread(total, s * cols + cols - 1, rows, akl), plain_west[s])

        def of_block(b, carry):
            columns = []
            for i in range(BLOCK):
                sx = s * cols + b * BLOCK + i
                columns.append(
                    total[
                        pl.ds(pl.multiple_of((sx >> 1) * 2 * akl, 8), 2 * akl),
                        pl.ds(pl.multiple_of((sx & 1) * rows, rows), rows),
                    ]
                )
            return tuple(edge_lanes(columns, kept, b * BLOCK, k == 0) for k, kept in enumerate(carry))

        none = jnp.zeros((2 * akl, rows), f32)
        ends = lax.fori_loop(0, cols // BLOCK, of_block, (none, none))
        for end, before, after in zip(ends, (plain_up, plain_down), (up, down)):
            after[s] = forced(jnp.concatenate(split(end), axis=0).astype(bf16), before[s])


def add_soundings(got, edges, table, cols):
    sources, held, slots = got.shape
    species, levels, rows = edges[0].shape
    akl = table.shape[1] // 4
    length = sources * slots
    pairs = -(-species * cols // 4)
    halves = [pltpu.VMEM((rows_held, length // 2), bf16) for rows_held in (4 * akl, TILE, TILE, WIDE)]
    edge = jax.ShapeDtypeStruct((species, levels, rows), f32)
    vmem, hbm = pl.BlockSpec(memory_space=pltpu.VMEM), pl.BlockSpec(memory_space=pl.ANY)
    return pl.pallas_call(
        functools.partial(add_kernel, cols=cols),
        out_shape=(jax.ShapeDtypeStruct((pairs * 4 * akl, WIDE), f32), edge, edge, edge, edge),
        in_specs=[hbm] + [vmem] * 5,
        out_specs=(vmem,) * 5,
        scratch_shapes=(
            pltpu.VMEM(got.shape, f32),
            *halves,
            *halves,
            pltpu.VMEM((2, WIDE), jnp.int32),
            pltpu.SemaphoreType.DMA((4,)),
        ),
        compiler_params=pltpu.CompilerParams(vmem_limit_bytes=ADD_LIMIT),
        cost_estimate=pl.CostEstimate(
            flops=2 * pairs * 4 * akl * WIDE * length,
            bytes_accessed=4 * got.size,
            transcendentals=0,
        ),
    )(got, *edges, table)


def on_device(
    adjoint_in,
    courant_lon,
    courant_lat,
    vertical_mix,
    sounding_values,
    sounding_dest,
    sounding_target,
    level_index,
):
    lat_size, lon_size = lax.axis_size("lat"), lax.axis_size("lon")
    n_tiles = lat_size * lon_size
    species, levels, cols, rows = adjoint_in.shape
    east_way = [(i, (i + 1) % lon_size) for i in range(lon_size)]
    west_way = [(j, i) for i, j in east_way]
    north_way = [(i, (i + 1) % lat_size) for i in range(lat_size)]
    south_way = [(j, i) for i, j in north_way]

    field = adjoint_in.transpose(0, 2, 1, 3)
    clon = courant_lon.transpose(1, 0, 2)
    clat = courant_lat.transpose(1, 0, 2)
    lat = lax.axis_index("lat").reshape(1)

    sent, *own = pack(sounding_dest, sounding_values, sounding_target, field, clon, clat, n_tiles)
    got = lax.all_to_all(sent, ("lat", "lon"), split_axis=0, concat_axis=0, tiled=True)

    def exchange(up, down, west, east):
        return (
            lax.ppermute(up, "lat", north_way),
            lax.ppermute(down, "lat", south_way),
            lax.ppermute(west, "lon", east_way),
            lax.ppermute(east, "lon", west_way),
        )

    halo = exchange(*own)
    weights = mix_weights(vertical_mix)
    table = (jnp.arange(levels, dtype=jnp.int32)[:, None] == level_index[None, :]).astype(bf16)
    table = jnp.concatenate([table] * 4, axis=1)
    plain, *edges = step(field, clon, clat, weights, lat_size)
    total, *edges = add_soundings(got, edges, table, cols)
    *edges, lanes, column_start, column_end = left_out(lat, own, halo, weights, edges, cols, lat_size)
    south, north, west, east = exchange(*edges)
    more = dict(
        lat=lat,
        south=south,
        north=north,
        west_col=west,
        east_col=east,
        clon_col=halo[2],
        clat_south=halo[0],
        total=total,
        table=table,
        lanes=lanes,
        column_start=column_start,
        column_end=column_end,
    )
    out, flux = step(plain, clon, clat, weights, lat_size, more)
    return out.transpose(0, 2, 1, 3), flux


def solution(mesh):
    return jax.shard_map(
        on_device,
        mesh=mesh,
        in_specs=(
            P(None, None, "lon", "lat"),
            P(None, "lon", "lat"),
            P(None, "lon", "lat"),
            P(),
            P(None, ("lat", "lon")),
            P(("lat", "lon"), None),
            P(("lat", "lon")),
            P(),
        ),
        out_specs=(P(None, None, "lon", "lat"), P(None, "lon", "lat")),
        check_vma=False,
    )
```
